32 devices in a mesh: groups: 2 (over y), tm: 4 (over z), head: 2 (over x), sub: 2 (over core).
Axes of the slice: x: 2, y: 2, z: 4, core: 2. Of those that a mesh axis runs over, the one named last changes fastest.
Arguments:
- queries: bfloat16 [4096, 4096], P(('groups', 'tm'), ('head', 'sub')), parts along dimension 0, may hold values from -6 to 6
- keys: bfloat16 [4096, 4096], P(('groups', 'tm'), ('head', 'sub')), parts along dimension 0, may hold values from -6 to 6
- values: bfloat16 [4096, 4096], P(('groups', 'tm'), ('head', 'sub')), parts along dimension 0, may hold values from -16 to 16
- band_blocks: int32 [4, 4, 2], replicated, may hold values from 0 to 4, as said below
Outputs:
- attended: bfloat16 [4096, 4096], P(('groups', 'tm'), ('head', 'sub')), parts along dimension 0
The draws below stay inside these ranges and needn't reach their ends.
There are 2 independent parts, one for each index of `groups`. The reference program is written for one: setup_inputs(seed, part) draws one part's arguments, and reference() takes and returns one part's arrays. A program takes and returns all parts, laid end to end along the dimension named above; an argument that names none is the same for every part. Nothing has to cross between parts.
Inputs may be any that keep to these rules, and one draw needn't show every extreme that they name: band_blocks[f, g] lists in rising order blocks of frame g; the slots after the listed ones hold 4. For d = |f - g| of 2 or more the list is o + k * 2 * 2 ** (floor(log2 d) - 1), k = 0, 1, ..., while below 4, for some offset o below that stride; for d of 1 or 0 the list is empty. So frames two or three apart list exactly 2 blocks and frames four or more apart at most one, in slot 0.
All inputs are finite; a program needn't handle non-finite values.
Results may differ from the reference program's by a relative error of at most 0.0032.
Values may be sent and summed in bfloat16 or wider, within the bound.
No kernel may reach another device: no remote copies, remote signals or barrier semaphores. Data moves between devices by JAX's collectives and lax.ppermute only.
A program may use at most 64 MiB of HBM per device.

```python
import jax
import jax.numpy as jnp
from jax import lax

HEADS = 32
HD = 128
BLOCK = 128
CAP = 2
BLK_FR = 4
FT = 512
FRAMES = 4
TOKENS = 2048


def draw_queries(key, part):
    key = jax.random.fold_in(key, 3)
    sample = jnp.clip(1.5 * jax.random.normal(key, (TOKENS, HEADS * HD), jnp.float32), -6.0, 6.0)
    return sample.astype(jnp.bfloat16)


def draw_keys(key, part):
    key = jax.random.fold_in(key, 5)
    sample = jnp.clip(1.5 * jax.random.normal(key, (TOKENS, HEADS * HD), jnp.float32), -6.0, 6.0)
    return sample.astype(jnp.bfloat16)


def draw_band_blocks(key, part):
    key = jax.random.fold_in(key, 11)
    frame_ids = jnp.arange(FRAMES, dtype=jnp.int32)
    distance = jnp.abs(frame_ids[:, None] - frame_ids[None, :])
    band_index = jnp.zeros_like(distance)
    for exponent in range(1, 20):
        band_index = band_index + (distance >= 2 ** exponent).astype(jnp.int32)
    stride = BLK_FR // CAP * jnp.left_shift(jnp.int32(1), jnp.maximum(band_index - 1, 0))
    offset = jax.random.randint(key, (FRAMES, FRAMES), 0, stride, dtype=jnp.int32)
    slot_index = jnp.arange(CAP, dtype=jnp.int32)
    picked = offset[:, :, None] + slot_index[None, None, :] * stride[:, :, None]
    usable = (picked < BLK_FR) & (distance[:, :, None] >= 2)
    return jnp.where(usable, picked, BLK_FR).astype(jnp.int32)


def shard_levels(stream_key, shape, shards, low, high):
    def one(dim, parts):
        heights = jax.random.uniform(jax.random.fold_in(jax.random.fold_in(stream_key, 6), dim), (parts,), jnp.float32, low / len(shards), high / len(shards))
        return jnp.repeat(jnp.exp(heights), shape[dim] // parts).reshape((-1,) + (1,) * (len(shape) - dim - 1))

    level = one(*shards[0])
    for cut in shards[1:]:
        level = level * one(*cut)
    return level


def noise(rng, shape, scale, most, split=(), held_as=jnp.bfloat16):
    values = jax.random.normal(rng, shape, jnp.float32) * scale
    if len(split) > 0:
        values = shard_levels(rng, shape, split, -0.22, 0.18) * values
    return jnp.clip(values, min=-most, max=most).astype(held_as)


def setup_inputs(seed: int = 0, part: int = 0) -> dict:
    splits = jax.random.split(jax.random.key(seed), 5)
    part_splits = jax.random.split(jax.random.fold_in(splits[4], part), 5)
    return {
        "queries": draw_queries(jax.random.fold_in(jax.random.fold_in(splits[4], part), 71), part),
        "keys": draw_keys(jax.random.fold_in(jax.random.fold_in(splits[4], part), 71), part),
        "values": noise(part_splits[2], (TOKENS, HEADS * HD), 3.0, 16.0, ((0, 4), (1, 4))),
        "band_blocks": draw_band_blocks(jax.random.fold_in(splits[4], 71), part),
    }


masked_fill = -1e30


def head_attention(query_head, key_head, value_head, visible):
    scores = jnp.dot(query_head, key_head.T, preferred_element_type=jnp.float32) * (HD ** -0.5)
    scores = jnp.where(visible[None, :], scores, masked_fill)
    row_max = jnp.max(scores, axis=1, keepdims=True)
    powers = jnp.exp(scores - row_max)
    row_sum = jnp.sum(powers, axis=1, keepdims=True)
    weights = powers.astype(jnp.bfloat16)
    mixed_sum = jnp.dot(weights, value_head, preferred_element_type=jnp.float32)
    return (mixed_sum / row_sum).astype(jnp.bfloat16)


def reference(queries, keys, values, band_blocks):
    columns = HEADS * HD
    half_rows = FT // 2
    frame_q = queries.reshape(FRAMES, FT, HEADS, HD)
    empty_frame = jnp.zeros((1, FT, columns), jnp.bfloat16)
    padded_k = jnp.concatenate([empty_frame, keys.reshape(FRAMES, FT, columns), empty_frame], 0)
    padded_v = jnp.concatenate([empty_frame, values.reshape(FRAMES, FT, columns), empty_frame], 0)
    empty_block = jnp.zeros((FRAMES, 1, BLOCK, columns), jnp.bfloat16)
    block_k = jnp.concatenate([keys.reshape(FRAMES, BLK_FR, BLOCK, columns), empty_block], 1)
    block_v = jnp.concatenate([values.reshape(FRAMES, BLK_FR, BLOCK, columns), empty_block], 1)
    frame_ids = jnp.arange(FRAMES, dtype=jnp.int32)
    position = jnp.arange(2 * FT, dtype=jnp.int32)

    def one_frame(current):
        def near_rows(padded):
            lower_rim = lax.dynamic_index_in_dim(padded, current, 0, keepdims=False)[half_rows:]
            middle = lax.dynamic_index_in_dim(padded, current + 1, 0, keepdims=False)
            upper_rim = lax.dynamic_index_in_dim(padded, current + 2, 0, keepdims=False)[:half_rows]
            return jnp.concatenate([lower_rim, middle, upper_rim], 0)

        listing = lax.dynamic_index_in_dim(band_blocks, current, 0, keepdims=False)
        far_keys = block_k[frame_ids[:, None], listing].reshape(-1, columns)
        far_values = block_v[frame_ids[:, None], listing].reshape(-1, columns)
        near_ok = ((position >= half_rows) | (current > 0)) & ((position < half_rows + FT) | (current < FRAMES - 1))
        far_ok = jnp.repeat((listing != BLK_FR).reshape(-1), BLOCK)
        all_keys = jnp.concatenate([near_rows(padded_k), far_keys], 0).reshape(-1, HEADS, HD)
        all_values = jnp.concatenate([near_rows(padded_v), far_values], 0).reshape(-1, HEADS, HD)
        visible = jnp.concatenate([near_ok, far_ok], 0)
        query_frame = lax.dynamic_index_in_dim(frame_q, current, 0, keepdims=False)

        def per_head(head_at):
            return head_attention(query_frame[:, head_at], all_keys[:, head_at], all_values[:, head_at], visible)

        result = lax.map(per_head, jnp.arange(HEADS, dtype=jnp.int32))
        return jnp.transpose(result, (1, 0, 2)).reshape(FT, columns)

    return lax.map(one_frame, frame_ids).reshape(FRAMES * FT, columns)
```

```python
import functools

import jax
import jax.numpy as jnp
from jax import lax
from jax.experimental import pallas as pl
from jax.experimental.pallas import tpu as pltpu
from jax.sharding import PartitionSpec as P

HD = 128
BLOCK = 128
LOG2E = 1.4426950408889634

masked_fill = -1e30


def padded(block, sides, width):
    for axis, dim in sides:
        count = lax.axis_size(axis)
        forward = [(i, i + 1) for i in range(count - 1)]
        backward = [(target, source) for source, target in forward]
        low = lax.ppermute(
            lax.slice_in_dim(block, block.shape[dim] - width, None, axis=dim), axis, forward
        )
        high = lax.ppermute(lax.slice_in_dim(block, 0, width, axis=dim), axis, backward)
        block = jnp.concatenate([low, block, high], axis=dim)
    return block


def any_frames(queries, keys, values, band_blocks):
    frame_rows, columns = queries.shape
    frames = lax.axis_size("tm")
    current = lax.axis_index("tm")
    half_rows = frame_rows // 2
    frame_blocks = frame_rows // BLOCK
    capacity = band_blocks.shape[2]
    heads_dev = columns // HD
    paired = jnp.stack([keys, values], 0)
    near_kv = padded(paired, (("tm", 1),), half_rows)
    position = jnp.arange(2 * frame_rows)
    near_ok = ((position >= half_rows) | (current > 0)) & (
        (position < half_rows + frame_rows) | (current < frames - 1)
    )
    kv_blocks = jnp.concatenate(
        [
            paired.reshape(2, frame_blocks, BLOCK, columns),
            jnp.zeros((2, 1, BLOCK, columns), jnp.bfloat16),
        ],
        1,
    )
    outgoing = lax.dynamic_index_in_dim(band_blocks, current, 1, keepdims=False)
    incoming = lax.dynamic_index_in_dim(band_blocks, current, 0, keepdims=False)
    outbound = jnp.take(kv_blocks, outgoing, axis=1)
    arrived = lax.all_to_all(outbound, "tm", split_axis=1, concat_axis=1, tiled=True)
    far_kv = arrived.reshape(2, frames * capacity * BLOCK, columns)
    far_ok = jnp.repeat((incoming != frame_blocks).reshape(-1), BLOCK)
    all_kv = jnp.concatenate([near_kv, far_kv], 1)
    visible = jnp.concatenate([near_ok, far_ok], 0)
    inv_root = HD ** (-0.5)

    def per_head(head_at):
        start = head_at * HD
        query_head = lax.dynamic_slice_in_dim(queries, start, HD, 1)
        key_head = lax.dynamic_slice_in_dim(all_kv[0], start, HD, 1)
        value_head = lax.dynamic_slice_in_dim(all_kv[1], start, HD, 1)
        scores = (
            lax.dot_general(
                query_head, key_head, (((1,), (1,)), ((), ())), preferred_element_type=jnp.float32
            )
            * inv_root
        )
        scores = jnp.where(visible[None, :], scores, masked_fill)
        row_max = jnp.max(scores, axis=1, keepdims=True)
        powers = jnp.exp(scores - row_max)
        row_sum = jnp.sum(powers, axis=1, keepdims=True)
        mixed_sum = jnp.dot(
            powers.astype(jnp.bfloat16), value_head, preferred_element_type=jnp.float32
        )
        return (mixed_sum / row_sum).astype(jnp.bfloat16)

    result = lax.map(per_head, jnp.arange(heads_dev, dtype=jnp.int32))
    return jnp.transpose(result, (1, 0, 2)).reshape(frame_rows, columns)


def run_copies(copies):
    for copy in copies:
        copy.start()
    for copy in copies:
        copy.wait()


def pick_kernel(groups, width, bands, keys, values, extra, *rest):
    direct, sems = rest[:groups], rest[groups]
    frame = lax.axis_index("tm")
    inner = (frame == 1) | (frame == 2)

    @pl.when(inner)
    def _():
        block = jnp.where(frame == 1, bands[3, 1, 0], bands[0, 2, 1])
        run_copies(
            [
                pltpu.make_async_copy(src.at[pl.ds(block * BLOCK, BLOCK)], extra.at[kv], sems.at[kv])
                for kv, src in enumerate((keys, values))
            ]
        )

    @pl.when(jnp.logical_not(inner))
    def _():
        other = 3 - frame
        copies = []
        for g in range(groups):
            for kv, src in enumerate((keys, values)):
                for slot in range(2):
                    block = bands[other, frame, slot]
                    copies.append(
                        pltpu.make_async_copy(
                            src.at[pl.ds(block * BLOCK, BLOCK), pl.ds(g * width, width)],
                            direct[g].at[kv, pl.ds(slot * BLOCK, BLOCK)],
                            sems.at[len(copies)],
                        )
                    )
        run_copies(copies)


def relay_kernel(groups, width, bands, keys, values, low, high, extra, *rest):
    relayed, sems = rest[:groups], rest[groups]
    frame = lax.axis_index("tm")

    def hand_on(source, picked):
        copies = []
        for g in range(groups):
            for kv in range(2):
                cols = pl.ds(g * width, width)
                copies.append(
                    pltpu.make_async_copy(
                        source.at[kv, pl.ds(picked * BLOCK, BLOCK), cols],
                        relayed[g].at[kv, pl.ds(0, BLOCK)],
                        sems.at[len(copies)],
                    )
                )
                copies.append(
                    pltpu.make_async_copy(
                        extra.at[kv, :, cols],
                        relayed[g].at[kv, pl.ds(BLOCK, BLOCK)],
                        sems.at[len(copies)],
                    )
                )
        run_copies(copies)

    @pl.when(frame == 1)
    def _():
        hand_on(high, bands[0, 2, 0])

    @pl.when(frame == 2)
    def _():
        hand_on(low, bands[3, 1, 1] - 2)

    @pl.when((frame == 0) | (frame == 3))
    def _():
        other = jnp.where(frame == 0, 2, 1)
        copies = []
        for g in range(groups):
            for kv, src in enumerate((keys, values)):
                for slot in range(2):
                    block = bands[other, frame, slot]
                    copies.append(
                        pltpu.make_async_copy(
                            src.at[pl.ds(block * BLOCK, BLOCK), pl.ds(g * width, width)],
                            relayed[g].at[kv, pl.ds(slot * BLOCK, BLOCK)],
                            sems.at[len(copies)],
                        )
                    )
        run_copies(copies)


def attend_kernel(chunk, queries, keys, values, low, high, relayed, direct, *rest):
    out = rest[-1]
    frame = lax.axis_index("tm")
    first = frame == 0
    edge = first | (frame == 3)

    def all_rows(own, kv):
        return jnp.concatenate(
            [
                own[...],
                jnp.where(first, high[kv], low[kv]),
                jnp.where(edge, direct[kv], high[kv]),
                relayed[kv],
            ],
            0,
        )

    key_rows = all_rows(keys, 0)
    value_rows = all_rows(values, 1)
    rate = LOG2E * HD ** (-0.5)
    for start in range(0, queries.shape[0], chunk):
        scores = lax.dot_general(
            queries[pl.ds(start, chunk)],
            key_rows,
            (((1,), (1,)), ((), ())),
            preferred_element_type=jnp.float32,
        )
        row_max = jnp.max(scores, axis=1, keepdims=True)
        powers = jnp.exp2((scores - row_max) * rate)
        row_sum = jnp.sum(powers, axis=1, keepdims=True)
        mixed = jnp.dot(powers.astype(jnp.bfloat16), value_rows, preferred_element_type=jnp.float32)
        out[pl.ds(start, chunk)] = (mixed / row_sum).astype(jnp.bfloat16)


def four_frames(queries, keys, values, band_blocks):
    rows, columns = queries.shape
    half = rows // 2
    heads = columns // HD
    groups = 4 if heads % 4 == 0 else 1
    width = columns // groups
    group_heads = heads // groups
    anywhere = pl.BlockSpec(memory_space=pl.ANY)
    scalars = pl.BlockSpec(memory_space=pltpu.SMEM)

    low = lax.ppermute(
        jnp.stack([keys[half:], values[half:]], 0), "tm", [(0, 1), (1, 2), (2, 3)]
    )
    high = lax.ppermute(
        jnp.stack([keys[:half], values[:half]], 0), "tm", [(1, 0), (2, 1), (3, 2)]
    )
    pair = jax.ShapeDtypeStruct((2, 2 * BLOCK, width), jnp.bfloat16)
    extra, *direct = pl.pallas_call(
        functools.partial(pick_kernel, groups, width),
        out_shape=[jax.ShapeDtypeStruct((2, BLOCK, columns), jnp.bfloat16)] + [pair] * groups,
        in_specs=[scalars, anywhere, anywhere],
        out_specs=[anywhere] * (1 + groups),
        scratch_shapes=[pltpu.SemaphoreType.DMA((4 * groups,))],
        name="pick_blocks",
    )(band_blocks, keys, values)
    extra = lax.ppermute(extra, "tm", [(1, 2), (2, 1)])
    direct = [lax.ppermute(part, "tm", [(0, 3), (3, 0)]) for part in direct]
    relayed = pl.pallas_call(
        functools.partial(relay_kernel, groups, width),
        out_shape=[pair] * groups,
        in_specs=[scalars] + [anywhere] * 5,
        out_specs=[anywhere] * groups,
        scratch_shapes=[pltpu.SemaphoreType.DMA((4 * groups,))],
        name="relay_blocks",
    )(band_blocks, keys, values, low, high, extra)
    relayed = [lax.ppermute(part, "tm", [(0, 2), (3, 1), (2, 3), (1, 0)]) for part in relayed]

    result = None
    for g in range(groups):
        own = pl.BlockSpec((rows, HD), lambda h, g=g: (0, g * group_heads + h))
        near = pl.BlockSpec((2, half, HD), lambda h, g=g: (0, 0, g * group_heads + h))
        far = pl.BlockSpec((2, half, HD), lambda h: (0, 0, h))
        in_specs = [own, own, own, near, near, far, far]
        operands = [queries, keys, values, low, high, relayed[g], direct[g]]
        aliases = {}
        if result is not None:
            aliases = {len(operands): 0}
            in_specs.append(anywhere)
            operands.append(result)
        seen = rows + 3 * half
        result = pl.pallas_call(
            functools.partial(attend_kernel, rows // 2),
            grid=(group_heads,),
            out_shape=jax.ShapeDtypeStruct(queries.shape, queries.dtype),
            in_specs=in_specs,
            out_specs=own,
            input_output_aliases=aliases,
            compiler_params=pltpu.CompilerParams(vmem_limit_bytes=32 << 20),
            cost_estimate=pl.CostEstimate(
                flops=4 * group_heads * rows * seen * HD,
                bytes_accessed=2 * width * (2 * rows + 2 * (rows + 4 * half)),
                transcendentals=group_heads * rows * seen,
            ),
            name=f"attend_{g}",
        )(*operands)
    return result


def shards(queries, keys, values, band_blocks):
    if lax.axis_size("tm") == 4 and queries.shape[0] == 4 * BLOCK and band_blocks.shape[2] == 2:
        return four_frames(queries, keys, values, band_blocks)
    return any_frames(queries, keys, values, band_blocks)


def solution(mesh):
    placed = (
        P(("groups", "tm"), ("head", "sub")),
        P(("groups", "tm"), ("head", "sub")),
        P(("groups", "tm"), ("head", "sub")),
        P(),
    )
    return jax.shard_map(
        shards,
        mesh=mesh,
        in_specs=placed,
        out_specs=P(("groups", "tm"), ("head", "sub")),
        check_vma=False,
    )
```

```python
import functools

import jax
import jax.numpy as jnp
from jax import lax
from jax.experimental import pallas as pl
from jax.experimental.pallas import tpu as pltpu
from jax.sharding import PartitionSpec as P

HD = 128
BLOCK = 128
LOG2E = 1.4426950408889634

masked_fill = -1e30


def padded(block, sides, width):
    for axis, dim in sides:
        count = lax.axis_size(axis)
        forward = [(i, i + 1) for i in range(count - 1)]
        backward = [(target, source) for source, target in forward]
        low = lax.ppermute(
            lax.slice_in_dim(block, block.shape[dim] - width, None, axis=dim), axis, forward
        )
        high = lax.ppermute(lax.slice_in_dim(block, 0, width, axis=dim), axis, backward)
        block = jnp.concatenate([low, block, high], axis=dim)
    return block


def any_frames(queries, keys, values, band_blocks):
    frame_rows, columns = queries.shape
    frames = lax.axis_size("tm")
    current = lax.axis_index("tm")
    half_rows = frame_rows // 2
    frame_blocks = frame_rows // BLOCK
    capacity = band_blocks.shape[2]
    heads_dev = columns // HD
    paired = jnp.stack([keys, values], 0)
    near_kv = padded(paired, (("tm", 1),), half_rows)
    position = jnp.arange(2 * frame_rows)
    near_ok = ((position >= half_rows) | (current > 0)) & (
        (position < half_rows + frame_rows) | (current < frames - 1)
    )
    kv_blocks = jnp.concatenate(
        [
            paired.reshape(2, frame_blocks, BLOCK, columns),
            jnp.zeros((2, 1, BLOCK, columns), jnp.bfloat16),
        ],
        1,
    )
    outgoing = lax.dynamic_index_in_dim(band_blocks, current, 1, keepdims=False)
    incoming = lax.dynamic_index_in_dim(band_blocks, current, 0, keepdims=False)
    outbound = jnp.take(kv_blocks, outgoing, axis=1)
    arrived = lax.all_to_all(outbound, "tm", split_axis=1, concat_axis=1, tiled=True)
    far_kv = arrived.reshape(2, frames * capacity * BLOCK, columns)
    far_ok = jnp.repeat((incoming != frame_blocks).reshape(-1), BLOCK)
    all_kv = jnp.concatenate([near_kv, far_kv], 1)
    visible = jnp.concatenate([near_ok, far_ok], 0)
    inv_root = HD ** (-0.5)

    def per_head(head_at):
        start = head_at * HD
        query_head = lax.dynamic_slice_in_dim(queries, start, HD, 1)
        key_head = lax.dynamic_slice_in_dim(all_kv[0], start, HD, 1)
        value_head = lax.dynamic_slice_in_dim(all_kv[1], start, HD, 1)
        scores = (
            lax.dot_general(
                query_head, key_head, (((1,), (1,)), ((), ())), preferred_element_type=jnp.float32
            )
            * inv_root
        )
        scores = jnp.where(visible[None, :], scores, masked_fill)
        row_max = jnp.max(scores, axis=1, keepdims=True)
        powers = jnp.exp(scores - row_max)
        row_sum = jnp.sum(powers, axis=1, keepdims=True)
        mixed_sum = jnp.dot(
            powers.astype(jnp.bfloat16), value_head, preferred_element_type=jnp.float32
        )
        return (mixed_sum / row_sum).astype(jnp.bfloat16)

    result = lax.map(per_head, jnp.arange(heads_dev, dtype=jnp.int32))
    return jnp.transpose(result, (1, 0, 2)).reshape(frame_rows, columns)


def pick_kernel(groups, width, bands, keys, values, extra, edge, *direct):
    frame = lax.axis_index("tm")
    inner = (frame == 1) | (frame == 2)

    @pl.when(inner)
    def _():
        block = jnp.where(frame == 1, bands[3, 1, 0], bands[0, 2, 1])
        rows = pl.ds(pl.multiple_of(block * BLOCK, BLOCK), BLOCK)
        extra[0] = keys[rows]
        extra[1] = values[rows]

    @pl.when(jnp.logical_not(inner))
    def _():
        for slot in range(2):
            to = pl.ds(slot * BLOCK, BLOCK)
            near = bands[jnp.where(frame == 0, 2, 1), frame, slot]
            far = bands[3 - frame, frame, slot]
            near_rows = pl.ds(pl.multiple_of(near * BLOCK, BLOCK), BLOCK)
            far_rows = pl.ds(pl.multiple_of(far * BLOCK, BLOCK), BLOCK)
            for kv, source in enumerate((keys, values)):
                edge[kv, to] = source[near_rows]
                for g in range(groups):
                    direct[g][kv, to] = source[far_rows, pl.ds(g * width, width)]


def relay_kernel(groups, width, bands, edge, low, high, extra, *relayed):
    frame = lax.axis_index("tm")

    def hand_on(source, picked):
        rows = pl.ds(pl.multiple_of(picked * BLOCK, BLOCK), BLOCK)
        for g in range(groups):
            cols = pl.ds(g * width, width)
            relayed[g][:, pl.ds(0, BLOCK)] = source[:, rows, cols]
            relayed[g][:, pl.ds(BLOCK, BLOCK)] = extra[:, :, cols]

    @pl.when(frame == 1)
    def _():
        hand_on(high, bands[0, 2, 0])

    @pl.when(frame == 2)
    def _():
        hand_on(low, bands[3, 1, 1] - 2)

    @pl.when((frame == 0) | (frame == 3))
    def _():
        for g in range(groups):
            relayed[g][...] = edge[:, :, pl.ds(g * width, width)]


def attend_kernel(chunk, queries, keys, values, low, high, relayed, direct, *rest):
    out = rest[-1]
    frame = lax.axis_index("tm")
    first = frame == 0
    edge = first | (frame == 3)

    def all_rows(own, kv):
        return jnp.concatenate(
            [
                own[...],
                jnp.where(first, high[kv], low[kv]),
                jnp.where(edge, direct[kv], high[kv]),
                relayed[kv],
            ],
            0,
        )

    key_rows = all_rows(keys, 0)
    value_rows = all_rows(values, 1)
    rate = LOG2E * HD ** (-0.5)
    for start in range(0, queries.shape[0], chunk):
        scores = lax.dot_general(
            queries[pl.ds(start, chunk)],
            key_rows,
            (((1,), (1,)), ((), ())),
            preferred_element_type=jnp.float32,
        )
        row_max = jnp.max(scores, axis=1, keepdims=True)
        powers = jnp.exp2((scores - row_max) * rate)
        row_sum = jnp.sum(powers, axis=1, keepdims=True)
        mixed = jnp.dot(powers.astype(jnp.bfloat16), value_rows, preferred_element_type=jnp.float32)
        out[pl.ds(start, chunk)] = (mixed / row_sum).astype(jnp.bfloat16)


def four_frames(queries, keys, values, band_blocks):
    rows, columns = queries.shape
    half = rows // 2
    heads = columns // HD
    groups = 4 if heads % 4 == 0 else 1
    width = columns // groups
    group_heads = heads // groups
    anywhere = pl.BlockSpec(memory_space=pl.ANY)
    local = pl.BlockSpec(memory_space=pltpu.VMEM)
    scalars = pl.BlockSpec(memory_space=pltpu.SMEM)

    low = lax.ppermute(
        jnp.stack([keys[half:], values[half:]], 0), "tm", [(0, 1), (1, 2), (2, 3)]
    )
    high = lax.ppermute(
        jnp.stack([keys[:half], values[:half]], 0), "tm", [(1, 0), (2, 1), (3, 2)]
    )
    pair = jax.ShapeDtypeStruct((2, 2 * BLOCK, width), jnp.bfloat16)
    extra, edge, *direct = pl.pallas_call(
        functools.partial(pick_kernel, groups, width),
        out_shape=[
            jax.ShapeDtypeStruct((2, BLOCK, columns), jnp.bfloat16),
            jax.ShapeDtypeStruct((2, 2 * BLOCK, columns), jnp.bfloat16),
        ]
        + [pair] * groups,
        in_specs=[scalars, local, local],
        out_specs=[local] * (2 + groups),
        compiler_params=pltpu.CompilerParams(vmem_limit_bytes=32 << 20),
        name="pick_blocks",
    )(band_blocks, keys, values)
    extra = lax.ppermute(extra, "tm", [(1, 2), (2, 1)])
    direct = [lax.ppermute(part, "tm", [(0, 3), (3, 0)]) for part in direct]
    relayed = pl.pallas_call(
        functools.partial(relay_kernel, groups, width),
        out_shape=[pair] * groups,
        in_specs=[scalars] + [local] * 4,
        out_specs=[local] * groups,
        compiler_params=pltpu.CompilerParams(vmem_limit_bytes=32 << 20),
        name="relay_blocks",
    )(band_blocks, edge, low, high, extra)
    relayed = [lax.ppermute(part, "tm", [(0, 2), (3, 1), (2, 3), (1, 0)]) for part in relayed]

    result = None
    for g in range(groups):
        own = pl.BlockSpec((rows, HD), lambda h, g=g: (0, g * group_heads + h))
        near = pl.BlockSpec((2, half, HD), lambda h, g=g: (0, 0, g * group_heads + h))
        far = pl.BlockSpec((2, half, HD), lambda h: (0, 0, h))
        in_specs = [own, own, own, near, near, far, far]
        operands = [queries, keys, values, low, high, relayed[g], direct[g]]
        aliases = {}
        if result is not None:
            aliases = {len(operands): 0}
            in_specs.append(anywhere)
            operands.append(result)
        seen = rows + 3 * half
        result = pl.pallas_call(
            functools.partial(attend_kernel, rows // 2),
            grid=(group_heads,),
            out_shape=jax.ShapeDtypeStruct(queries.shape, queries.dtype),
            in_specs=in_specs,
            out_specs=own,
            input_output_aliases=aliases,
            compiler_params=pltpu.CompilerParams(vmem_limit_bytes=32 << 20),
            cost_estimate=pl.CostEstimate(
                flops=4 * group_heads * rows * seen * HD,
                bytes_accessed=2 * width * (2 * rows + 2 * (rows + 4 * half)),
                transcendentals=group_heads * rows * seen,
            ),
            name=f"attend_{g}",
        )(*operands)
    return result


def shards(queries, keys, values, band_blocks):
    if lax.axis_size("tm") == 4 and queries.shape[0] == 4 * BLOCK and band_blocks.shape[2] == 2:
        return four_frames(queries, keys, values, band_blocks)
    return any_frames(queries, keys, values, band_blocks)


def solution(mesh):
    placed = (
        P(("groups", "tm"), ("head", "sub")),
        P(("groups", "tm"), ("head", "sub")),
        P(("groups", "tm"), ("head", "sub")),
        P(),
    )
    return jax.shard_map(
        shards,
        mesh=mesh,
        in_specs=placed,
        out_specs=P(("groups", "tm"), ("head", "sub")),
        check_vma=False,
    )
```

```python
import functools

import jax
import jax.numpy as jnp
from jax import lax
from jax.experimental import pallas as pl
from jax.experimental.pallas import tpu as pltpu
from jax.sharding import PartitionSpec as P

HD = 128
BLOCK = 128
LOG2E = 1.4426950408889634

masked_fill = -1e30


def padded(block, sides, width):
    for axis, dim in sides:
        count = lax.axis_size(axis)
        forward = [(i, i + 1) for i in range(count - 1)]
        backward = [(target, source) for source, target in forward]
        low = lax.ppermute(
            lax.slice_in_dim(block, block.shape[dim] - width, None, axis=dim), axis, forward
        )
        high = lax.ppermute(lax.slice_in_dim(block, 0, width, axis=dim), axis, backward)
        block = jnp.concatenate([low, block, high], axis=dim)
    return block


def any_frames(queries, keys, values, band_blocks):
    frame_rows, columns = queries.shape
    frames = lax.axis_size("tm")
    current = lax.axis_index("tm")
    half_rows = frame_rows // 2
    frame_blocks = frame_rows // BLOCK
    capacity = band_blocks.shape[2]
    heads_dev = columns // HD
    paired = jnp.stack([keys, values], 0)
    near_kv = padded(paired, (("tm", 1),), half_rows)
    position = jnp.arange(2 * frame_rows)
    near_ok = ((position >= half_rows) | (current > 0)) & (
        (position < half_rows + frame_rows) | (current < frames - 1)
    )
    kv_blocks = jnp.concatenate(
        [
            paired.reshape(2, frame_blocks, BLOCK, columns),
            jnp.zeros((2, 1, BLOCK, columns), jnp.bfloat16),
        ],
        1,
    )
    outgoing = lax.dynamic_index_in_dim(band_blocks, current, 1, keepdims=False)
    incoming = lax.dynamic_index_in_dim(band_blocks, current, 0, keepdims=False)
    outbound = jnp.take(kv_blocks, outgoing, axis=1)
    arrived = lax.all_to_all(outbound, "tm", split_axis=1, concat_axis=1, tiled=True)
    far_kv = arrived.reshape(2, frames * capacity * BLOCK, columns)
    far_ok = jnp.repeat((incoming != frame_blocks).reshape(-1), BLOCK)
    all_kv = jnp.concatenate([near_kv, far_kv], 1)
    visible = jnp.concatenate([near_ok, far_ok], 0)
    inv_root = HD ** (-0.5)

    def per_head(head_at):
        start = head_at * HD
        query_head = lax.dynamic_slice_in_dim(queries, start, HD, 1)
        key_head = lax.dynamic_slice_in_dim(all_kv[0], start, HD, 1)
        value_head = lax.dynamic_slice_in_dim(all_kv[1], start, HD, 1)
        scores = (
            lax.dot_general(
                query_head, key_head, (((1,), (1,)), ((), ())), preferred_element_type=jnp.float32
            )
            * inv_root
        )
        scores = jnp.where(visible[None, :], scores, masked_fill)
        row_max = jnp.max(scores, axis=1, keepdims=True)
        powers = jnp.exp(scores - row_max)
        row_sum = jnp.sum(powers, axis=1, keepdims=True)
        mixed_sum = jnp.dot(
            powers.astype(jnp.bfloat16), value_head, preferred_element_type=jnp.float32
        )
        return (mixed_sum / row_sum).astype(jnp.bfloat16)

    result = lax.map(per_head, jnp.arange(heads_dev, dtype=jnp.int32))
    return jnp.transpose(result, (1, 0, 2)).reshape(frame_rows, columns)


def near_kernel(half, keys, values, up, down, sems):
    copies = [
        pltpu.make_async_copy(source.at[pl.ds(start, half)], target.at[kv], sems.at[way, kv])
        for way, (target, start) in enumerate(((up, half), (down, 0)))
        for kv, source in enumerate((keys, values))
    ]
    for copy in copies:
        copy.start()
    for copy in copies:
        copy.wait()


def pick_kernel(cuts, bands, keys, values, extra, *far):
    frame = lax.axis_index("tm")
    inner = (frame == 1) | (frame == 2)

    @pl.when(inner)
    def _():
        block = jnp.where(frame == 1, bands[3, 1, 0], bands[0, 2, 1])
        rows = pl.ds(pl.multiple_of(block * BLOCK, BLOCK), BLOCK)
        extra[0] = keys[rows]
        extra[1] = values[rows]

    @pl.when(jnp.logical_not(inner))
    def _():
        for target, parts in enumerate((far[: len(cuts)], far[len(cuts) :])):
            reader = jnp.where(frame == 0, 2 + target, 1 - target)
            for slot in range(2):
                block = bands[reader, frame, slot]
                rows = pl.ds(pl.multiple_of(block * BLOCK, BLOCK), BLOCK)
                for part, (first, size) in zip(parts, cuts):
                    for kv, source in enumerate((keys, values)):
                        part[kv, pl.ds(slot * BLOCK, BLOCK)] = source[rows, pl.ds(first, size)]


def relay_kernel(cuts, bands, low, high, extra, *relayed):
    frame = lax.axis_index("tm")

    def hand_on(source, picked):
        rows = pl.ds(pl.multiple_of(picked * BLOCK, BLOCK), BLOCK)
        for part, (first, size) in zip(relayed, cuts):
            cols = pl.ds(first, size)
            part[:, pl.ds(0, BLOCK)] = source[:, rows, cols]
            part[:, pl.ds(BLOCK, BLOCK)] = extra[:, :, cols]

    @pl.when(frame == 1)
    def _():
        hand_on(high, bands[0, 2, 0])

    @pl.when(frame == 2)
    def _():
        hand_on(low, bands[3, 1, 1] - 2)


def attend_kernel(chunk, queries, keys, values, low, high, relayed, crossed, direct, *rest):
    out = rest[-1]
    frame = lax.axis_index("tm")
    first = frame == 0
    edge = first | (frame == 3)

    def all_rows(own, kv):
        return jnp.concatenate(
            [
                own[...],
                jnp.where(first, high[kv], low[kv]),
                jnp.where(edge, direct[kv], high[kv]),
                jnp.where(edge, relayed[kv], crossed[kv]),
            ],
            0,
        )

    key_rows = all_rows(keys, 0)
    value_rows = all_rows(values, 1)
    rate = LOG2E * HD ** (-0.5)
    for start in range(0, queries.shape[0], chunk):
        scores = lax.dot_general(
            queries[pl.ds(start, chunk)],
            key_rows,
            (((1,), (1,)), ((), ())),
            preferred_element_type=jnp.float32,
        )
        row_max = jnp.max(scores, axis=1, keepdims=True)
        powers = jnp.exp2((scores - row_max) * rate)
        row_sum = jnp.sum(powers, axis=1, keepdims=True)
        mixed = jnp.dot(powers.astype(jnp.bfloat16), value_rows, preferred_element_type=jnp.float32)
        out[pl.ds(start, chunk)] = (mixed / row_sum).astype(jnp.bfloat16)


def four_frames(queries, keys, values, band_blocks):
    rows, columns = queries.shape
    half = rows // 2
    heads = columns // HD
    last = heads // 4
    cuts = ((0, (heads - last) * HD), ((heads - last) * HD, last * HD)) if last else ((0, columns),)
    anywhere = pl.BlockSpec(memory_space=pl.ANY)
    local = pl.BlockSpec(memory_space=pltpu.VMEM)
    scalars = pl.BlockSpec(memory_space=pltpu.SMEM)
    roomy = pltpu.CompilerParams(vmem_limit_bytes=32 << 20)

    def send(array, pairs):
        return lax.ppermute(array, "tm", pairs)

    near = jax.ShapeDtypeStruct((2, half, columns), jnp.bfloat16)
    up, down = pl.pallas_call(
        functools.partial(near_kernel, half),
        out_shape=[near] * 2,
        in_specs=[pl.BlockSpec(memory_space=pltpu.HBM)] * 2,
        out_specs=[local] * 2,
        scratch_shapes=[pltpu.SemaphoreType.DMA((2, 2))],
        compiler_params=roomy,
        name="near_halves",
    )(keys, values)
    low = send(up, [(0, 1), (1, 2), (2, 3)])
    high = send(down, [(1, 0), (2, 1), (3, 2)])
    parts = [jax.ShapeDtypeStruct((2, half, size), jnp.bfloat16) for _, size in cuts]
    extra, *far = pl.pallas_call(
        functools.partial(pick_kernel, cuts),
        out_shape=[jax.ShapeDtypeStruct((2, BLOCK, columns), jnp.bfloat16)] + parts + parts,
        in_specs=[scalars, local, local],
        out_specs=[local] * (1 + 2 * len(cuts)),
        compiler_params=roomy,
        name="pick_blocks",
    )(band_blocks, keys, values)
    extra = send(extra, [(1, 2), (2, 1)])
    crossed = [send(part, [(0, 2), (3, 1)]) for part in far[: len(cuts)]]
    direct = [send(part, [(0, 3), (3, 0)]) for part in far[len(cuts) :]]
    relayed = pl.pallas_call(
        functools.partial(relay_kernel, cuts),
        out_shape=parts,
        in_specs=[scalars] + [local] * 3,
        out_specs=[local] * len(cuts),
        compiler_params=roomy,
        name="relay_blocks",
    )(band_blocks, low, high, extra)
    relayed = [send(part, [(2, 3), (1, 0)]) for part in relayed]

    result = None
    for g, (first, size) in enumerate(cuts):
        skip = first // HD
        own = pl.BlockSpec((rows, HD), lambda h, skip=skip: (0, skip + h))
        beside = pl.BlockSpec((2, half, HD), lambda h, skip=skip: (0, 0, skip + h))
        away = pl.BlockSpec((2, half, HD), lambda h: (0, 0, h))
        in_specs = [own] * 3 + [beside] * 2 + [away] * 3
        operands = [queries, keys, values, low, high, relayed[g], crossed[g], direct[g]]
        aliases = {}
        if result is not None:
            aliases = {len(operands): 0}
            in_specs.append(anywhere)
            operands.append(result)
        seen = rows + 3 * half
        result = pl.pallas_call(
            functools.partial(attend_kernel, rows // 2),
            grid=(size // HD,),
            out_shape=jax.ShapeDtypeStruct(queries.shape, queries.dtype),
            in_specs=in_specs,
            out_specs=own,
            input_output_aliases=aliases,
            compiler_params=roomy,
            cost_estimate=pl.CostEstimate(
                flops=4 * size * rows * seen,
                bytes_accessed=2 * size * (2 * rows + 2 * (rows + 5 * half)),
                transcendentals=size // HD * rows * seen,
            ),
            name=f"attend_{g}",
        )(*operands)
    return result


def shards(queries, keys, values, band_blocks):
    if lax.axis_size("tm") == 4 and queries.shape[0] == 4 * BLOCK and band_blocks.shape[2] == 2:
        return four_frames(queries, keys, values, band_blocks)
    return any_frames(queries, keys, values, band_blocks)


def solution(mesh):
    placed = (
        P(("groups", "tm"), ("head", "sub")),
        P(("groups", "tm"), ("head", "sub")),
        P(("groups", "tm"), ("head", "sub")),
        P(),
    )
    return jax.shard_map(
        shards,
        mesh=mesh,
        in_specs=placed,
        out_specs=P(("groups", "tm"), ("head", "sub")),
        check_vma=False,
    )
```

```python
import functools

import jax
import jax.numpy as jnp
from jax import lax
from jax.experimental import pallas as pl
from jax.experimental.pallas import tpu as pltpu
from jax.sharding import PartitionSpec as P

HD = 128
BLOCK = 128
LOG2E = 1.4426950408889634

masked_fill = -1e30


def padded(block, sides, width):
    for axis, dim in sides:
        count = lax.axis_size(axis)
        forward = [(i, i + 1) for i in range(count - 1)]
        backward = [(target, source) for source, target in forward]
        low = lax.ppermute(
            lax.slice_in_dim(block, block.shape[dim] - width, None, axis=dim), axis, forward
        )
        high = lax.ppermute(lax.slice_in_dim(block, 0, width, axis=dim), axis, backward)
        block = jnp.concatenate([low, block, high], axis=dim)
    return block


def any_frames(queries, keys, values, band_blocks):
    frame_rows, columns = queries.shape
    frames = lax.axis_size("tm")
    current = lax.axis_index("tm")
    half_rows = frame_rows // 2
    frame_blocks = frame_rows // BLOCK
    capacity = band_blocks.shape[2]
    heads_dev = columns // HD
    paired = jnp.stack([keys, values], 0)
    near_kv = padded(paired, (("tm", 1),), half_rows)
    position = jnp.arange(2 * frame_rows)
    near_ok = ((position >= half_rows) | (current > 0)) & (
        (position < half_rows + frame_rows) | (current < frames - 1)
    )
    kv_blocks = jnp.concatenate(
        [
            paired.reshape(2, frame_blocks, BLOCK, columns),
            jnp.zeros((2, 1, BLOCK, columns), jnp.bfloat16),
        ],
        1,
    )
    outgoing = lax.dynamic_index_in_dim(band_blocks, current, 1, keepdims=False)
    incoming = lax.dynamic_index_in_dim(band_blocks, current, 0, keepdims=False)
    outbound = jnp.take(kv_blocks, outgoing, axis=1)
    arrived = lax.all_to_all(outbound, "tm", split_axis=1, concat_axis=1, tiled=True)
    far_kv = arrived.reshape(2, frames * capacity * BLOCK, columns)
    far_ok = jnp.repeat((incoming != frame_blocks).reshape(-1), BLOCK)
    all_kv = jnp.concatenate([near_kv, far_kv], 1)
    visible = jnp.concatenate([near_ok, far_ok], 0)
    inv_root = HD ** (-0.5)

    def per_head(head_at):
        start = head_at * HD
        query_head = lax.dynamic_slice_in_dim(queries, start, HD, 1)
        key_head = lax.dynamic_slice_in_dim(all_kv[0], start, HD, 1)
        value_head = lax.dynamic_slice_in_dim(all_kv[1], start, HD, 1)
        scores = (
            lax.dot_general(
                query_head, key_head, (((1,), (1,)), ((), ())), preferred_element_type=jnp.float32
            )
            * inv_root
        )
        scores = jnp.where(visible[None, :], scores, masked_fill)
        row_max = jnp.max(scores, axis=1, keepdims=True)
        powers = jnp.exp(scores - row_max)
        row_sum = jnp.sum(powers, axis=1, keepdims=True)
        mixed_sum = jnp.dot(
            powers.astype(jnp.bfloat16), value_head, preferred_element_type=jnp.float32
        )
        return (mixed_sum / row_sum).astype(jnp.bfloat16)

    result = lax.map(per_head, jnp.arange(heads_dev, dtype=jnp.int32))
    return jnp.transpose(result, (1, 0, 2)).reshape(frame_rows, columns)


def run_copies(pairs, sems):
    copies = [
        pltpu.make_async_copy(source, target, sems.at[at])
        for at, (source, target) in enumerate(pairs)
    ]
    for copy in copies:
        copy.start()
    for copy in copies:
        copy.wait()


def rows_of(block):
    return pl.ds(pl.multiple_of(block * BLOCK, BLOCK), BLOCK)


def stage_near_kernel(half, bands, keys, values, inner, beside, sems):
    frame = lax.axis_index("tm")
    rows = pl.ds(pl.multiple_of(lax.rem(frame + 1, 2) * half, half), half)
    near = [
        pltpu.make_async_copy(source.at[rows], beside.at[kv], sems.at[kv])
        for kv, source in enumerate((keys, values))
    ]

    @pl.when((frame == 1) | (frame == 2))
    def _():
        facing = pl.ds(pl.multiple_of((2 - frame) * half, half), half)
        missing = rows_of(jnp.where(frame == 1, bands[3, 0, 1], bands[0, 1, 2]))
        pairs = []
        for kv, source in enumerate((keys, values)):
            pairs.append((source.at[facing], inner.at[kv, pl.ds(0, half)]))
            pairs.append((source.at[missing], inner.at[kv, pl.ds(half, BLOCK)]))
        for copy in near:
            copy.start()
        run_copies(pairs, sems.at[pl.ds(2, 4)])

    @pl.when((frame == 0) | (frame == 3))
    def _():
        for copy in near:
            copy.start()

    for copy in near:
        copy.wait()


def stage_far_kernel(cuts, bands, keys, values, direct, *rest):
    crossed, sems = rest[:-1], rest[-1]
    frame = lax.axis_index("tm")

    @pl.when((frame == 0) | (frame == 3))
    def _():
        reader = jnp.where(frame == 0, 2, 1)
        pairs = []
        for slot in range(2):
            to = pl.ds(slot * BLOCK, BLOCK)
            for kv, source in enumerate((keys, values)):
                rows = rows_of(bands[3 - frame, slot, frame])
                pairs.append((source.at[rows], direct.at[kv, to]))
                rows = rows_of(bands[reader, slot, frame])
                for part, (first, size) in zip(crossed, cuts):
                    pairs.append((source.at[rows, pl.ds(first, size)], part.at[kv, to]))
        run_copies(pairs, sems)


def relay_kernel(half, cuts, bands, inner, *relayed):
    frame = lax.axis_index("tm")

    @pl.when((frame == 1) | (frame == 2))
    def _():
        rows = rows_of(jnp.where(frame == 1, bands[0, 0, 2], bands[3, 1, 1] - 2))
        for part, (first, size) in zip(relayed, cuts):
            cols = pl.ds(first, size)
            part[:, pl.ds(0, BLOCK)] = inner[:, rows, cols]
            part[:, pl.ds(BLOCK, BLOCK)] = inner[:, pl.ds(half, BLOCK), cols]


def attend_kernel(
    chunk, first, size, queries, keys, values, beside, inner, direct, relayed, crossed, *rest
):
    out, mixed_out, sems = rest[-3:]
    frame = lax.axis_index("tm")
    edge = (frame == 0) | (frame == 3)
    rate = LOG2E * HD ** (-0.5)
    rows = queries.shape[0]
    half = rows // 2
    heads = range(size // HD)

    def pieces(head, own, kv):
        here, there = pl.ds(first + head * HD, HD), pl.ds(head * HD, HD)
        return [
            own[:, here],
            beside[kv, :, here],
            jnp.where(edge, direct[kv, :, here], inner[kv, pl.ds(0, half), here]),
            jnp.where(edge, relayed[kv, :, there], crossed[kv, :, there]),
        ]

    def score(head, start):
        rows_q = queries[pl.ds(start, chunk), pl.ds(first + head * HD, HD)]
        return [
            lax.dot_general(
                rows_q, piece, (((1,), (1,)), ((), ())), preferred_element_type=jnp.float32
            )
            for piece in pieces(head, keys, 0)
        ]

    def finish(head, start, scores):
        row_max = functools.reduce(
            jnp.maximum, [jnp.max(part, axis=1, keepdims=True) for part in scores]
        )
        powers = [jnp.exp2((part - row_max) * rate) for part in scores]
        row_sum = sum(jnp.sum(part, axis=1, keepdims=True) for part in powers)
        mixed = sum(
            jnp.dot(part.astype(jnp.bfloat16), piece, preferred_element_type=jnp.float32)
            for part, piece in zip(powers, pieces(head, values, 1))
        )
        mixed_out[head, pl.ds(start, chunk)] = (mixed / row_sum).astype(jnp.bfloat16)

    units = [(head, start) for head in heads for start in range(0, rows, chunk)]
    copies = []
    scores = score(*units[0])
    for unit, following in zip(units, units[1:] + [None]):
        ahead = score(*following) if following else None
        finish(*unit, scores)
        scores = ahead
        head, start = unit
        if start + chunk == rows:
            copies.append(
                pltpu.make_async_copy(
                    mixed_out.at[head], out.at[:, pl.ds(first + head * HD, HD)], sems.at[head]
                )
            )
            copies[-1].start()
    for copy in copies:
        copy.wait()


def four_frames(queries, keys, values, band_blocks):
    rows, columns = queries.shape
    half = rows // 2
    heads = columns // HD
    last = heads // 4
    cuts = [(0, heads - 2 * last), (heads - 2 * last, last), (heads - last, last)]
    cuts = [(first * HD, size * HD) for first, size in cuts if size]
    anywhere = pl.BlockSpec(memory_space=pl.ANY)
    local = pl.BlockSpec(memory_space=pltpu.VMEM)
    scalars = pl.BlockSpec(memory_space=pltpu.SMEM)
    roomy = pltpu.CompilerParams(vmem_limit_bytes=32 << 20)

    def send(array, pairs):
        return lax.ppermute(array, "tm", pairs)

    bands = jnp.transpose(band_blocks, (0, 2, 1))
    facing = jax.ShapeDtypeStruct((2, half, columns), jnp.bfloat16)
    more = jax.ShapeDtypeStruct((2, half + BLOCK, columns), jnp.bfloat16)
    parts = [jax.ShapeDtypeStruct((2, half, size), jnp.bfloat16) for _, size in cuts]

    def stage(kernel, shapes, copies, name):
        return pl.pallas_call(
            kernel,
            out_shape=shapes,
            in_specs=[scalars, anywhere, anywhere],
            out_specs=[local] * len(shapes),
            scratch_shapes=[pltpu.SemaphoreType.DMA((copies,))],
            compiler_params=pltpu.CompilerParams(vmem_limit_bytes=60 << 20),
            name=name,
        )(bands, keys, values)

    inner, beside = stage(
        functools.partial(stage_near_kernel, half), [more, facing], 6, "stage_near"
    )
    direct, *crossed = stage(
        functools.partial(stage_far_kernel, cuts),
        [facing] + parts,
        4 * (1 + len(cuts)),
        "stage_far",
    )
    inner = send(inner, [(1, 2), (2, 1)])
    beside = send(beside, [(0, 1), (1, 0), (2, 3), (3, 2)])
    direct = send(direct, [(0, 3), (3, 0)])
    crossed = [send(part, [(0, 2), (3, 1)]) for part in crossed]
    relayed = pl.pallas_call(
        functools.partial(relay_kernel, half, cuts),
        out_shape=parts,
        in_specs=[scalars, local],
        out_specs=[local] * len(cuts),
        compiler_params=roomy,
        name="relay",
    )(bands, inner)
    relayed = [send(part, [(2, 3), (1, 0)]) for part in relayed]

    result = None
    seen = rows + 3 * half
    for g, (first, size) in enumerate(cuts):
        operands = [queries, keys, values, beside, inner, direct, relayed[g], crossed[g]]
        in_specs = [local] * len(operands)
        aliases = {}
        if result is not None:
            aliases = {len(operands): 0}
            in_specs.append(anywhere)
            operands.append(result)
        result = pl.pallas_call(
            functools.partial(attend_kernel, rows // 2, first, size),
            out_shape=jax.ShapeDtypeStruct(queries.shape, queries.dtype),
            in_specs=in_specs,
            out_specs=anywhere,
            input_output_aliases=aliases,
            scratch_shapes=[
                pltpu.VMEM((size // HD, rows, HD), jnp.bfloat16),
                pltpu.SemaphoreType.DMA((size // HD,)),
            ],
            compiler_params=roomy,
            cost_estimate=pl.CostEstimate(
                flops=4 * size * rows * seen,
                bytes_accessed=2 * size * (2 * rows + 2 * (rows + 4 * half)),
                transcendentals=size // HD * rows * seen,
            ),
            name=f"attend_{g}",
        )(*operands)
    return result


def shards(queries, keys, values, band_blocks):
    if lax.axis_size("tm") == 4 and queries.shape[0] == 4 * BLOCK and band_blocks.shape[2] == 2:
        return four_frames(queries, keys, values, band_blocks)
    return any_frames(queries, keys, values, band_blocks)


def solution(mesh):
    placed = (
        P(("groups", "tm"), ("head", "sub")),
        P(("groups", "tm"), ("head", "sub")),
        P(("groups", "tm"), ("head", "sub")),
        P(),
    )
    return jax.shard_map(
        shards,
        mesh=mesh,
        in_specs=placed,
        out_specs=P(("groups", "tm"), ("head", "sub")),
        check_vma=False,
    )
```

```python
import functools

import jax
import jax.numpy as jnp
from jax import lax
from jax.experimental import pallas as pl
from jax.experimental.pallas import tpu as pltpu
from jax.sharding import PartitionSpec as P

HD = 128
BLOCK = 128
LOG2E = 1.4426950408889634

masked_fill = -1e30


def padded(block, sides, width):
    for axis, dim in sides:
        count = lax.axis_size(axis)
        forward = [(i, i + 1) for i in range(count - 1)]
        backward = [(target, source) for source, target in forward]
        low = lax.ppermute(
            lax.slice_in_dim(block, block.shape[dim] - width, None, axis=dim), axis, forward
        )
        high = lax.ppermute(lax.slice_in_dim(block, 0, width, axis=dim), axis, backward)
        block = jnp.concatenate([low, block, high], axis=dim)
    return block


def any_frames(queries, keys, values, band_blocks):
    frame_rows, columns = queries.shape
    frames = lax.axis_size("tm")
    current = lax.axis_index("tm")
    half_rows = frame_rows // 2
    frame_blocks = frame_rows // BLOCK
    capacity = band_blocks.shape[2]
    heads_dev = columns // HD
    paired = jnp.stack([keys, values], 0)
    near_kv = padded(paired, (("tm", 1),), half_rows)
    position = jnp.arange(2 * frame_rows)
    near_ok = ((position >= half_rows) | (current > 0)) & (
        (position < half_rows + frame_rows) | (current < frames - 1)
    )
    kv_blocks = jnp.concatenate(
        [
            paired.reshape(2, frame_blocks, BLOCK, columns),
            jnp.zeros((2, 1, BLOCK, columns), jnp.bfloat16),
        ],
        1,
    )
    outgoing = lax.dynamic_index_in_dim(band_blocks, current, 1, keepdims=False)
    incoming = lax.dynamic_index_in_dim(band_blocks, current, 0, keepdims=False)
    outbound = jnp.take(kv_blocks, outgoing, axis=1)
    arrived = lax.all_to_all(outbound, "tm", split_axis=1, concat_axis=1, tiled=True)
    far_kv = arrived.reshape(2, frames * capacity * BLOCK, columns)
    far_ok = jnp.repeat((incoming != frame_blocks).reshape(-1), BLOCK)
    all_kv = jnp.concatenate([near_kv, far_kv], 1)
    visible = jnp.concatenate([near_ok, far_ok], 0)
    inv_root = HD ** (-0.5)

    def per_head(head_at):
        start = head_at * HD
        query_head = lax.dynamic_slice_in_dim(queries, start, HD, 1)
        key_head = lax.dynamic_slice_in_dim(all_kv[0], start, HD, 1)
        value_head = lax.dynamic_slice_in_dim(all_kv[1], start, HD, 1)
        scores = (
            lax.dot_general(
                query_head, key_head, (((1,), (1,)), ((), ())), preferred_element_type=jnp.float32
            )
            * inv_root
        )
        scores = jnp.where(visible[None, :], scores, masked_fill)
        row_max = jnp.max(scores, axis=1, keepdims=True)
        powers = jnp.exp(scores - row_max)
        row_sum = jnp.sum(powers, axis=1, keepdims=True)
        mixed_sum = jnp.dot(
            powers.astype(jnp.bfloat16), value_head, preferred_element_type=jnp.float32
        )
        return (mixed_sum / row_sum).astype(jnp.bfloat16)

    result = lax.map(per_head, jnp.arange(heads_dev, dtype=jnp.int32))
    return jnp.transpose(result, (1, 0, 2)).reshape(frame_rows, columns)


def run_copies(pairs, sems):
    copies = [
        pltpu.make_async_copy(source, target, sems.at[at])
        for at, (source, target) in enumerate(pairs)
    ]
    for copy in copies:
        copy.start()
    for copy in copies:
        copy.wait()


def rows_of(block):
    return pl.ds(pl.multiple_of(block * BLOCK, BLOCK), BLOCK)


def stage_missing_kernel(bands, keys, values, missing, sems):
    frame = lax.axis_index("tm")

    @pl.when((frame == 1) | (frame == 2))
    def _():
        rows = rows_of(jnp.where(frame == 1, bands[3, 0, 1], bands[0, 1, 2]))
        run_copies([(keys.at[rows], missing.at[0]), (values.at[rows], missing.at[1])], sems)


def stage_near_kernel(half, after, keys, values, inner, beside, sems):
    frame = lax.axis_index("tm")
    outer = pl.ds(pl.multiple_of(lax.rem(frame + 1, 2) * half, half), half)
    facing = pl.ds(pl.multiple_of(lax.rem(frame, 2) * half, half), half)
    pairs = []
    for kv, source in enumerate((keys, values)):
        pairs.append((source.at[facing], inner.at[kv]))
        pairs.append((source.at[outer], beside.at[kv]))
    run_copies(pairs, sems)


def stage_crossed_kernel(after, bands, keys, values, crossed, sems):
    frame = lax.axis_index("tm")

    @pl.when((frame == 0) | (frame == 3))
    def _():
        reader = jnp.where(frame == 0, 2, 1)
        pairs = []
        for slot in range(2):
            rows = rows_of(bands[reader, slot, frame])
            for kv, source in enumerate((keys, values)):
                pairs.append((source.at[rows], crossed.at[kv, pl.ds(slot * BLOCK, BLOCK)]))
        run_copies(pairs, sems)


def stage_last_kernel(cuts, inner, bands, keys, values, picked, *rest):
    direct, sems = rest[:-1], rest[-1]
    frame = lax.axis_index("tm")
    edge = (frame == 0) | (frame == 3)

    @pl.when(edge)
    def _():
        pairs = []
        for slot in range(2):
            rows = rows_of(bands[3 - frame, slot, frame])
            for part, (first, size) in zip(direct, cuts):
                for kv, source in enumerate((keys, values)):
                    pairs.append(
                        (
                            source.at[rows, pl.ds(first, size)],
                            part.at[kv, pl.ds(slot * BLOCK, BLOCK)],
                        )
                    )
        run_copies(pairs, sems)

    @pl.when(jnp.logical_not(edge))
    def _():
        rows = rows_of(jnp.where(frame == 1, bands[0, 0, 2], bands[3, 1, 1] - 2))
        run_copies([(inner.at[:, rows], picked)], sems)


def attend_kernel(
    chunk, first, size, queries, keys, values, beside, inner, crossed, lone, picked, direct, *rest
):
    out, mixed_out, sems = rest[-3:]
    frame = lax.axis_index("tm")
    edge = (frame == 0) | (frame == 3)
    rate = LOG2E * HD ** (-0.5)
    rows = queries.shape[0]
    heads = range(size // HD)

    def pieces(head, own, kv):
        here, there = pl.ds(first + head * HD, HD), pl.ds(head * HD, HD)
        relayed = jnp.concatenate([lone[kv, :, here], picked[kv, :, here]], 0)
        return [
            own[:, here],
            beside[kv, :, here],
            jnp.where(edge, direct[kv, :, there], inner[kv, :, here]),
            jnp.where(edge, relayed, crossed[kv, :, here]),
        ]

    def score(head, start):
        rows_q = queries[pl.ds(start, chunk), pl.ds(first + head * HD, HD)]
        return [
            lax.dot_general(
                rows_q, piece, (((1,), (1,)), ((), ())), preferred_element_type=jnp.float32
            )
            for piece in pieces(head, keys, 0)
        ]

    def finish(head, start, scores):
        row_max = functools.reduce(
            jnp.maximum, [jnp.max(part, axis=1, keepdims=True) for part in scores]
        )
        powers = [jnp.exp2((part - row_max) * rate) for part in scores]
        row_sum = sum(jnp.sum(part, axis=1, keepdims=True) for part in powers)
        mixed = sum(
            jnp.dot(part.astype(jnp.bfloat16), piece, preferred_element_type=jnp.float32)
            for part, piece in zip(powers, pieces(head, values, 1))
        )
        mixed_out[head, pl.ds(start, chunk)] = (mixed / row_sum).astype(jnp.bfloat16)

    units = [(head, start) for head in heads for start in range(0, rows, chunk)]
    copies = []
    scores = score(*units[0])
    for unit, following in zip(units, units[1:] + [None]):
        ahead = score(*following) if following else None
        finish(*unit, scores)
        scores = ahead
        head, start = unit
        if start + chunk == rows:
            copies.append(
                pltpu.make_async_copy(
                    mixed_out.at[head], out.at[:, pl.ds(first + head * HD, HD)], sems.at[head]
                )
            )
            copies[-1].start()
    for copy in copies:
        copy.wait()


def four_frames(queries, keys, values, band_blocks):
    rows, columns = queries.shape
    half = rows // 2
    heads = columns // HD
    last = heads // 4
    cuts = [(0, heads - 2 * last), (heads - 2 * last, last), (heads - last, last)]
    cuts = [(first * HD, size * HD) for first, size in cuts if size]
    anywhere = pl.BlockSpec(memory_space=pl.ANY)
    local = pl.BlockSpec(memory_space=pltpu.VMEM)
    scalars = pl.BlockSpec(memory_space=pltpu.SMEM)
    roomy = pltpu.CompilerParams(vmem_limit_bytes=32 << 20)

    def send(array, pairs):
        return lax.ppermute(array, "tm", pairs)

    bands = jnp.transpose(band_blocks, (0, 2, 1))
    block = jax.ShapeDtypeStruct((2, BLOCK, columns), jnp.bfloat16)
    facing = jax.ShapeDtypeStruct((2, half, columns), jnp.bfloat16)
    parts = [jax.ShapeDtypeStruct((2, half, size), jnp.bfloat16) for _, size in cuts]

    def stage(kernel, shapes, copies, operands, name):
        return pl.pallas_call(
            kernel,
            out_shape=shapes,
            in_specs=[scalars if operand is bands else anywhere for operand in operands],
            out_specs=[local] * len(shapes),
            scratch_shapes=[pltpu.SemaphoreType.DMA((copies,))],
            compiler_params=pltpu.CompilerParams(vmem_limit_bytes=60 << 20),
            name=name,
        )(*operands)

    (missing,) = stage(
        stage_missing_kernel, [block], 2, [bands, keys, values], "stage_missing"
    )
    inner, beside = stage(
        functools.partial(stage_near_kernel, half),
        [facing, facing],
        4,
        [missing, keys, values],
        "stage_near",
    )
    missing = send(missing, [(1, 2), (2, 1)])
    beside = send(beside, [(0, 1), (1, 0), (2, 3), (3, 2)])
    inner = send(inner, [(1, 2), (2, 1)])
    lone = send(missing, [(2, 3), (1, 0)])
    (crossed,) = stage(
        stage_crossed_kernel, [facing], 4, [missing, bands, keys, values], "stage_crossed"
    )
    crossed = send(crossed, [(0, 2), (3, 1)])
    picked, *direct = stage(
        functools.partial(stage_last_kernel, cuts),
        [block] + parts,
        4 * len(cuts),
        [inner, bands, keys, values],
        "stage_last",
    )
    picked = send(picked, [(2, 3), (1, 0)])
    direct = [send(part, [(0, 3), (3, 0)]) for part in direct]

    result = None
    seen = rows + 3 * half
    for g, (first, size) in enumerate(cuts):
        operands = [queries, keys, values, beside, inner, crossed, lone, picked, direct[g]]
        in_specs = [local] * len(operands)
        aliases = {}
        if result is not None:
            aliases = {len(operands): 0}
            in_specs.append(anywhere)
            operands.append(result)
        result = pl.pallas_call(
            functools.partial(attend_kernel, rows // 2, first, size),
            out_shape=jax.ShapeDtypeStruct(queries.shape, queries.dtype),
            in_specs=in_specs,
            out_specs=anywhere,
            input_output_aliases=aliases,
            scratch_shapes=[
                pltpu.VMEM((size // HD, rows, HD), jnp.bfloat16),
                pltpu.SemaphoreType.DMA((size // HD,)),
            ],
            compiler_params=roomy,
            cost_estimate=pl.CostEstimate(
                flops=4 * size * rows * seen,
                bytes_accessed=2 * size * (2 * rows + 2 * (rows + 4 * half)),
                transcendentals=size // HD * rows * seen,
            ),
            name=f"attend_{g}",
        )(*operands)
    return result


def shards(queries, keys, values, band_blocks):
    if lax.axis_size("tm") == 4 and queries.shape[0] == 4 * BLOCK and band_blocks.shape[2] == 2:
        return four_frames(queries, keys, values, band_blocks)
    return any_frames(queries, keys, values, band_blocks)


def solution(mesh):
    placed = (
        P(("groups", "tm"), ("head", "sub")),
        P(("groups", "tm"), ("head", "sub")),
        P(("groups", "tm"), ("head", "sub")),
        P(),
    )
    return jax.shard_map(
        shards,
        mesh=mesh,
        in_specs=placed,
        out_specs=P(("groups", "tm"), ("head", "sub")),
        check_vma=False,
    )
```

```python
import functools

import jax
import jax.numpy as jnp
from jax import lax
from jax.experimental import pallas as pl
from jax.experimental.pallas import tpu as pltpu
from jax.sharding import PartitionSpec as P

HD = 128
BLOCK = 128
LOG2E = 1.4426950408889634

masked_fill = -1e30


def padded(block, sides, width):
    for axis, dim in sides:
        count = lax.axis_size(axis)
        forward = [(i, i + 1) for i in range(count - 1)]
        backward = [(target, source) for source, target in forward]
        low = lax.ppermute(
            lax.slice_in_dim(block, block.shape[dim] - width, None, axis=dim), axis, forward
        )
        high = lax.ppermute(lax.slice_in_dim(block, 0, width, axis=dim), axis, backward)
        block = jnp.concatenate([low, block, high], axis=dim)
    return block


def any_frames(queries, keys, values, band_blocks):
    frame_rows, columns = queries.shape
    frames = lax.axis_size("tm")
    current = lax.axis_index("tm")
    half_rows = frame_rows // 2
    frame_blocks = frame_rows // BLOCK
    capacity = band_blocks.shape[2]
    heads_dev = columns // HD
    paired = jnp.stack([keys, values], 0)
    near_kv = padded(paired, (("tm", 1),), half_rows)
    position = jnp.arange(2 * frame_rows)
    near_ok = ((position >= half_rows) | (current > 0)) & (
        (position < half_rows + frame_rows) | (current < frames - 1)
    )
    kv_blocks = jnp.concatenate(
        [
            paired.reshape(2, frame_blocks, BLOCK, columns),
            jnp.zeros((2, 1, BLOCK, columns), jnp.bfloat16),
        ],
        1,
    )
    outgoing = lax.dynamic_index_in_dim(band_blocks, current, 1, keepdims=False)
    incoming = lax.dynamic_index_in_dim(band_blocks, current, 0, keepdims=False)
    outbound = jnp.take(kv_blocks, outgoing, axis=1)
    arrived = lax.all_to_all(outbound, "tm", split_axis=1, concat_axis=1, tiled=True)
    far_kv = arrived.reshape(2, frames * capacity * BLOCK, columns)
    far_ok = jnp.repeat((incoming != frame_blocks).reshape(-1), BLOCK)
    all_kv = jnp.concatenate([near_kv, far_kv], 1)
    visible = jnp.concatenate([near_ok, far_ok], 0)
    inv_root = HD ** (-0.5)

    def per_head(head_at):
        start = head_at * HD
        query_head = lax.dynamic_slice_in_dim(queries, start, HD, 1)
        key_head = lax.dynamic_slice_in_dim(all_kv[0], start, HD, 1)
        value_head = lax.dynamic_slice_in_dim(all_kv[1], start, HD, 1)
        scores = (
            lax.dot_general(
                query_head, key_head, (((1,), (1,)), ((), ())), preferred_element_type=jnp.float32
            )
            * inv_root
        )
        scores = jnp.where(visible[None, :], scores, masked_fill)
        row_max = jnp.max(scores, axis=1, keepdims=True)
        powers = jnp.exp(scores - row_max)
        row_sum = jnp.sum(powers, axis=1, keepdims=True)
        mixed_sum = jnp.dot(
            powers.astype(jnp.bfloat16), value_head, preferred_element_type=jnp.float32
        )
        return (mixed_sum / row_sum).astype(jnp.bfloat16)

    result = lax.map(per_head, jnp.arange(heads_dev, dtype=jnp.int32))
    return jnp.transpose(result, (1, 0, 2)).reshape(frame_rows, columns)


def run_copies(pairs, sems):
    copies = [
        pltpu.make_async_copy(source, target, sems.at[at])
        for at, (source, target) in enumerate(pairs)
    ]
    for copy in copies:
        copy.start()
    for copy in copies:
        copy.wait()


def rows_of(block):
    return pl.ds(pl.multiple_of(block * BLOCK, BLOCK), BLOCK)


def stage_near_kernel(half, bands, keys, values, listed, beside, sems):
    frame = lax.axis_index("tm")
    rows = pl.ds(pl.multiple_of(lax.rem(frame + 1, 2) * half, half), half)
    near = [
        pltpu.make_async_copy(source.at[rows], beside.at[kv], sems.at[kv])
        for kv, source in enumerate((keys, values))
    ]

    @pl.when((frame == 1) | (frame == 2))
    def _():
        reader = jnp.where(frame == 1, 3, 0)
        pairs = []
        for place in range(2):
            slot = jnp.where(frame == 1, place, 1 - place)
            rows = rows_of(bands[reader, slot, frame])
            for kv, source in enumerate((keys, values)):
                pairs.append((source.at[rows], listed.at[kv, pl.ds(place * BLOCK, BLOCK)]))
        for copy in near:
            copy.start()
        run_copies(pairs, sems.at[pl.ds(2, 4)])

    @pl.when((frame == 0) | (frame == 3))
    def _():
        for copy in near:
            copy.start()

    for copy in near:
        copy.wait()


def stage_crossed_kernel(after, bands, keys, values, crossed, sems):
    frame = lax.axis_index("tm")

    @pl.when((frame == 0) | (frame == 3))
    def _():
        reader = jnp.where(frame == 0, 2, 1)
        pairs = []
        for slot in range(2):
            rows = rows_of(bands[reader, slot, frame])
            for kv, source in enumerate((keys, values)):
                pairs.append((source.at[rows], crossed.at[kv, pl.ds(slot * BLOCK, BLOCK)]))
        run_copies(pairs, sems)


def stage_last_kernel(after, bands, keys, values, direct, closing, sems):
    frame = lax.axis_index("tm")
    inner = (frame == 1) | (frame == 2)
    other = jnp.where(frame == 1, 5 - bands[3, 1, 1], 1 - bands[0, 0, 2])
    first = jnp.where(inner, other, bands[3 - frame, 0, frame])
    second = jnp.where(inner, other, bands[3 - frame, 1, frame])
    pairs = []
    for kv, source in enumerate((keys, values)):
        pairs.append((source.at[rows_of(first)], direct.at[kv]))
        pairs.append((source.at[rows_of(second)], closing.at[kv]))
    run_copies(pairs, sems)


RATE = LOG2E * HD ** (-0.5)


def scores_of(queries, keys):
    return lax.dot_general(
        queries, keys, (((1,), (1,)), ((), ())), preferred_element_type=jnp.float32
    )


def attend_kernel(
    chunk, queries, keys, values, beside, listed, crossed, relayed, direct, mixed, tops, sums
):
    frame = lax.axis_index("tm")
    edge = (frame == 0) | (frame == 3)
    rows, columns = queries.shape

    def pieces(head, own, kv):
        cols = pl.ds(head * HD, HD)
        return [
            own[:, cols],
            beside[kv, :, cols],
            jnp.where(edge, relayed[kv, :, cols], crossed[kv, :, cols]),
            jnp.where(edge, direct[kv, :, cols], listed[kv, pl.ds(BLOCK, BLOCK), cols]),
        ]

    def score(head, start):
        rows_q = queries[pl.ds(start, chunk), pl.ds(head * HD, HD)]
        return [scores_of(rows_q, piece) for piece in pieces(head, keys, 0)]

    def finish(head, start, scores):
        at = pl.ds(start, chunk)
        row_max = functools.reduce(
            jnp.maximum, [jnp.max(part, axis=1, keepdims=True) for part in scores]
        )
        powers = [jnp.exp2((part - row_max) * RATE) for part in scores]
        row_sum = sum(jnp.sum(part, axis=1, keepdims=True) for part in powers)
        mixed[head, at] = sum(
            jnp.dot(part.astype(jnp.bfloat16), piece, preferred_element_type=jnp.float32)
            for part, piece in zip(powers, pieces(head, values, 1))
        )
        tops[head, at] = jnp.broadcast_to(row_max, (chunk, HD))
        sums[head, at] = jnp.broadcast_to(row_sum, (chunk, HD))

    units = [(head, start) for head in range(columns // HD) for start in range(0, rows, chunk)]
    scores = score(*units[0])
    for unit, following in zip(units, units[1:] + [None]):
        ahead = score(*following) if following else None
        finish(*unit, scores)
        scores = ahead


def close_kernel(queries, closing, mixed, tops, sums, out, ready, sems):
    rows, columns = queries.shape
    copies = []
    for head in range(columns // HD):
        cols = pl.ds(head * HD, HD)
        scores = scores_of(queries[:, cols], closing[0, :, cols])
        top = jnp.maximum(tops[head], jnp.max(scores, axis=1, keepdims=True))
        shrink = jnp.exp2((tops[head] - top) * RATE)
        powers = jnp.exp2((scores - top) * RATE)
        total = sums[head] * shrink + jnp.sum(powers, axis=1, keepdims=True)
        more = jnp.dot(
            powers.astype(jnp.bfloat16), closing[1, :, cols], preferred_element_type=jnp.float32
        )
        ready[head] = ((mixed[head] * shrink + more) / total).astype(jnp.bfloat16)
        copies.append(pltpu.make_async_copy(ready.at[head], out.at[:, cols], sems.at[head]))
        copies[-1].start()
    for copy in copies:
        copy.wait()


def four_frames(queries, keys, values, band_blocks):
    rows, columns = queries.shape
    half = rows // 2
    heads = columns // HD
    anywhere = pl.BlockSpec(memory_space=pl.ANY)
    local = pl.BlockSpec(memory_space=pltpu.VMEM)
    scalars = pl.BlockSpec(memory_space=pltpu.SMEM)

    def send(array, pairs):
        return lax.ppermute(array, "tm", pairs)

    bands = jnp.transpose(band_blocks, (0, 2, 1))
    one = jax.ShapeDtypeStruct((2, BLOCK, columns), jnp.bfloat16)
    two = jax.ShapeDtypeStruct((2, 2 * BLOCK, columns), jnp.bfloat16)

    def stage(kernel, shapes, copies, operands, name, room):
        return pl.pallas_call(
            kernel,
            out_shape=shapes,
            in_specs=[scalars if operand is bands else anywhere for operand in operands],
            out_specs=[local] * len(shapes),
            scratch_shapes=[pltpu.SemaphoreType.DMA((copies,))],
            compiler_params=pltpu.CompilerParams(vmem_limit_bytes=room << 20),
            name=name,
        )(*operands)

    listed, beside = stage(
        functools.partial(stage_near_kernel, half),
        [two, two],
        6,
        [bands, keys, values],
        "stage_near",
        60,
    )
    (crossed,) = stage(
        stage_crossed_kernel, [two], 4, [beside, bands, keys, values], "stage_crossed", 32
    )
    beside = send(beside, [(0, 1), (1, 0), (2, 3), (3, 2)])
    listed = send(listed, [(1, 2), (2, 1)])
    crossed = send(crossed, [(0, 2), (3, 1)])
    relayed = send(listed, [(2, 3), (1, 0)])
    direct, closing = stage(
        stage_last_kernel, [one, one], 4, [beside, bands, keys, values], "stage_last", 32
    )
    direct = send(direct, [(0, 3), (3, 0)])
    closing = send(closing, [(1, 2), (2, 1), (0, 3), (3, 0)])

    state = jax.ShapeDtypeStruct((heads, rows, HD), jnp.float32)
    roomy = pltpu.CompilerParams(vmem_limit_bytes=32 << 20)
    mixed, tops, sums = pl.pallas_call(
        functools.partial(attend_kernel, rows // 2),
        out_shape=[state] * 3,
        in_specs=[local] * 8,
        out_specs=[local] * 3,
        compiler_params=roomy,
        name="attend",
    )(queries, keys, values, beside, listed, crossed, relayed, direct)
    return pl.pallas_call(
        close_kernel,
        out_shape=jax.ShapeDtypeStruct(queries.shape, queries.dtype),
        in_specs=[local] * 5,
        out_specs=anywhere,
        scratch_shapes=[
            pltpu.VMEM((heads, rows, HD), jnp.bfloat16),
            pltpu.SemaphoreType.DMA((heads,)),
        ],
        compiler_params=roomy,
        name="close",
    )(queries, closing, mixed, tops, sums)


def shards(queries, keys, values, band_blocks):
    if lax.axis_size("tm") == 4 and queries.shape[0] == 4 * BLOCK and band_blocks.shape[2] == 2:
        return four_frames(queries, keys, values, band_blocks)
    return any_frames(queries, keys, values, band_blocks)


def solution(mesh):
    placed = (
        P(("groups", "tm"), ("head", "sub")),
        P(("groups", "tm"), ("head", "sub")),
        P(("groups", "tm"), ("head", "sub")),
        P(),
    )
    return jax.shard_map(
        shards,
        mesh=mesh,
        in_specs=placed,
        out_specs=P(("groups", "tm"), ("head", "sub")),
        check_vma=False,
    )
```

```python
import functools

import jax
import jax.numpy as jnp
from jax import lax
from jax.experimental import pallas as pl
from jax.experimental.pallas import tpu as pltpu
from jax.sharding import PartitionSpec as P

HD = 128
BLOCK = 128
LOG2E = 1.4426950408889634

masked_fill = -1e30


def padded(block, sides, width):
    for axis, dim in sides:
        count = lax.axis_size(axis)
        forward = [(i, i + 1) for i in range(count - 1)]
        backward = [(target, source) for source, target in forward]
        low = lax.ppermute(
            lax.slice_in_dim(block, block.shape[dim] - width, None, axis=dim), axis, forward
        )
        high = lax.ppermute(lax.slice_in_dim(block, 0, width, axis=dim), axis, backward)
        block = jnp.concatenate([low, block, high], axis=dim)
    return block


def any_frames(queries, keys, values, band_blocks):
    frame_rows, columns = queries.shape
    frames = lax.axis_size("tm")
    current = lax.axis_index("tm")
    half_rows = frame_rows // 2
    frame_blocks = frame_rows // BLOCK
    capacity = band_blocks.shape[2]
    heads_dev = columns // HD
    paired = jnp.stack([keys, values], 0)
    near_kv = padded(paired, (("tm", 1),), half_rows)
    position = jnp.arange(2 * frame_rows)
    near_ok = ((position >= half_rows) | (current > 0)) & (
        (position < half_rows + frame_rows) | (current < frames - 1)
    )
    kv_blocks = jnp.concatenate(
        [
            paired.reshape(2, frame_blocks, BLOCK, columns),
            jnp.zeros((2, 1, BLOCK, columns), jnp.bfloat16),
        ],
        1,
    )
    outgoing = lax.dynamic_index_in_dim(band_blocks, current, 1, keepdims=False)
    incoming = lax.dynamic_index_in_dim(band_blocks, current, 0, keepdims=False)
    outbound = jnp.take(kv_blocks, outgoing, axis=1)
    arrived = lax.all_to_all(outbound, "tm", split_axis=1, concat_axis=1, tiled=True)
    far_kv = arrived.reshape(2, frames * capacity * BLOCK, columns)
    far_ok = jnp.repeat((incoming != frame_blocks).reshape(-1), BLOCK)
    all_kv = jnp.concatenate([near_kv, far_kv], 1)
    visible = jnp.concatenate([near_ok, far_ok], 0)
    inv_root = HD ** (-0.5)

    def per_head(head_at):
        start = head_at * HD
        query_head = lax.dynamic_slice_in_dim(queries, start, HD, 1)
        key_head = lax.dynamic_slice_in_dim(all_kv[0], start, HD, 1)
        value_head = lax.dynamic_slice_in_dim(all_kv[1], start, HD, 1)
        scores = (
            lax.dot_general(
                query_head, key_head, (((1,), (1,)), ((), ())), preferred_element_type=jnp.float32
            )
            * inv_root
        )
        scores = jnp.where(visible[None, :], scores, masked_fill)
        row_max = jnp.max(scores, axis=1, keepdims=True)
        powers = jnp.exp(scores - row_max)
        row_sum = jnp.sum(powers, axis=1, keepdims=True)
        mixed_sum = jnp.dot(
            powers.astype(jnp.bfloat16), value_head, preferred_element_type=jnp.float32
        )
        return (mixed_sum / row_sum).astype(jnp.bfloat16)

    result = lax.map(per_head, jnp.arange(heads_dev, dtype=jnp.int32))
    return jnp.transpose(result, (1, 0, 2)).reshape(frame_rows, columns)


def run_copies(pairs, sems):
    copies = [
        pltpu.make_async_copy(source, target, sems.at[at])
        for at, (source, target) in enumerate(pairs)
    ]
    for copy in copies:
        copy.start()
    for copy in copies:
        copy.wait()


def rows_of(block):
    return pl.ds(pl.multiple_of(block * BLOCK, BLOCK), BLOCK)


def stage_listed_kernel(bands, keys, values, listed, token, sems):
    frame = lax.axis_index("tm")
    token[...] = jnp.zeros_like(token)

    @pl.when((frame == 1) | (frame == 2))
    def _():
        reader = jnp.where(frame == 1, 3, 0)
        pairs = []
        for place in range(2):
            slot = jnp.where(frame == 1, place, 1 - place)
            rows = rows_of(bands[reader, slot, frame])
            for kv, source in enumerate((keys, values)):
                pairs.append((source.at[rows], listed.at[kv, pl.ds(place * BLOCK, BLOCK)]))
        run_copies(pairs, sems)


def stage_beside_kernel(half, after, keys, values, beside, token, sems):
    frame = lax.axis_index("tm")
    token[...] = jnp.zeros_like(token)
    rows = pl.ds(pl.multiple_of(lax.rem(frame + 1, 2) * half, half), half)
    run_copies([(keys.at[rows], beside.at[0]), (values.at[rows], beside.at[1])], sems)


def stage_crossed_kernel(after, bands, keys, values, crossed, sems):
    frame = lax.axis_index("tm")

    @pl.when((frame == 0) | (frame == 3))
    def _():
        reader = jnp.where(frame == 0, 2, 1)
        pairs = []
        for slot in range(2):
            rows = rows_of(bands[reader, slot, frame])
            for kv, source in enumerate((keys, values)):
                pairs.append((source.at[rows], crossed.at[kv, pl.ds(slot * BLOCK, BLOCK)]))
        run_copies(pairs, sems)


def stage_direct_kernel(after, bands, keys, values, direct, sems):
    frame = lax.axis_index("tm")

    @pl.when((frame == 0) | (frame == 3))
    def _():
        rows = rows_of(bands[3 - frame, 0, frame])
        run_copies([(keys.at[rows], direct.at[0]), (values.at[rows], direct.at[1])], sems)


def stage_closing_kernel(after, bands, keys, values, closing, sems):
    frame = lax.axis_index("tm")
    inner = (frame == 1) | (frame == 2)
    other = jnp.where(frame == 1, 5 - bands[3, 1, 1], 1 - bands[0, 0, 2])
    rows = rows_of(jnp.where(inner, other, bands[3 - frame, 1, frame]))
    run_copies([(keys.at[rows], closing.at[0]), (values.at[rows], closing.at[1])], sems)


RATE = LOG2E * HD ** (-0.5)


def scores_of(queries, keys):
    return lax.dot_general(
        queries, keys, (((1,), (1,)), ((), ())), preferred_element_type=jnp.float32
    )


def attend_kernel(
    chunk, queries, keys, values, beside, listed, crossed, relayed, direct, mixed, tops, sums
):
    frame = lax.axis_index("tm")
    edge = (frame == 0) | (frame == 3)
    rows, columns = queries.shape

    def pieces(head, own, kv):
        cols = pl.ds(head * HD, HD)
        return [
            own[:, cols],
            beside[kv, :, cols],
            jnp.where(edge, relayed[kv, :, cols], crossed[kv, :, cols]),
            jnp.where(edge, direct[kv, :, cols], listed[kv, pl.ds(BLOCK, BLOCK), cols]),
        ]

    def score(head, start):
        rows_q = queries[pl.ds(start, chunk), pl.ds(head * HD, HD)]
        return [scores_of(rows_q, piece) for piece in pieces(head, keys, 0)]

    def finish(head, start, scores):
        at = pl.ds(start, chunk)
        row_max = functools.reduce(
            jnp.maximum, [jnp.max(part, axis=1, keepdims=True) for part in scores]
        )
        powers = [jnp.exp2((part - row_max) * RATE) for part in scores]
        row_sum = sum(jnp.sum(part, axis=1, keepdims=True) for part in powers)
        mixed[head, at] = sum(
            jnp.dot(part.astype(jnp.bfloat16), piece, preferred_element_type=jnp.float32)
            for part, piece in zip(powers, pieces(head, values, 1))
        )
        tops[head, at] = jnp.broadcast_to(row_max, (chunk, HD))
        sums[head, at] = jnp.broadcast_to(row_sum, (chunk, HD))

    units = [(head, start) for head in range(columns // HD) for start in range(0, rows, chunk)]
    scores = score(*units[0])
    for unit, following in zip(units, units[1:] + [None]):
        ahead = score(*following) if following else None
        finish(*unit, scores)
        scores = ahead


def close_kernel(queries, closing, mixed, tops, sums, out, ready, sems):
    rows, columns = queries.shape
    copies = []
    for head in range(columns // HD):
        cols = pl.ds(head * HD, HD)
        scores = scores_of(queries[:, cols], closing[0, :, cols])
        top = jnp.maximum(tops[head], jnp.max(scores, axis=1, keepdims=True))
        shrink = jnp.exp2((tops[head] - top) * RATE)
        powers = jnp.exp2((scores - top) * RATE)
        total = sums[head] * shrink + jnp.sum(powers, axis=1, keepdims=True)
        more = jnp.dot(
            powers.astype(jnp.bfloat16), closing[1, :, cols], preferred_element_type=jnp.float32
        )
        ready[head] = ((mixed[head] * shrink + more) / total).astype(jnp.bfloat16)
        copies.append(pltpu.make_async_copy(ready.at[head], out.at[:, cols], sems.at[head]))
        copies[-1].start()
    for copy in copies:
        copy.wait()


def four_frames(queries, keys, values, band_blocks):
    rows, columns = queries.shape
    half = rows // 2
    heads = columns // HD
    anywhere = pl.BlockSpec(memory_space=pl.ANY)
    local = pl.BlockSpec(memory_space=pltpu.VMEM)
    scalars = pl.BlockSpec(memory_space=pltpu.SMEM)

    def send(array, pairs):
        return lax.ppermute(array, "tm", pairs)

    bands = jnp.transpose(band_blocks, (0, 2, 1))
    one = jax.ShapeDtypeStruct((2, BLOCK, columns), jnp.bfloat16)
    two = jax.ShapeDtypeStruct((2, 2 * BLOCK, columns), jnp.bfloat16)

    def stage(kernel, shapes, copies, operands, name, room):
        return pl.pallas_call(
            kernel,
            out_shape=shapes,
            in_specs=[scalars if operand is bands else anywhere for operand in operands],
            out_specs=[local] * len(shapes),
            scratch_shapes=[pltpu.SemaphoreType.DMA((copies,))],
            compiler_params=pltpu.CompilerParams(vmem_limit_bytes=room << 20),
            name=name,
        )(*operands)

    token = jax.ShapeDtypeStruct((8, HD), jnp.int32)
    listed, after = stage(
        stage_listed_kernel, [two, token], 4, [bands, keys, values], "stage_listed", 52
    )
    beside, after = stage(
        functools.partial(stage_beside_kernel, half),
        [two, token],
        2,
        [after, keys, values],
        "stage_beside",
        52,
    )
    (crossed,) = stage(
        stage_crossed_kernel, [two], 4, [after, bands, keys, values], "stage_crossed", 32
    )
    beside = send(beside, [(0, 1), (1, 0), (2, 3), (3, 2)])
    listed = send(listed, [(1, 2), (2, 1)])
    crossed = send(crossed, [(0, 2), (3, 1)])
    relayed = send(listed, [(2, 3), (1, 0)])
    (direct,) = stage(
        stage_direct_kernel, [one], 2, [beside, bands, keys, values], "stage_direct", 32
    )
    direct = send(direct, [(0, 3), (3, 0)])
    (closing,) = stage(
        stage_closing_kernel, [one], 2, [crossed, bands, keys, values], "stage_closing", 32
    )
    closing = send(closing, [(1, 2), (2, 1), (0, 3), (3, 0)])

    state = jax.ShapeDtypeStruct((heads, rows, HD), jnp.float32)
    roomy = pltpu.CompilerParams(vmem_limit_bytes=32 << 20)
    mixed, tops, sums = pl.pallas_call(
        functools.partial(attend_kernel, rows // 2),
        out_shape=[state] * 3,
        in_specs=[local] * 8,
        out_specs=[local] * 3,
        compiler_params=roomy,
        name="attend",
    )(queries, keys, values, beside, listed, crossed, relayed, direct)
    return pl.pallas_call(
        close_kernel,
        out_shape=jax.ShapeDtypeStruct(queries.shape, queries.dtype),
        in_specs=[local] * 5,
        out_specs=anywhere,
        scratch_shapes=[
            pltpu.VMEM((heads, rows, HD), jnp.bfloat16),
            pltpu.SemaphoreType.DMA((heads,)),
        ],
        compiler_params=roomy,
        name="close",
    )(queries, closing, mixed, tops, sums)


def shards(queries, keys, values, band_blocks):
    if lax.axis_size("tm") == 4 and queries.shape[0] == 4 * BLOCK and band_blocks.shape[2] == 2:
        return four_frames(queries, keys, values, band_blocks)
    return any_frames(queries, keys, values, band_blocks)


def solution(mesh):
    placed = (
        P(("groups", "tm"), ("head", "sub")),
        P(("groups", "tm"), ("head", "sub")),
        P(("groups", "tm"), ("head", "sub")),
        P(),
    )
    return jax.shard_map(
        shards,
        mesh=mesh,
        in_specs=placed,
        out_specs=P(("groups", "tm"), ("head", "sub")),
        check_vma=False,
    )
```

```python
import functools

import jax
import jax.numpy as jnp
from jax import lax
from jax.experimental import pallas as pl
from jax.experimental.pallas import tpu as pltpu
from jax.sharding import PartitionSpec as P

HD = 128
BLOCK = 128
LOG2E = 1.4426950408889634

masked_fill = -1e30


def padded(block, sides, width):
    for axis, dim in sides:
        count = lax.axis_size(axis)
        forward = [(i, i + 1) for i in range(count - 1)]
        backward = [(target, source) for source, target in forward]
        low = lax.ppermute(
            lax.slice_in_dim(block, block.shape[dim] - width, None, axis=dim), axis, forward
        )
        high = lax.ppermute(lax.slice_in_dim(block, 0, width, axis=dim), axis, backward)
        block = jnp.concatenate([low, block, high], axis=dim)
    return block


def any_frames(queries, keys, values, band_blocks):
    frame_rows, columns = queries.shape
    frames = lax.axis_size("tm")
    current = lax.axis_index("tm")
    half_rows = frame_rows // 2
    frame_blocks = frame_rows // BLOCK
    capacity = band_blocks.shape[2]
    heads_dev = columns // HD
    paired = jnp.stack([keys, values], 0)
    near_kv = padded(paired, (("tm", 1),), half_rows)
    position = jnp.arange(2 * frame_rows)
    near_ok = ((position >= half_rows) | (current > 0)) & (
        (position < half_rows + frame_rows) | (current < frames - 1)
    )
    kv_blocks = jnp.concatenate(
        [
            paired.reshape(2, frame_blocks, BLOCK, columns),
            jnp.zeros((2, 1, BLOCK, columns), jnp.bfloat16),
        ],
        1,
    )
    outgoing = lax.dynamic_index_in_dim(band_blocks, current, 1, keepdims=False)
    incoming = lax.dynamic_index_in_dim(band_blocks, current, 0, keepdims=False)
    outbound = jnp.take(kv_blocks, outgoing, axis=1)
    arrived = lax.all_to_all(outbound, "tm", split_axis=1, concat_axis=1, tiled=True)
    far_kv = arrived.reshape(2, frames * capacity * BLOCK, columns)
    far_ok = jnp.repeat((incoming != frame_blocks).reshape(-1), BLOCK)
    all_kv = jnp.concatenate([near_kv, far_kv], 1)
    visible = jnp.concatenate([near_ok, far_ok], 0)
    inv_root = HD ** (-0.5)

    def per_head(head_at):
        start = head_at * HD
        query_head = lax.dynamic_slice_in_dim(queries, start, HD, 1)
        key_head = lax.dynamic_slice_in_dim(all_kv[0], start, HD, 1)
        value_head = lax.dynamic_slice_in_dim(all_kv[1], start, HD, 1)
        scores = (
            lax.dot_general(
                query_head, key_head, (((1,), (1,)), ((), ())), preferred_element_type=jnp.float32
            )
            * inv_root
        )
        scores = jnp.where(visible[None, :], scores, masked_fill)
        row_max = jnp.max(scores, axis=1, keepdims=True)
        powers = jnp.exp(scores - row_max)
        row_sum = jnp.sum(powers, axis=1, keepdims=True)
        mixed_sum = jnp.dot(
            powers.astype(jnp.bfloat16), value_head, preferred_element_type=jnp.float32
        )
        return (mixed_sum / row_sum).astype(jnp.bfloat16)

    result = lax.map(per_head, jnp.arange(heads_dev, dtype=jnp.int32))
    return jnp.transpose(result, (1, 0, 2)).reshape(frame_rows, columns)


def run_copies(pairs, sems):
    copies = [
        pltpu.make_async_copy(source, target, sems.at[at])
        for at, (source, target) in enumerate(pairs)
    ]
    for copy in copies:
        copy.start()
    for copy in copies:
        copy.wait()


def rows_of(block):
    return pl.ds(pl.multiple_of(block * BLOCK, BLOCK), BLOCK)


def stage_first_kernel(bands, keys, values, first, token, sems):
    frame = lax.axis_index("tm")
    token[...] = jnp.zeros_like(token)
    inner = (frame == 1) | (frame == 2)
    reader = jnp.where(frame == 1, 3, 0)
    pairs = []
    for place in range(2):
        slot = jnp.where(frame == 1, place, 1 - place)
        facing = jnp.where(frame == 0, 2 + place, place)
        rows = rows_of(jnp.where(inner, bands[reader, slot, frame], facing))
        for kv, source in enumerate((keys, values)):
            pairs.append((source.at[rows], first.at[kv, pl.ds(place * BLOCK, BLOCK)]))
    run_copies(pairs, sems)


def stage_second_kernel(after, bands, keys, values, second, sems):
    frame = lax.axis_index("tm")
    inner = (frame == 1) | (frame == 2)
    reader = jnp.where(frame == 0, 2, 1)
    pairs = []
    for place in range(2):
        facing = jnp.where(frame == 1, place, 2 + place)
        rows = rows_of(jnp.where(inner, facing, bands[reader, place, frame]))
        for kv, source in enumerate((keys, values)):
            pairs.append((source.at[rows], second.at[kv, pl.ds(place * BLOCK, BLOCK)]))
    run_copies(pairs, sems)


def stage_direct_kernel(after, bands, keys, values, direct, sems):
    frame = lax.axis_index("tm")

    @pl.when((frame == 0) | (frame == 3))
    def _():
        rows = rows_of(bands[3 - frame, 0, frame])
        run_copies([(keys.at[rows], direct.at[0]), (values.at[rows], direct.at[1])], sems)


def stage_closing_kernel(cuts, after, bands, keys, values, *rest):
    closing, sems = rest[:-1], rest[-1]
    frame = lax.axis_index("tm")
    inner = (frame == 1) | (frame == 2)
    other = jnp.where(frame == 1, 5 - bands[3, 1, 1], 1 - bands[0, 0, 2])
    rows = rows_of(jnp.where(inner, other, bands[3 - frame, 1, frame]))
    run_copies(
        [
            (source.at[rows, pl.ds(first, size)], part.at[kv])
            for part, (first, size) in zip(closing, cuts)
            for kv, source in enumerate((keys, values))
        ],
        sems,
    )


RATE = LOG2E * HD ** (-0.5)


def scores_of(queries, keys):
    return lax.dot_general(
        queries, keys, (((1,), (1,)), ((), ())), preferred_element_type=jnp.float32
    )


def attend_kernel(
    chunk, queries, keys, values, inward, listed, around, relayed, direct, mixed, tops, sums
):
    frame = lax.axis_index("tm")
    edge = (frame == 0) | (frame == 3)
    rows, columns = queries.shape

    def pieces(head, own, kv):
        cols = pl.ds(head * HD, HD)
        return [
            own[:, cols],
            around[kv, :, cols],
            jnp.where(edge, relayed[kv, :, cols], inward[kv, :, cols]),
            jnp.where(edge, direct[kv, :, cols], listed[kv, pl.ds(BLOCK, BLOCK), cols]),
        ]

    def score(head, start):
        rows_q = queries[pl.ds(start, chunk), pl.ds(head * HD, HD)]
        return [scores_of(rows_q, piece) for piece in pieces(head, keys, 0)]

    def finish(head, start, scores):
        at = pl.ds(start, chunk)
        row_max = functools.reduce(
            jnp.maximum, [jnp.max(part, axis=1, keepdims=True) for part in scores]
        )
        powers = [jnp.exp2((part - row_max) * RATE) for part in scores]
        row_sum = sum(jnp.sum(part, axis=1, keepdims=True) for part in powers)
        mixed[head, at] = sum(
            jnp.dot(part.astype(jnp.bfloat16), piece, preferred_element_type=jnp.float32)
            for part, piece in zip(powers, pieces(head, values, 1))
        )
        tops[head, at] = jnp.broadcast_to(row_max, (chunk, HD))
        sums[head, at] = jnp.broadcast_to(row_sum, (chunk, HD))

    units = [(head, start) for head in range(columns // HD) for start in range(0, rows, chunk)]
    scores = score(*units[0])
    for unit, following in zip(units, units[1:] + [None]):
        ahead = score(*following) if following else None
        finish(*unit, scores)
        scores = ahead


def close_kernel(first, queries, closing, mixed, tops, sums, *rest):
    out, ready, sems = rest[-3:]
    copies = []
    for at in range(ready.shape[0]):
        head = first // HD + at
        here, there = pl.ds(first + at * HD, HD), pl.ds(at * HD, HD)
        scores = scores_of(queries[:, here], closing[0, :, there])
        top = jnp.maximum(tops[head], jnp.max(scores, axis=1, keepdims=True))
        shrink = jnp.exp2((tops[head] - top) * RATE)
        powers = jnp.exp2((scores - top) * RATE)
        total = sums[head] * shrink + jnp.sum(powers, axis=1, keepdims=True)
        more = jnp.dot(
            powers.astype(jnp.bfloat16), closing[1, :, there], preferred_element_type=jnp.float32
        )
        ready[at] = ((mixed[head] * shrink + more) / total).astype(jnp.bfloat16)
        copies.append(pltpu.make_async_copy(ready.at[at], out.at[:, here], sems.at[at]))
        copies[-1].start()
    for copy in copies:
        copy.wait()


def four_frames(queries, keys, values, band_blocks):
    rows, columns = queries.shape
    half = rows // 2
    heads = columns // HD
    anywhere = pl.BlockSpec(memory_space=pl.ANY)
    local = pl.BlockSpec(memory_space=pltpu.VMEM)
    scalars = pl.BlockSpec(memory_space=pltpu.SMEM)

    def send(array, pairs):
        return lax.ppermute(array, "tm", pairs)

    bands = jnp.transpose(band_blocks, (0, 2, 1))
    one = jax.ShapeDtypeStruct((2, BLOCK, columns), jnp.bfloat16)
    two = jax.ShapeDtypeStruct((2, 2 * BLOCK, columns), jnp.bfloat16)

    def stage(kernel, shapes, copies, operands, name, room):
        return pl.pallas_call(
            kernel,
            out_shape=shapes,
            in_specs=[scalars if operand is bands else anywhere for operand in operands],
            out_specs=[local] * len(shapes),
            scratch_shapes=[pltpu.SemaphoreType.DMA((copies,))],
            compiler_params=pltpu.CompilerParams(vmem_limit_bytes=room << 20),
            name=name,
        )(*operands)

    token = jax.ShapeDtypeStruct((8, HD), jnp.int32)
    first, after = stage(
        stage_first_kernel, [two, token], 4, [bands, keys, values], "stage_first", 52
    )
    (second,) = stage(
        stage_second_kernel, [two], 4, [after, bands, keys, values], "stage_second", 32
    )
    listed = send(first, [(1, 2), (2, 1)])
    inward = send(first, [(0, 1), (3, 2)])
    around = send(second, [(1, 0), (2, 3), (0, 2), (3, 1)])
    relayed = send(listed, [(2, 3), (1, 0)])
    (direct,) = stage(
        stage_direct_kernel, [one], 2, [inward, bands, keys, values], "stage_direct", 32
    )
    direct = send(direct, [(0, 3), (3, 0)])
    last = heads // 4
    cuts = [(0, heads - last), (heads - last, last)] if last else [(0, heads)]
    cuts = [(start * HD, size * HD) for start, size in cuts]
    closing = stage(
        functools.partial(stage_closing_kernel, cuts),
        [jax.ShapeDtypeStruct((2, BLOCK, size), jnp.bfloat16) for _, size in cuts],
        2 * len(cuts),
        [around, bands, keys, values],
        "stage_closing",
        32,
    )
    closing = [send(part, [(1, 2), (2, 1), (0, 3), (3, 0)]) for part in closing]

    state = jax.ShapeDtypeStruct((heads, rows, HD), jnp.float32)
    roomy = pltpu.CompilerParams(vmem_limit_bytes=32 << 20)
    mixed, tops, sums = pl.pallas_call(
        functools.partial(attend_kernel, rows // 2),
        out_shape=[state] * 3,
        in_specs=[local] * 8,
        out_specs=[local] * 3,
        compiler_params=roomy,
        name="attend",
    )(queries, keys, values, inward, listed, around, relayed, direct)
    result = None
    for part, (start, size) in zip(closing, cuts):
        operands = [queries, part, mixed, tops, sums]
        in_specs = [local] * len(operands)
        aliases = {}
        if result is not None:
            aliases = {len(operands): 0}
            in_specs.append(anywhere)
            operands.append(result)
        result = pl.pallas_call(
            functools.partial(close_kernel, start),
            out_shape=jax.ShapeDtypeStruct(queries.shape, queries.dtype),
            in_specs=in_specs,
            out_specs=anywhere,
            input_output_aliases=aliases,
            scratch_shapes=[
                pltpu.VMEM((size // HD, rows, HD), jnp.bfloat16),
                pltpu.SemaphoreType.DMA((size // HD,)),
            ],
            compiler_params=roomy,
            name="close",
        )(*operands)
    return result


def shards(queries, keys, values, band_blocks):
    if lax.axis_size("tm") == 4 and queries.shape[0] == 4 * BLOCK and band_blocks.shape[2] == 2:
        return four_frames(queries, keys, values, band_blocks)
    return any_frames(queries, keys, values, band_blocks)


def solution(mesh):
    placed = (
        P(("groups", "tm"), ("head", "sub")),
        P(("groups", "tm"), ("head", "sub")),
        P(("groups", "tm"), ("head", "sub")),
        P(),
    )
    return jax.shard_map(
        shards,
        mesh=mesh,
        in_specs=placed,
        out_specs=P(("groups", "tm"), ("head", "sub")),
        check_vma=False,
    )
```

```python
import functools

import jax
import jax.numpy as jnp
from jax import lax
from jax.experimental import pallas as pl
from jax.experimental.pallas import tpu as pltpu
from jax.sharding import PartitionSpec as P

HD = 128
BLOCK = 128
LOG2E = 1.4426950408889634

masked_fill = -1e30


def padded(block, sides, width):
    for axis, dim in sides:
        count = lax.axis_size(axis)
        forward = [(i, i + 1) for i in range(count - 1)]
        backward = [(target, source) for source, target in forward]
        low = lax.ppermute(
            lax.slice_in_dim(block, block.shape[dim] - width, None, axis=dim), axis, forward
        )
        high = lax.ppermute(lax.slice_in_dim(block, 0, width, axis=dim), axis, backward)
        block = jnp.concatenate([low, block, high], axis=dim)
    return block


def any_frames(queries, keys, values, band_blocks):
    frame_rows, columns = queries.shape
    frames = lax.axis_size("tm")
    current = lax.axis_index("tm")
    half_rows = frame_rows // 2
    frame_blocks = frame_rows // BLOCK
    capacity = band_blocks.shape[2]
    heads_dev = columns // HD
    paired = jnp.stack([keys, values], 0)
    near_kv = padded(paired, (("tm", 1),), half_rows)
    position = jnp.arange(2 * frame_rows)
    near_ok = ((position >= half_rows) | (current > 0)) & (
        (position < half_rows + frame_rows) | (current < frames - 1)
    )
    kv_blocks = jnp.concatenate(
        [
            paired.reshape(2, frame_blocks, BLOCK, columns),
            jnp.zeros((2, 1, BLOCK, columns), jnp.bfloat16),
        ],
        1,
    )
    outgoing = lax.dynamic_index_in_dim(band_blocks, current, 1, keepdims=False)
    incoming = lax.dynamic_index_in_dim(band_blocks, current, 0, keepdims=False)
    outbound = jnp.take(kv_blocks, outgoing, axis=1)
    arrived = lax.all_to_all(outbound, "tm", split_axis=1, concat_axis=1, tiled=True)
    far_kv = arrived.reshape(2, frames * capacity * BLOCK, columns)
    far_ok = jnp.repeat((incoming != frame_blocks).reshape(-1), BLOCK)
    all_kv = jnp.concatenate([near_kv, far_kv], 1)
    visible = jnp.concatenate([near_ok, far_ok], 0)
    inv_root = HD ** (-0.5)

    def per_head(head_at):
        start = head_at * HD
        query_head = lax.dynamic_slice_in_dim(queries, start, HD, 1)
        key_head = lax.dynamic_slice_in_dim(all_kv[0], start, HD, 1)
        value_head = lax.dynamic_slice_in_dim(all_kv[1], start, HD, 1)
        scores = (
            lax.dot_general(
                query_head, key_head, (((1,), (1,)), ((), ())), preferred_element_type=jnp.float32
            )
            * inv_root
        )
        scores = jnp.where(visible[None, :], scores, masked_fill)
        row_max = jnp.max(scores, axis=1, keepdims=True)
        powers = jnp.exp(scores - row_max)
        row_sum = jnp.sum(powers, axis=1, keepdims=True)
        mixed_sum = jnp.dot(
            powers.astype(jnp.bfloat16), value_head, preferred_element_type=jnp.float32
        )
        return (mixed_sum / row_sum).astype(jnp.bfloat16)

    result = lax.map(per_head, jnp.arange(heads_dev, dtype=jnp.int32))
    return jnp.transpose(result, (1, 0, 2)).reshape(frame_rows, columns)


def run_copies(pairs, sems):
    copies = [
        pltpu.make_async_copy(source, target, sems.at[at])
        for at, (source, target) in enumerate(pairs)
    ]
    for copy in copies:
        copy.start()
    for copy in copies:
        copy.wait()


def rows_of(block):
    return pl.ds(pl.multiple_of(block * BLOCK, BLOCK), BLOCK)


def stage_first_kernel(bands, keys, values, first, sems):
    frame = lax.axis_index("tm")
    inner = (frame == 1) | (frame == 2)
    reader = jnp.where(frame == 1, 3, 0)
    pairs = []
    for place in range(2):
        slot = jnp.where(frame == 1, place, 1 - place)
        facing = jnp.where(frame == 0, 2 + place, place)
        rows = rows_of(jnp.where(inner, bands[reader, slot, frame], facing))
        for kv, source in enumerate((keys, values)):
            pairs.append((source.at[rows], first.at[kv, pl.ds(place * BLOCK, BLOCK)]))
    run_copies(pairs, sems)


def stage_outward_kernel(half, keys, values, outward, sems):
    frame = lax.axis_index("tm")

    @pl.when((frame == 1) | (frame == 2))
    def _():
        rows = pl.ds(pl.multiple_of((frame - 1) * half, half), half)
        run_copies([(keys.at[rows], outward.at[0]), (values.at[rows], outward.at[1])], sems)


def stage_crossed_kernel(after, bands, keys, values, crossed, sems):
    frame = lax.axis_index("tm")

    @pl.when((frame == 0) | (frame == 3))
    def _():
        reader = jnp.where(frame == 0, 2, 1)
        pairs = []
        for slot in range(2):
            rows = rows_of(bands[reader, slot, frame])
            for kv, source in enumerate((keys, values)):
                pairs.append((source.at[rows], crossed.at[kv, pl.ds(slot * BLOCK, BLOCK)]))
        run_copies(pairs, sems)


def stage_direct_kernel(after, bands, keys, values, direct, sems):
    frame = lax.axis_index("tm")

    @pl.when((frame == 0) | (frame == 3))
    def _():
        rows = rows_of(bands[3 - frame, 0, frame])
        run_copies([(keys.at[rows], direct.at[0]), (values.at[rows], direct.at[1])], sems)


def stage_closing_kernel(cuts, after, after_too, bands, keys, values, *rest):
    closing, sems = rest[:-1], rest[-1]
    frame = lax.axis_index("tm")
    inner = (frame == 1) | (frame == 2)
    other = jnp.where(frame == 1, 5 - bands[3, 1, 1], 1 - bands[0, 0, 2])
    rows = rows_of(jnp.where(inner, other, bands[3 - frame, 1, frame]))
    run_copies(
        [
            (source.at[rows, pl.ds(first, size)], part.at[kv])
            for part, (first, size) in zip(closing, cuts)
            for kv, source in enumerate((keys, values))
        ],
        sems,
    )


RATE = LOG2E * HD ** (-0.5)


def scores_of(queries, keys):
    return lax.dot_general(
        queries, keys, (((1,), (1,)), ((), ())), preferred_element_type=jnp.float32
    )


def attend_kernel(
    chunk, queries, keys, values, inward, outward, listed, crossed, relayed, direct,
    mixed, tops, sums
):
    frame = lax.axis_index("tm")
    edge = (frame == 0) | (frame == 3)
    rows, columns = queries.shape

    def pieces(head, own, kv):
        cols = pl.ds(head * HD, HD)
        return [
            own[:, cols],
            jnp.where(edge, outward[kv, :, cols], inward[kv, :, cols]),
            jnp.where(edge, relayed[kv, :, cols], crossed[kv, :, cols]),
            jnp.where(edge, direct[kv, :, cols], listed[kv, pl.ds(BLOCK, BLOCK), cols]),
        ]

    def score(head, start):
        rows_q = queries[pl.ds(start, chunk), pl.ds(head * HD, HD)]
        return [scores_of(rows_q, piece) for piece in pieces(head, keys, 0)]

    def finish(head, start, scores):
        at = pl.ds(start, chunk)
        row_max = functools.reduce(
            jnp.maximum, [jnp.max(part, axis=1, keepdims=True) for part in scores]
        )
        powers = [jnp.exp2((part - row_max) * RATE) for part in scores]
        row_sum = sum(jnp.sum(part, axis=1, keepdims=True) for part in powers)
        mixed[head, at] = sum(
            jnp.dot(part.astype(jnp.bfloat16), piece, preferred_element_type=jnp.float32)
            for part, piece in zip(powers, pieces(head, values, 1))
        )
        tops[head, at] = jnp.broadcast_to(row_max, (chunk, HD))
        sums[head, at] = jnp.broadcast_to(row_sum, (chunk, HD))

    units = [(head, start) for head in range(columns // HD) for start in range(0, rows, chunk)]
    scores = score(*units[0])
    for unit, following in zip(units, units[1:] + [None]):
        ahead = score(*following) if following else None
        finish(*unit, scores)
        scores = ahead


def close_kernel(first, queries, closing, mixed, tops, sums, *rest):
    out, ready, sems = rest[-3:]
    copies = []
    for at in range(ready.shape[0]):
        head = first // HD + at
        here, there = pl.ds(first + at * HD, HD), pl.ds(at * HD, HD)
        scores = scores_of(queries[:, here], closing[0, :, there])
        top = jnp.maximum(tops[head], jnp.max(scores, axis=1, keepdims=True))
        shrink = jnp.exp2((tops[head] - top) * RATE)
        powers = jnp.exp2((scores - top) * RATE)
        total = sums[head] * shrink + jnp.sum(powers, axis=1, keepdims=True)
        more = jnp.dot(
            powers.astype(jnp.bfloat16), closing[1, :, there], preferred_element_type=jnp.float32
        )
        ready[at] = ((mixed[head] * shrink + more) / total).astype(jnp.bfloat16)
        copies.append(pltpu.make_async_copy(ready.at[at], out.at[:, here], sems.at[at]))
        copies[-1].start()
    for copy in copies:
        copy.wait()


def four_frames(queries, keys, values, band_blocks):
    rows, columns = queries.shape
    half = rows // 2
    heads = columns // HD
    anywhere = pl.BlockSpec(memory_space=pl.ANY)
    local = pl.BlockSpec(memory_space=pltpu.VMEM)
    scalars = pl.BlockSpec(memory_space=pltpu.SMEM)

    def send(array, pairs):
        return lax.ppermute(array, "tm", pairs)

    bands = jnp.transpose(band_blocks, (0, 2, 1))
    one = jax.ShapeDtypeStruct((2, BLOCK, columns), jnp.bfloat16)
    two = jax.ShapeDtypeStruct((2, 2 * BLOCK, columns), jnp.bfloat16)

    def stage(kernel, shapes, copies, operands, name, room):
        return pl.pallas_call(
            kernel,
            out_shape=shapes,
            in_specs=[scalars if operand is bands else anywhere for operand in operands],
            out_specs=[local] * len(shapes),
            scratch_shapes=[pltpu.SemaphoreType.DMA((copies,))],
            compiler_params=pltpu.CompilerParams(vmem_limit_bytes=room << 20),
            name=name,
        )(*operands)

    (first,) = stage(
        stage_first_kernel, [two], 4, [bands, keys, values], "stage_first", 52
    )
    inward = send(first, [(0, 1), (3, 2)])
    listed = send(first, [(1, 2), (2, 1)])
    (outward,) = stage(
        functools.partial(stage_outward_kernel, half),
        [two],
        2,
        [keys, values],
        "stage_outward",
        32,
    )
    outward = send(outward, [(1, 0), (2, 3)])
    (crossed,) = stage(
        stage_crossed_kernel, [two], 4, [inward, bands, keys, values], "stage_crossed", 32
    )
    crossed = send(crossed, [(0, 2), (3, 1)])
    relayed = send(listed, [(2, 3), (1, 0)])
    (direct,) = stage(
        stage_direct_kernel, [one], 2, [outward, bands, keys, values], "stage_direct", 32
    )
    direct = send(direct, [(0, 3), (3, 0)])
    last = heads // 4
    cuts = [(0, heads - last), (heads - last, last)] if last else [(0, heads)]
    cuts = [(start * HD, size * HD) for start, size in cuts]
    closing = stage(
        functools.partial(stage_closing_kernel, cuts),
        [jax.ShapeDtypeStruct((2, BLOCK, size), jnp.bfloat16) for _, size in cuts],
        2 * len(cuts),
        [crossed, relayed, bands, keys, values],
        "stage_closing",
        32,
    )
    closing = [send(part, [(1, 2), (2, 1), (0, 3), (3, 0)]) for part in closing]

    state = jax.ShapeDtypeStruct((heads, rows, HD), jnp.float32)
    roomy = pltpu.CompilerParams(vmem_limit_bytes=32 << 20)
    mixed, tops, sums = pl.pallas_call(
        functools.partial(attend_kernel, rows // 2),
        out_shape=[state] * 3,
        in_specs=[local] * 9,
        out_specs=[local] * 3,
        compiler_params=roomy,
        name="attend",
    )(queries, keys, values, inward, outward, listed, crossed, relayed, direct)
    result = None
    for part, (start, size) in zip(closing, cuts):
        operands = [queries, part, mixed, tops, sums]
        in_specs = [local] * len(operands)
        aliases = {}
        if result is not None:
            aliases = {len(operands): 0}
            in_specs.append(anywhere)
            operands.append(result)
        result = pl.pallas_call(
            functools.partial(close_kernel, start),
            out_shape=jax.ShapeDtypeStruct(queries.shape, queries.dtype),
            in_specs=in_specs,
            out_specs=anywhere,
            input_output_aliases=aliases,
            scratch_shapes=[
                pltpu.VMEM((size // HD, rows, HD), jnp.bfloat16),
                pltpu.SemaphoreType.DMA((size // HD,)),
            ],
            compiler_params=roomy,
            name="close",
        )(*operands)
    return result


def shards(queries, keys, values, band_blocks):
    if lax.axis_size("tm") == 4 and queries.shape[0] == 4 * BLOCK and band_blocks.shape[2] == 2:
        return four_frames(queries, keys, values, band_blocks)
    return any_frames(queries, keys, values, band_blocks)


def solution(mesh):
    placed = (
        P(("groups", "tm"), ("head", "sub")),
        P(("groups", "tm"), ("head", "sub")),
        P(("groups", "tm"), ("head", "sub")),
        P(),
    )
    return jax.shard_map(
        shards,
        mesh=mesh,
        in_specs=placed,
        out_specs=P(("groups", "tm"), ("head", "sub")),
        check_vma=False,
    )
```

```python
import functools

import jax
import jax.numpy as jnp
from jax import lax
from jax.experimental import pallas as pl
from jax.experimental.pallas import tpu as pltpu
from jax.sharding import PartitionSpec as P

HD = 128
BLOCK = 128
LOG2E = 1.4426950408889634

masked_fill = -1e30


def padded(block, sides, width):
    for axis, dim in sides:
        count = lax.axis_size(axis)
        forward = [(i, i + 1) for i in range(count - 1)]
        backward = [(target, source) for source, target in forward]
        low = lax.ppermute(
            lax.slice_in_dim(block, block.shape[dim] - width, None, axis=dim), axis, forward
        )
        high = lax.ppermute(lax.slice_in_dim(block, 0, width, axis=dim), axis, backward)
        block = jnp.concatenate([low, block, high], axis=dim)
    return block


def any_frames(queries, keys, values, band_blocks):
    frame_rows, columns = queries.shape
    frames = lax.axis_size("tm")
    current = lax.axis_index("tm")
    half_rows = frame_rows // 2
    frame_blocks = frame_rows // BLOCK
    capacity = band_blocks.shape[2]
    heads_dev = columns // HD
    paired = jnp.stack([keys, values], 0)
    near_kv = padded(paired, (("tm", 1),), half_rows)
    position = jnp.arange(2 * frame_rows)
    near_ok = ((position >= half_rows) | (current > 0)) & (
        (position < half_rows + frame_rows) | (current < frames - 1)
    )
    kv_blocks = jnp.concatenate(
        [
            paired.reshape(2, frame_blocks, BLOCK, columns),
            jnp.zeros((2, 1, BLOCK, columns), jnp.bfloat16),
        ],
        1,
    )
    outgoing = lax.dynamic_index_in_dim(band_blocks, current, 1, keepdims=False)
    incoming = lax.dynamic_index_in_dim(band_blocks, current, 0, keepdims=False)
    outbound = jnp.take(kv_blocks, outgoing, axis=1)
    arrived = lax.all_to_all(outbound, "tm", split_axis=1, concat_axis=1, tiled=True)
    far_kv = arrived.reshape(2, frames * capacity * BLOCK, columns)
    far_ok = jnp.repeat((incoming != frame_blocks).reshape(-1), BLOCK)
    all_kv = jnp.concatenate([near_kv, far_kv], 1)
    visible = jnp.concatenate([near_ok, far_ok], 0)
    inv_root = HD ** (-0.5)

    def per_head(head_at):
        start = head_at * HD
        query_head = lax.dynamic_slice_in_dim(queries, start, HD, 1)
        key_head = lax.dynamic_slice_in_dim(all_kv[0], start, HD, 1)
        value_head = lax.dynamic_slice_in_dim(all_kv[1], start, HD, 1)
        scores = (
            lax.dot_general(
                query_head, key_head, (((1,), (1,)), ((), ())), preferred_element_type=jnp.float32
            )
            * inv_root
        )
        scores = jnp.where(visible[None, :], scores, masked_fill)
        row_max = jnp.max(scores, axis=1, keepdims=True)
        powers = jnp.exp(scores - row_max)
        row_sum = jnp.sum(powers, axis=1, keepdims=True)
        mixed_sum = jnp.dot(
            powers.astype(jnp.bfloat16), value_head, preferred_element_type=jnp.float32
        )
        return (mixed_sum / row_sum).astype(jnp.bfloat16)

    result = lax.map(per_head, jnp.arange(heads_dev, dtype=jnp.int32))
    return jnp.transpose(result, (1, 0, 2)).reshape(frame_rows, columns)


def run_copies(pairs, sems):
    copies = [
        pltpu.make_async_copy(source, target, sems.at[at])
        for at, (source, target) in enumerate(pairs)
    ]
    for copy in copies:
        copy.start()
    for copy in copies:
        copy.wait()


def rows_of(block):
    return pl.ds(pl.multiple_of(block * BLOCK, BLOCK), BLOCK)


def stage_listed_kernel(bands, keys, values, listed, token, sems):
    frame = lax.axis_index("tm")
    token[...] = jnp.zeros_like(token)

    @pl.when((frame == 1) | (frame == 2))
    def _():
        reader = jnp.where(frame == 1, 3, 0)
        pairs = []
        for place in range(2):
            slot = jnp.where(frame == 1, place, 1 - place)
            rows = rows_of(bands[reader, slot, frame])
            for kv, source in enumerate((keys, values)):
                pairs.append((source.at[rows], listed.at[kv, pl.ds(place * BLOCK, BLOCK)]))
        run_copies(pairs, sems)


def stage_beside_kernel(half, after, keys, values, beside, token, sems):
    frame = lax.axis_index("tm")
    token[...] = jnp.zeros_like(token)
    rows = pl.ds(pl.multiple_of(lax.rem(frame + 1, 2) * half, half), half)
    run_copies([(keys.at[rows], beside.at[0]), (values.at[rows], beside.at[1])], sems)


def stage_crossed_kernel(after, bands, keys, values, crossed, sems):
    frame = lax.axis_index("tm")

    @pl.when((frame == 0) | (frame == 3))
    def _():
        reader = jnp.where(frame == 0, 2, 1)
        pairs = []
        for slot in range(2):
            rows = rows_of(bands[reader, slot, frame])
            for kv, source in enumerate((keys, values)):
                pairs.append((source.at[rows], crossed.at[kv, pl.ds(slot * BLOCK, BLOCK)]))
        run_copies(pairs, sems)


def stage_direct_kernel(after, bands, keys, values, direct, sems):
    frame = lax.axis_index("tm")

    @pl.when((frame == 0) | (frame == 3))
    def _():
        rows = rows_of(bands[3 - frame, 0, frame])
        run_copies([(keys.at[rows], direct.at[0]), (values.at[rows], direct.at[1])], sems)


def stage_closing_kernel(cuts, after, bands, keys, values, *rest):
    closing, sems = rest[:-1], rest[-1]
    frame = lax.axis_index("tm")
    inner = (frame == 1) | (frame == 2)
    other = jnp.where(frame == 1, 5 - bands[3, 1, 1], 1 - bands[0, 0, 2])
    rows = rows_of(jnp.where(inner, other, bands[3 - frame, 1, frame]))
    run_copies(
        [
            (source.at[rows, pl.ds(first, size)], part.at[kv])
            for part, (first, size) in zip(closing, cuts)
            for kv, source in enumerate((keys, values))
        ],
        sems,
    )


RATE = LOG2E * HD ** (-0.5)


def scores_of(queries, keys):
    return lax.dot_general(
        queries, keys, (((1,), (1,)), ((), ())), preferred_element_type=jnp.float32
    )


def attend_kernel(
    chunk, queries, keys, values, beside, listed, crossed, relayed, direct, mixed, tops, sums
):
    frame = lax.axis_index("tm")
    edge = (frame == 0) | (frame == 3)
    rows, columns = queries.shape

    def pieces(head, own, kv):
        cols = pl.ds(head * HD, HD)
        return [
            own[:, cols],
            beside[kv, :, cols],
            jnp.where(edge, relayed[kv, :, cols], crossed[kv, :, cols]),
            jnp.where(edge, direct[kv, :, cols], listed[kv, pl.ds(BLOCK, BLOCK), cols]),
        ]

    def score(head, start):
        rows_q = queries[pl.ds(start, chunk), pl.ds(head * HD, HD)]
        return [scores_of(rows_q, piece) for piece in pieces(head, keys, 0)]

    def finish(head, start, scores):
        at = pl.ds(start, chunk)
        row_max = functools.reduce(
            jnp.maximum, [jnp.max(part, axis=1, keepdims=True) for part in scores]
        )
        powers = [jnp.exp2((part - row_max) * RATE) for part in scores]
        row_sum = sum(jnp.sum(part, axis=1, keepdims=True) for part in powers)
        mixed[head, at] = sum(
            jnp.dot(part.astype(jnp.bfloat16), piece, preferred_element_type=jnp.float32)
            for part, piece in zip(powers, pieces(head, values, 1))
        )
        tops[head, at] = jnp.broadcast_to(row_max, (chunk, HD))
        sums[head, at] = jnp.broadcast_to(row_sum, (chunk, HD))

    units = [(head, start) for head in range(columns // HD) for start in range(0, rows, chunk)]
    scores = score(*units[0])
    for unit, following in zip(units, units[1:] + [None]):
        ahead = score(*following) if following else None
        finish(*unit, scores)
        scores = ahead


def close_kernel(first, queries, closing, mixed, tops, sums, *rest):
    out, ready, sems = rest[-3:]
    copies = []
    for at in range(ready.shape[0]):
        head = first // HD + at
        here, there = pl.ds(first + at * HD, HD), pl.ds(at * HD, HD)
        scores = scores_of(queries[:, here], closing[0, :, there])
        top = jnp.maximum(tops[head], jnp.max(scores, axis=1, keepdims=True))
        shrink = jnp.exp2((tops[head] - top) * RATE)
        powers = jnp.exp2((scores - top) * RATE)
        total = sums[head] * shrink + jnp.sum(powers, axis=1, keepdims=True)
        more = jnp.dot(
            powers.astype(jnp.bfloat16), closing[1, :, there], preferred_element_type=jnp.float32
        )
        ready[at] = ((mixed[head] * shrink + more) / total).astype(jnp.bfloat16)
        copies.append(pltpu.make_async_copy(ready.at[at], out.at[:, here], sems.at[at]))
        copies[-1].start()
    for copy in copies:
        copy.wait()


def four_frames(queries, keys, values, band_blocks):
    rows, columns = queries.shape
    half = rows // 2
    heads = columns // HD
    anywhere = pl.BlockSpec(memory_space=pl.ANY)
    local = pl.BlockSpec(memory_space=pltpu.VMEM)
    scalars = pl.BlockSpec(memory_space=pltpu.SMEM)

    def send(array, pairs):
        return lax.ppermute(array, "tm", pairs)

    bands = jnp.transpose(band_blocks, (0, 2, 1))
    one = jax.ShapeDtypeStruct((2, BLOCK, columns), jnp.bfloat16)
    two = jax.ShapeDtypeStruct((2, 2 * BLOCK, columns), jnp.bfloat16)

    def stage(kernel, shapes, copies, operands, name, room):
        return pl.pallas_call(
            kernel,
            out_shape=shapes,
            in_specs=[scalars if operand is bands else anywhere for operand in operands],
            out_specs=[local] * len(shapes),
            scratch_shapes=[pltpu.SemaphoreType.DMA((copies,))],
            compiler_params=pltpu.CompilerParams(vmem_limit_bytes=room << 20),
            name=name,
        )(*operands)

    token = jax.ShapeDtypeStruct((8, HD), jnp.int32)
    listed, after = stage(
        stage_listed_kernel, [two, token], 4, [bands, keys, values], "stage_listed", 52
    )
    beside, after = stage(
        functools.partial(stage_beside_kernel, half),
        [two, token],
        2,
        [after, keys, values],
        "stage_beside",
        52,
    )
    (crossed,) = stage(
        stage_crossed_kernel, [two], 4, [after, bands, keys, values], "stage_crossed", 32
    )
    beside = send(beside, [(0, 1), (1, 0), (2, 3), (3, 2)])
    listed = send(listed, [(1, 2), (2, 1)])
    crossed = send(crossed, [(0, 2), (3, 1)])
    relayed = send(listed, [(2, 3), (1, 0)])
    (direct,) = stage(
        stage_direct_kernel, [one], 2, [beside, bands, keys, values], "stage_direct", 32
    )
    direct = send(direct, [(0, 3), (3, 0)])
    last = heads // 4
    cuts = [(0, heads - last), (heads - last, last)] if last else [(0, heads)]
    cuts = [(start * HD, size * HD) for start, size in cuts]
    closing = stage(
        functools.partial(stage_closing_kernel, cuts),
        [jax.ShapeDtypeStruct((2, BLOCK, size), jnp.bfloat16) for _, size in cuts],
        2 * len(cuts),
        [crossed, bands, keys, values],
        "stage_closing",
        32,
    )
    closing = [send(part, [(1, 2), (2, 1), (0, 3), (3, 0)]) for part in closing]

    state = jax.ShapeDtypeStruct((heads, rows, HD), jnp.float32)
    roomy = pltpu.CompilerParams(vmem_limit_bytes=32 << 20)
    mixed, tops, sums = pl.pallas_call(
        functools.partial(attend_kernel, rows // 2),
        out_shape=[state] * 3,
        in_specs=[local] * 8,
        out_specs=[local] * 3,
        compiler_params=roomy,
        name="attend",
    )(queries, keys, values, beside, listed, crossed, relayed, direct)
    result = None
    for part, (start, size) in zip(closing, cuts):
        operands = [queries, part, mixed, tops, sums]
        in_specs = [local] * len(operands)
        aliases = {}
        if result is not None:
            aliases = {len(operands): 0}
            in_specs.append(anywhere)
            operands.append(result)
        result = pl.pallas_call(
            functools.partial(close_kernel, start),
            out_shape=jax.ShapeDtypeStruct(queries.shape, queries.dtype),
            in_specs=in_specs,
            out_specs=anywhere,
            input_output_aliases=aliases,
            scratch_shapes=[
                pltpu.VMEM((size // HD, rows, HD), jnp.bfloat16),
                pltpu.SemaphoreType.DMA((size // HD,)),
            ],
            compiler_params=roomy,
            name="close",
        )(*operands)
    return result


def shards(queries, keys, values, band_blocks):
    if lax.axis_size("tm") == 4 and queries.shape[0] == 4 * BLOCK and band_blocks.shape[2] == 2:
        return four_frames(queries, keys, values, band_blocks)
    return any_frames(queries, keys, values, band_blocks)


def solution(mesh):
    placed = (
        P(("groups", "tm"), ("head", "sub")),
        P(("groups", "tm"), ("head", "sub")),
        P(("groups", "tm"), ("head", "sub")),
        P(),
    )
    return jax.shard_map(
        shards,
        mesh=mesh,
        in_specs=placed,
        out_specs=P(("groups", "tm"), ("head", "sub")),
        check_vma=False,
    )
```

```python
import functools

import jax
import jax.numpy as jnp
from jax import lax
from jax.experimental import pallas as pl
from jax.experimental.pallas import tpu as pltpu
from jax.sharding import PartitionSpec as P

HD = 128
BLOCK = 128
LOG2E = 1.4426950408889634

masked_fill = -1e30


def padded(block, sides, width):
    for axis, dim in sides:
        count = lax.axis_size(axis)
        forward = [(i, i + 1) for i in range(count - 1)]
        backward = [(target, source) for source, target in forward]
        low = lax.ppermute(
            lax.slice_in_dim(block, block.shape[dim] - width, None, axis=dim), axis, forward
        )
        high = lax.ppermute(lax.slice_in_dim(block, 0, width, axis=dim), axis, backward)
        block = jnp.concatenate([low, block, high], axis=dim)
    return block


def any_frames(queries, keys, values, band_blocks):
    frame_rows, columns = queries.shape
    frames = lax.axis_size("tm")
    current = lax.axis_index("tm")
    half_rows = frame_rows // 2
    frame_blocks = frame_rows // BLOCK
    capacity = band_blocks.shape[2]
    heads_dev = columns // HD
    paired = jnp.stack([keys, values], 0)
    near_kv = padded(paired, (("tm", 1),), half_rows)
    position = jnp.arange(2 * frame_rows)
    near_ok = ((position >= half_rows) | (current > 0)) & (
        (position < half_rows + frame_rows) | (current < frames - 1)
    )
    kv_blocks = jnp.concatenate(
        [
            paired.reshape(2, frame_blocks, BLOCK, columns),
            jnp.zeros((2, 1, BLOCK, columns), jnp.bfloat16),
        ],
        1,
    )
    outgoing = lax.dynamic_index_in_dim(band_blocks, current, 1, keepdims=False)
    incoming = lax.dynamic_index_in_dim(band_blocks, current, 0, keepdims=False)
    outbound = jnp.take(kv_blocks, outgoing, axis=1)
    arrived = lax.all_to_all(outbound, "tm", split_axis=1, concat_axis=1, tiled=True)
    far_kv = arrived.reshape(2, frames * capacity * BLOCK, columns)
    far_ok = jnp.repeat((incoming != frame_blocks).reshape(-1), BLOCK)
    all_kv = jnp.concatenate([near_kv, far_kv], 1)
    visible = jnp.concatenate([near_ok, far_ok], 0)
    inv_root = HD ** (-0.5)

    def per_head(head_at):
        start = head_at * HD
        query_head = lax.dynamic_slice_in_dim(queries, start, HD, 1)
        key_head = lax.dynamic_slice_in_dim(all_kv[0], start, HD, 1)
        value_head = lax.dynamic_slice_in_dim(all_kv[1], start, HD, 1)
        scores = (
            lax.dot_general(
                query_head, key_head, (((1,), (1,)), ((), ())), preferred_element_type=jnp.float32
            )
            * inv_root
        )
        scores = jnp.where(visible[None, :], scores, masked_fill)
        row_max = jnp.max(scores, axis=1, keepdims=True)
        powers = jnp.exp(scores - row_max)
        row_sum = jnp.sum(powers, axis=1, keepdims=True)
        mixed_sum = jnp.dot(
            powers.astype(jnp.bfloat16), value_head, preferred_element_type=jnp.float32
        )
        return (mixed_sum / row_sum).astype(jnp.bfloat16)

    result = lax.map(per_head, jnp.arange(heads_dev, dtype=jnp.int32))
    return jnp.transpose(result, (1, 0, 2)).reshape(frame_rows, columns)


def run_copies(pairs, sems):
    copies = [
        pltpu.make_async_copy(source, target, sems.at[at])
        for at, (source, target) in enumerate(pairs)
    ]
    for copy in copies:
        copy.start()
    for copy in copies:
        copy.wait()


def rows_of(block):
    return pl.ds(pl.multiple_of(block * BLOCK, BLOCK), BLOCK)


def stage_near_kernel(half, bands, keys, values, listed, beside, token, sems):
    frame = lax.axis_index("tm")
    rows = pl.ds(pl.multiple_of(lax.rem(frame + 1, 2) * half, half), half)
    near = [
        pltpu.make_async_copy(source.at[rows], beside.at[kv], sems.at[kv])
        for kv, source in enumerate((keys, values))
    ]

    @pl.when((frame == 1) | (frame == 2))
    def _():
        reader = jnp.where(frame == 1, 3, 0)
        pairs = []
        for place in range(2):
            slot = jnp.where(frame == 1, place, 1 - place)
            rows = rows_of(bands[reader, slot, frame])
            for kv, source in enumerate((keys, values)):
                pairs.append((source.at[rows], listed.at[kv, pl.ds(place * BLOCK, BLOCK)]))
        for copy in near:
            copy.start()
        run_copies(pairs, sems.at[pl.ds(2, 4)])

    @pl.when((frame == 0) | (frame == 3))
    def _():
        for copy in near:
            copy.start()

    token[...] = jnp.zeros_like(token)
    for copy in near:
        copy.wait()


def stage_crossed_kernel(after, bands, keys, values, crossed, sems):
    frame = lax.axis_index("tm")

    @pl.when((frame == 0) | (frame == 3))
    def _():
        reader = jnp.where(frame == 0, 2, 1)
        pairs = []
        for slot in range(2):
            rows = rows_of(bands[reader, slot, frame])
            for kv, source in enumerate((keys, values)):
                pairs.append((source.at[rows], crossed.at[kv, pl.ds(slot * BLOCK, BLOCK)]))
        run_copies(pairs, sems)


def stage_direct_kernel(after, bands, keys, values, direct, sems):
    frame = lax.axis_index("tm")

    @pl.when((frame == 0) | (frame == 3))
    def _():
        rows = rows_of(bands[3 - frame, 0, frame])
        run_copies([(keys.at[rows], direct.at[0]), (values.at[rows], direct.at[1])], sems)


def stage_closing_kernel(cuts, after, bands, keys, values, *rest):
    closing, sems = rest[:-1], rest[-1]
    frame = lax.axis_index("tm")
    inner = (frame == 1) | (frame == 2)
    other = jnp.where(frame == 1, 5 - bands[3, 1, 1], 1 - bands[0, 0, 2])
    rows = rows_of(jnp.where(inner, other, bands[3 - frame, 1, frame]))
    run_copies(
        [
            (source.at[rows, pl.ds(first, size)], part.at[kv])
            for part, (first, size) in zip(closing, cuts)
            for kv, source in enumerate((keys, values))
        ],
        sems,
    )


RATE = LOG2E * HD ** (-0.5)


def scores_of(queries, keys):
    return lax.dot_general(
        queries, keys, (((1,), (1,)), ((), ())), preferred_element_type=jnp.float32
    )


def attend_kernel(
    chunk, queries, keys, values, beside, listed, crossed, relayed, direct, mixed, tops, sums
):
    frame = lax.axis_index("tm")
    edge = (frame == 0) | (frame == 3)
    rows, columns = queries.shape

    def pieces(head, own, kv):
        cols = pl.ds(head * HD, HD)
        return [
            own[:, cols],
            beside[kv, :, cols],
            jnp.where(edge, relayed[kv, :, cols], crossed[kv, :, cols]),
            jnp.where(edge, direct[kv, :, cols], listed[kv, pl.ds(BLOCK, BLOCK), cols]),
        ]

    def score(head, start):
        rows_q = queries[pl.ds(start, chunk), pl.ds(head * HD, HD)]
        return [scores_of(rows_q, piece) for piece in pieces(head, keys, 0)]

    def finish(head, start, scores):
        at = pl.ds(start, chunk)
        row_max = functools.reduce(
            jnp.maximum, [jnp.max(part, axis=1, keepdims=True) for part in scores]
        )
        powers = [jnp.exp2((part - row_max) * RATE) for part in scores]
        row_sum = sum(jnp.sum(part, axis=1, keepdims=True) for part in powers)
        mixed[head, at] = sum(
            jnp.dot(part.astype(jnp.bfloat16), piece, preferred_element_type=jnp.float32)
            for part, piece in zip(powers, pieces(head, values, 1))
        )
        tops[head, at] = jnp.broadcast_to(row_max, (chunk, HD))
        sums[head, at] = jnp.broadcast_to(row_sum, (chunk, HD))

    units = [(head, start) for head in range(columns // HD) for start in range(0, rows, chunk)]
    scores = score(*units[0])
    for unit, following in zip(units, units[1:] + [None]):
        ahead = score(*following) if following else None
        finish(*unit, scores)
        scores = ahead


def close_kernel(first, queries, closing, mixed, tops, sums, *rest):
    out, ready, sems = rest[-3:]
    copies = []
    for at in range(ready.shape[0]):
        head = first // HD + at
        here, there = pl.ds(first + at * HD, HD), pl.ds(at * HD, HD)
        scores = scores_of(queries[:, here], closing[0, :, there])
        top = jnp.maximum(tops[head], jnp.max(scores, axis=1, keepdims=True))
        shrink = jnp.exp2((tops[head] - top) * RATE)
        powers = jnp.exp2((scores - top) * RATE)
        total = sums[head] * shrink + jnp.sum(powers, axis=1, keepdims=True)
        more = jnp.dot(
            powers.astype(jnp.bfloat16), closing[1, :, there], preferred_element_type=jnp.float32
        )
        ready[at] = ((mixed[head] * shrink + more) / total).astype(jnp.bfloat16)
        copies.append(pltpu.make_async_copy(ready.at[at], out.at[:, here], sems.at[at]))
        copies[-1].start()
    for copy in copies:
        copy.wait()


def four_frames(queries, keys, values, band_blocks):
    rows, columns = queries.shape
    half = rows // 2
    heads = columns // HD
    anywhere = pl.BlockSpec(memory_space=pl.ANY)
    local = pl.BlockSpec(memory_space=pltpu.VMEM)
    scalars = pl.BlockSpec(memory_space=pltpu.SMEM)

    def send(array, pairs):
        return lax.ppermute(array, "tm", pairs)

    bands = jnp.transpose(band_blocks, (0, 2, 1))
    one = jax.ShapeDtypeStruct((2, BLOCK, columns), jnp.bfloat16)
    two = jax.ShapeDtypeStruct((2, 2 * BLOCK, columns), jnp.bfloat16)

    def stage(kernel, shapes, copies, operands, name, room):
        return pl.pallas_call(
            kernel,
            out_shape=shapes,
            in_specs=[scalars if operand is bands else anywhere for operand in operands],
            out_specs=[local] * len(shapes),
            scratch_shapes=[pltpu.SemaphoreType.DMA((copies,))],
            compiler_params=pltpu.CompilerParams(vmem_limit_bytes=room << 20),
            name=name,
        )(*operands)

    token = jax.ShapeDtypeStruct((8, HD), jnp.int32)
    listed, beside, after = stage(
        functools.partial(stage_near_kernel, half),
        [two, two, token],
        6,
        [bands, keys, values],
        "stage_near",
        51,
    )
    (crossed,) = stage(
        stage_crossed_kernel, [two], 4, [after, bands, keys, values], "stage_crossed", 32
    )
    beside = send(beside, [(0, 1), (1, 0), (2, 3), (3, 2)])
    listed = send(listed, [(1, 2), (2, 1)])
    crossed = send(crossed, [(0, 2), (3, 1)])
    relayed = send(listed, [(2, 3), (1, 0)])
    (direct,) = stage(
        stage_direct_kernel, [one], 2, [beside, bands, keys, values], "stage_direct", 32
    )
    direct = send(direct, [(0, 3), (3, 0)])
    last = heads // 4
    cuts = [(0, heads - last), (heads - last, last)] if last else [(0, heads)]
    cuts = [(start * HD, size * HD) for start, size in cuts]
    closing = stage(
        functools.partial(stage_closing_kernel, cuts),
        [jax.ShapeDtypeStruct((2, BLOCK, size), jnp.bfloat16) for _, size in cuts],
        2 * len(cuts),
        [crossed, bands, keys, values],
        "stage_closing",
        32,
    )
    closing = [send(part, [(1, 2), (2, 1), (0, 3), (3, 0)]) for part in closing]

    state = jax.ShapeDtypeStruct((heads, rows, HD), jnp.float32)
    roomy = pltpu.CompilerParams(vmem_limit_bytes=32 << 20)
    mixed, tops, sums = pl.pallas_call(
        functools.partial(attend_kernel, rows // 2),
        out_shape=[state] * 3,
        in_specs=[local] * 8,
        out_specs=[local] * 3,
        compiler_params=roomy,
        name="attend",
    )(queries, keys, values, beside, listed, crossed, relayed, direct)
    result = None
    for part, (start, size) in zip(closing, cuts):
        operands = [queries, part, mixed, tops, sums]
        in_specs = [local] * len(operands)
        aliases = {}
        if result is not None:
            aliases = {len(operands): 0}
            in_specs.append(anywhere)
            operands.append(result)
        result = pl.pallas_call(
            functools.partial(close_kernel, start),
            out_shape=jax.ShapeDtypeStruct(queries.shape, queries.dtype),
            in_specs=in_specs,
            out_specs=anywhere,
            input_output_aliases=aliases,
            scratch_shapes=[
                pltpu.VMEM((size // HD, rows, HD), jnp.bfloat16),
                pltpu.SemaphoreType.DMA((size // HD,)),
            ],
            compiler_params=roomy,
            name="close",
        )(*operands)
    return result


def shards(queries, keys, values, band_blocks):
    if lax.axis_size("tm") == 4 and queries.shape[0] == 4 * BLOCK and band_blocks.shape[2] == 2:
        return four_frames(queries, keys, values, band_blocks)
    return any_frames(queries, keys, values, band_blocks)


def solution(mesh):
    placed = (
        P(("groups", "tm"), ("head", "sub")),
        P(("groups", "tm"), ("head", "sub")),
        P(("groups", "tm"), ("head", "sub")),
        P(),
    )
    return jax.shard_map(
        shards,
        mesh=mesh,
        in_specs=placed,
        out_specs=P(("groups", "tm"), ("head", "sub")),
        check_vma=False,
    )
```

```python
import functools

import jax
import jax.numpy as jnp
from jax import lax
from jax.experimental import pallas as pl
from jax.experimental.pallas import tpu as pltpu
from jax.sharding import PartitionSpec as P

HD = 128
BLOCK = 128
LOG2E = 1.4426950408889634

masked_fill = -1e30


def padded(block, sides, width):
    for axis, dim in sides:
        count = lax.axis_size(axis)
        forward = [(i, i + 1) for i in range(count - 1)]
        backward = [(target, source) for source, target in forward]
        low = lax.ppermute(
            lax.slice_in_dim(block, block.shape[dim] - width, None, axis=dim), axis, forward
        )
        high = lax.ppermute(lax.slice_in_dim(block, 0, width, axis=dim), axis, backward)
        block = jnp.concatenate([low, block, high], axis=dim)
    return block


def any_frames(queries, keys, values, band_blocks):
    frame_rows, columns = queries.shape
    frames = lax.axis_size("tm")
    current = lax.axis_index("tm")
    half_rows = frame_rows // 2
    frame_blocks = frame_rows // BLOCK
    capacity = band_blocks.shape[2]
    heads_dev = columns // HD
    paired = jnp.stack([keys, values], 0)
    near_kv = padded(paired, (("tm", 1),), half_rows)
    position = jnp.arange(2 * frame_rows)
    near_ok = ((position >= half_rows) | (current > 0)) & (
        (position < half_rows + frame_rows) | (current < frames - 1)
    )
    kv_blocks = jnp.concatenate(
        [
            paired.reshape(2, frame_blocks, BLOCK, columns),
            jnp.zeros((2, 1, BLOCK, columns), jnp.bfloat16),
        ],
        1,
    )
    outgoing = lax.dynamic_index_in_dim(band_blocks, current, 1, keepdims=False)
    incoming = lax.dynamic_index_in_dim(band_blocks, current, 0, keepdims=False)
    outbound = jnp.take(kv_blocks, outgoing, axis=1)
    arrived = lax.all_to_all(outbound, "tm", split_axis=1, concat_axis=1, tiled=True)
    far_kv = arrived.reshape(2, frames * capacity * BLOCK, columns)
    far_ok = jnp.repeat((incoming != frame_blocks).reshape(-1), BLOCK)
    all_kv = jnp.concatenate([near_kv, far_kv], 1)
    visible = jnp.concatenate([near_ok, far_ok], 0)
    inv_root = HD ** (-0.5)

    def per_head(head_at):
        start = head_at * HD
        query_head = lax.dynamic_slice_in_dim(queries, start, HD, 1)
        key_head = lax.dynamic_slice_in_dim(all_kv[0], start, HD, 1)
        value_head = lax.dynamic_slice_in_dim(all_kv[1], start, HD, 1)
        scores = (
            lax.dot_general(
                query_head, key_head, (((1,), (1,)), ((), ())), preferred_element_type=jnp.float32
            )
            * inv_root
        )
        scores = jnp.where(visible[None, :], scores, masked_fill)
        row_max = jnp.max(scores, axis=1, keepdims=True)
        powers = jnp.exp(scores - row_max)
        row_sum = jnp.sum(powers, axis=1, keepdims=True)
        mixed_sum = jnp.dot(
            powers.astype(jnp.bfloat16), value_head, preferred_element_type=jnp.float32
        )
        return (mixed_sum / row_sum).astype(jnp.bfloat16)

    result = lax.map(per_head, jnp.arange(heads_dev, dtype=jnp.int32))
    return jnp.transpose(result, (1, 0, 2)).reshape(frame_rows, columns)


def run_copies(pairs, sems):
    copies = [
        pltpu.make_async_copy(source, target, sems.at[at])
        for at, (source, target) in enumerate(pairs)
    ]
    for copy in copies:
        copy.start()
    for copy in copies:
        copy.wait()


def rows_of(block):
    return pl.ds(pl.multiple_of(block * BLOCK, BLOCK), BLOCK)


def stage_near_kernel(half, bands, keys, values, listed, beside, token, sems):
    frame = lax.axis_index("tm")
    rows = pl.ds(pl.multiple_of(lax.rem(frame + 1, 2) * half, half), half)
    near = [
        pltpu.make_async_copy(source.at[rows], beside.at[kv], sems.at[kv])
        for kv, source in enumerate((keys, values))
    ]

    @pl.when((frame == 1) | (frame == 2))
    def _():
        reader = jnp.where(frame == 1, 3, 0)
        pairs = []
        for place in range(2):
            slot = jnp.where(frame == 1, place, 1 - place)
            rows = rows_of(bands[reader, slot, frame])
            for kv, source in enumerate((keys, values)):
                pairs.append((source.at[rows], listed.at[kv, pl.ds(place * BLOCK, BLOCK)]))
        for copy in near:
            copy.start()
        run_copies(pairs, sems.at[pl.ds(2, 4)])

    @pl.when((frame == 0) | (frame == 3))
    def _():
        for copy in near:
            copy.start()

    token[...] = jnp.zeros_like(token)
    for copy in near:
        copy.wait()


def stage_crossed_kernel(after, bands, keys, values, crossed, sems):
    frame = lax.axis_index("tm")

    @pl.when((frame == 0) | (frame == 3))
    def _():
        reader = jnp.where(frame == 0, 2, 1)
        pairs = []
        for slot in range(2):
            rows = rows_of(bands[reader, slot, frame])
            for kv, source in enumerate((keys, values)):
                pairs.append((source.at[rows], crossed.at[kv, pl.ds(slot * BLOCK, BLOCK)]))
        run_copies(pairs, sems)


def stage_last_kernel(cuts, after, bands, keys, values, *rest):
    direct, closing, sems = rest[: len(cuts)], rest[len(cuts) : -1], rest[-1]
    frame = lax.axis_index("tm")
    inner = (frame == 1) | (frame == 2)

    @pl.when(inner)
    def _():
        rows = rows_of(jnp.where(frame == 1, 5 - bands[3, 1, 1], 1 - bands[0, 0, 2]))
        run_copies(
            [
                (source.at[rows, pl.ds(*cut)], part.at[kv])
                for part, cut in zip(closing, cuts)
                for kv, source in enumerate((keys, values))
            ],
            sems,
        )

    @pl.when(jnp.logical_not(inner))
    def _():
        pairs = []
        for slot in range(2):
            rows = rows_of(bands[3 - frame, slot, frame])
            to = pl.ds(slot * BLOCK, BLOCK)
            for part, cut in zip(direct, cuts):
                for kv, source in enumerate((keys, values)):
                    pairs.append((source.at[rows, pl.ds(*cut)], part.at[kv, to]))
        run_copies(pairs, sems)


RATE = LOG2E * HD ** (-0.5)


def scores_of(queries, keys):
    return lax.dot_general(
        queries, keys, (((1,), (1,)), ((), ())), preferred_element_type=jnp.float32
    )


def attend_kernel(chunk, queries, keys, values, beside, crossed, mixed, tops, sums):
    frame = lax.axis_index("tm")
    inner = (frame == 1) | (frame == 2)
    rows, columns = queries.shape
    units = [(head, start) for head in range(columns // HD) for start in range(0, rows, chunk)]

    def attend(received):
        def pieces(head, kv):
            cols = pl.ds(head * HD, HD)
            own = values if kv else keys
            return [own[:, cols]] + [part[kv, :, cols] for part in received]

        def score(head, start):
            rows_q = queries[pl.ds(start, chunk), pl.ds(head * HD, HD)]
            return [scores_of(rows_q, piece) for piece in pieces(head, 0)]

        def finish(head, start, scores):
            at = pl.ds(start, chunk)
            row_max = functools.reduce(
                jnp.maximum, [jnp.max(part, axis=1, keepdims=True) for part in scores]
            )
            powers = [jnp.exp2((part - row_max) * RATE) for part in scores]
            row_sum = sum(jnp.sum(part, axis=1, keepdims=True) for part in powers)
            mixed[head, at] = sum(
                jnp.dot(part.astype(jnp.bfloat16), piece, preferred_element_type=jnp.float32)
                for part, piece in zip(powers, pieces(head, 1))
            )
            tops[head, at] = jnp.broadcast_to(row_max, (chunk, HD))
            sums[head, at] = jnp.broadcast_to(row_sum, (chunk, HD))

        scores = score(*units[0])
        for unit, following in zip(units, units[1:] + [None]):
            ahead = score(*following) if following else None
            finish(*unit, scores)
            scores = ahead

    pl.when(inner)(lambda: attend([beside, crossed]))
    pl.when(jnp.logical_not(inner))(lambda: attend([beside]))


def close_kernel(first, queries, listed, closing, relayed, direct, mixed, tops, sums, *rest):
    out, ready, sems = rest[-3:]
    frame = lax.axis_index("tm")
    inner = (frame == 1) | (frame == 2)

    def close(pieces):
        copies = []
        for at in range(ready.shape[0]):
            head = first // HD + at
            here, there = pl.ds(first + at * HD, HD), pl.ds(at * HD, HD)
            scores = [scores_of(queries[:, here], piece) for piece in pieces(0, here, there)]
            top = functools.reduce(
                jnp.maximum, [jnp.max(part, axis=1, keepdims=True) for part in scores], tops[head]
            )
            shrink = jnp.exp2((tops[head] - top) * RATE)
            powers = [jnp.exp2((part - top[:, :1]) * RATE) for part in scores]
            total = sums[head] * shrink + sum(
                jnp.sum(part, axis=1, keepdims=True) for part in powers
            )
            more = sum(
                jnp.dot(part.astype(jnp.bfloat16), piece, preferred_element_type=jnp.float32)
                for part, piece in zip(powers, pieces(1, here, there))
            )
            ready[at] = ((mixed[head] * shrink + more) / total).astype(jnp.bfloat16)
            copies.append(pltpu.make_async_copy(ready.at[at], out.at[:, here], sems.at[at]))
            copies[-1].start()
        for copy in copies:
            copy.wait()

    def of_inner(kv, here, there):
        facing = [listed[kv, pl.ds(BLOCK, BLOCK), here], closing[kv, :, there]]
        return [jnp.concatenate(facing, 0)]

    def of_edge(kv, here, there):
        return [relayed[kv, :, here], direct[kv, :, there]]

    pl.when(inner)(lambda: close(of_inner))
    pl.when(jnp.logical_not(inner))(lambda: close(of_edge))


def four_frames(queries, keys, values, band_blocks):
    rows, columns = queries.shape
    half = rows // 2
    heads = columns // HD
    anywhere = pl.BlockSpec(memory_space=pl.ANY)
    local = pl.BlockSpec(memory_space=pltpu.VMEM)
    scalars = pl.BlockSpec(memory_space=pltpu.SMEM)

    def send(array, pairs):
        return lax.ppermute(array, "tm", pairs)

    bands = jnp.transpose(band_blocks, (0, 2, 1))
    two = jax.ShapeDtypeStruct((2, 2 * BLOCK, columns), jnp.bfloat16)

    def stage(kernel, shapes, copies, operands, name, room):
        return pl.pallas_call(
            kernel,
            out_shape=shapes,
            in_specs=[scalars if operand is bands else anywhere for operand in operands],
            out_specs=[local] * len(shapes),
            scratch_shapes=[pltpu.SemaphoreType.DMA((copies,))],
            compiler_params=pltpu.CompilerParams(vmem_limit_bytes=room << 20),
            name=name,
        )(*operands)

    token = jax.ShapeDtypeStruct((8, HD), jnp.int32)
    listed, beside, after = stage(
        functools.partial(stage_near_kernel, half),
        [two, two, token],
        6,
        [bands, keys, values],
        "stage_near",
        51,
    )
    (crossed,) = stage(
        stage_crossed_kernel, [two], 4, [after, bands, keys, values], "stage_crossed", 32
    )
    beside = send(beside, [(0, 1), (1, 0), (2, 3), (3, 2)])
    listed = send(listed, [(1, 2), (2, 1)])
    crossed = send(crossed, [(0, 2), (3, 1)])
    relayed = send(listed, [(2, 3), (1, 0)])
    last = heads // 4
    cuts = [(0, heads - last), (heads - last, last)] if last else [(0, heads)]
    cuts = [(start * HD, size * HD) for start, size in cuts]
    last_parts = stage(
        functools.partial(stage_last_kernel, cuts),
        [
            jax.ShapeDtypeStruct((2, count * BLOCK, size), jnp.bfloat16)
            for count in (2, 1)
            for _, size in cuts
        ],
        4 * len(cuts),
        [beside, bands, keys, values],
        "stage_last",
        32,
    )
    direct, closing = last_parts[: len(cuts)], last_parts[len(cuts) :]
    direct = [send(part, [(0, 3), (3, 0)]) for part in direct]
    closing = [send(part, [(1, 2), (2, 1)]) for part in closing]

    state = jax.ShapeDtypeStruct((heads, rows, HD), jnp.float32)
    roomy = pltpu.CompilerParams(vmem_limit_bytes=32 << 20)
    mixed, tops, sums = pl.pallas_call(
        functools.partial(attend_kernel, rows // 2),
        out_shape=[state] * 3,
        in_specs=[local] * 5,
        out_specs=[local] * 3,
        compiler_params=roomy,
        name="attend",
    )(queries, keys, values, beside, crossed)
    result = None
    for near, far, (start, size) in zip(closing, direct, cuts):
        operands = [queries, listed, near, relayed, far, mixed, tops, sums]
        in_specs = [local] * len(operands)
        aliases = {}
        if result is not None:
            aliases = {len(operands): 0}
            in_specs.append(anywhere)
            operands.append(result)
        result = pl.pallas_call(
            functools.partial(close_kernel, start),
            out_shape=jax.ShapeDtypeStruct(queries.shape, queries.dtype),
            in_specs=in_specs,
            out_specs=anywhere,
            input_output_aliases=aliases,
            scratch_shapes=[
                pltpu.VMEM((size // HD, rows, HD), jnp.bfloat16),
                pltpu.SemaphoreType.DMA((size // HD,)),
            ],
            compiler_params=roomy,
            name="close",
        )(*operands)
    return result


def shards(queries, keys, values, band_blocks):
    if lax.axis_size("tm") == 4 and queries.shape[0] == 4 * BLOCK and band_blocks.shape[2] == 2:
        return four_frames(queries, keys, values, band_blocks)
    return any_frames(queries, keys, values, band_blocks)


def solution(mesh):
    placed = (
        P(("groups", "tm"), ("head", "sub")),
        P(("groups", "tm"), ("head", "sub")),
        P(("groups", "tm"), ("head", "sub")),
        P(),
    )
    return jax.shard_map(
        shards,
        mesh=mesh,
        in_specs=placed,
        out_specs=P(("groups", "tm"), ("head", "sub")),
        check_vma=False,
    )
```

```python
import functools

import jax
import jax.numpy as jnp
from jax import lax
from jax.experimental import pallas as pl
from jax.experimental.pallas import tpu as pltpu
from jax.sharding import PartitionSpec as P

HD = 128
BLOCK = 128
LOG2E = 1.4426950408889634

masked_fill = -1e30


def padded(block, sides, width):
    for axis, dim in sides:
        count = lax.axis_size(axis)
        forward = [(i, i + 1) for i in range(count - 1)]
        backward = [(target, source) for source, target in forward]
        low = lax.ppermute(
            lax.slice_in_dim(block, block.shape[dim] - width, None, axis=dim), axis, forward
        )
        high = lax.ppermute(lax.slice_in_dim(block, 0, width, axis=dim), axis, backward)
        block = jnp.concatenate([low, block, high], axis=dim)
    return block


def any_frames(queries, keys, values, band_blocks):
    frame_rows, columns = queries.shape
    frames = lax.axis_size("tm")
    current = lax.axis_index("tm")
    half_rows = frame_rows // 2
    frame_blocks = frame_rows // BLOCK
    capacity = band_blocks.shape[2]
    heads_dev = columns // HD
    paired = jnp.stack([keys, values], 0)
    near_kv = padded(paired, (("tm", 1),), half_rows)
    position = jnp.arange(2 * frame_rows)
    near_ok = ((position >= half_rows) | (current > 0)) & (
        (position < half_rows + frame_rows) | (current < frames - 1)
    )
    kv_blocks = jnp.concatenate(
        [
            paired.reshape(2, frame_blocks, BLOCK, columns),
            jnp.zeros((2, 1, BLOCK, columns), jnp.bfloat16),
        ],
        1,
    )
    outgoing = lax.dynamic_index_in_dim(band_blocks, current, 1, keepdims=False)
    incoming = lax.dynamic_index_in_dim(band_blocks, current, 0, keepdims=False)
    outbound = jnp.take(kv_blocks, outgoing, axis=1)
    arrived = lax.all_to_all(outbound, "tm", split_axis=1, concat_axis=1, tiled=True)
    far_kv = arrived.reshape(2, frames * capacity * BLOCK, columns)
    far_ok = jnp.repeat((incoming != frame_blocks).reshape(-1), BLOCK)
    all_kv = jnp.concatenate([near_kv, far_kv], 1)
    visible = jnp.concatenate([near_ok, far_ok], 0)
    inv_root = HD ** (-0.5)

    def per_head(head_at):
        start = head_at * HD
        query_head = lax.dynamic_slice_in_dim(queries, start, HD, 1)
        key_head = lax.dynamic_slice_in_dim(all_kv[0], start, HD, 1)
        value_head = lax.dynamic_slice_in_dim(all_kv[1], start, HD, 1)
        scores = (
            lax.dot_general(
                query_head, key_head, (((1,), (1,)), ((), ())), preferred_element_type=jnp.float32
            )
            * inv_root
        )
        scores = jnp.where(visible[None, :], scores, masked_fill)
        row_max = jnp.max(scores, axis=1, keepdims=True)
        powers = jnp.exp(scores - row_max)
        row_sum = jnp.sum(powers, axis=1, keepdims=True)
        mixed_sum = jnp.dot(
            powers.astype(jnp.bfloat16), value_head, preferred_element_type=jnp.float32
        )
        return (mixed_sum / row_sum).astype(jnp.bfloat16)

    result = lax.map(per_head, jnp.arange(heads_dev, dtype=jnp.int32))
    return jnp.transpose(result, (1, 0, 2)).reshape(frame_rows, columns)


def run_copies(pairs, sems):
    copies = [
        pltpu.make_async_copy(source, target, sems.at[at])
        for at, (source, target) in enumerate(pairs)
    ]
    for copy in copies:
        copy.start()
    for copy in copies:
        copy.wait()


def rows_of(block):
    return pl.ds(pl.multiple_of(block * BLOCK, BLOCK), BLOCK)


def stage_near_kernel(half, bands, keys, values, listed, beside, token, sems):
    frame = lax.axis_index("tm")
    rows = pl.ds(pl.multiple_of(lax.rem(frame + 1, 2) * half, half), half)
    near = [
        pltpu.make_async_copy(source.at[rows], beside.at[kv], sems.at[kv])
        for kv, source in enumerate((keys, values))
    ]

    @pl.when((frame == 1) | (frame == 2))
    def _():
        reader = jnp.where(frame == 1, 3, 0)
        pairs = []
        for place in range(2):
            slot = jnp.where(frame == 1, place, 1 - place)
            rows = rows_of(bands[reader, slot, frame])
            for kv, source in enumerate((keys, values)):
                pairs.append((source.at[rows], listed.at[kv, pl.ds(place * BLOCK, BLOCK)]))
        for copy in near:
            copy.start()
        run_copies(pairs, sems.at[pl.ds(2, 4)])

    @pl.when((frame == 0) | (frame == 3))
    def _():
        for copy in near:
            copy.start()

    token[...] = jnp.zeros_like(token)
    for copy in near:
        copy.wait()


def stage_crossed_kernel(after, bands, keys, values, crossed, sems):
    frame = lax.axis_index("tm")

    @pl.when((frame == 0) | (frame == 3))
    def _():
        reader = jnp.where(frame == 0, 2, 1)
        pairs = []
        for slot in range(2):
            rows = rows_of(bands[reader, slot, frame])
            for kv, source in enumerate((keys, values)):
                pairs.append((source.at[rows], crossed.at[kv, pl.ds(slot * BLOCK, BLOCK)]))
        run_copies(pairs, sems)


def stage_last_kernel(cuts, after, bands, keys, values, *rest):
    direct, closing, sems = rest[: len(cuts)], rest[len(cuts) : -1], rest[-1]
    frame = lax.axis_index("tm")
    inner = (frame == 1) | (frame == 2)

    @pl.when(inner)
    def _():
        rows = rows_of(jnp.where(frame == 1, 5 - bands[3, 1, 1], 1 - bands[0, 0, 2]))
        run_copies(
            [
                (source.at[rows, pl.ds(*cut)], part.at[kv])
                for part, cut in zip(closing, cuts)
                for kv, source in enumerate((keys, values))
            ],
            sems,
        )

    @pl.when(jnp.logical_not(inner))
    def _():
        pairs = []
        for slot in range(2):
            rows = rows_of(bands[3 - frame, slot, frame])
            to = pl.ds(slot * BLOCK, BLOCK)
            for part, cut in zip(direct, cuts):
                for kv, source in enumerate((keys, values)):
                    pairs.append((source.at[rows, pl.ds(*cut)], part.at[kv, to]))
        run_copies(pairs, sems)


RATE = LOG2E * HD ** (-0.5)


def scores_of(queries, keys):
    return lax.dot_general(
        queries, keys, (((1,), (1,)), ((), ())), preferred_element_type=jnp.float32
    )


def attend_kernel(
    chunk, queries, keys, values, beside, listed, crossed, mixed, tops, sums
):
    frame = lax.axis_index("tm")
    inner = (frame == 1) | (frame == 2)
    rows, columns = queries.shape
    units = [(head, start) for head in range(columns // HD) for start in range(0, rows, chunk)]

    def attend(pieces_of):
        def pieces(head, kv):
            cols = pl.ds(head * HD, HD)
            own = values if kv else keys
            return [own[:, cols], beside[kv, :, cols]] + pieces_of(kv, cols)

        def score(head, start):
            rows_q = queries[pl.ds(start, chunk), pl.ds(head * HD, HD)]
            return [scores_of(rows_q, piece) for piece in pieces(head, 0)]

        def finish(head, start, scores):
            at = pl.ds(start, chunk)
            row_max = functools.reduce(
                jnp.maximum, [jnp.max(part, axis=1, keepdims=True) for part in scores]
            )
            powers = [jnp.exp2((part - row_max) * RATE) for part in scores]
            row_sum = sum(jnp.sum(part, axis=1, keepdims=True) for part in powers)
            mixed[head, at] = sum(
                jnp.dot(part.astype(jnp.bfloat16), piece, preferred_element_type=jnp.float32)
                for part, piece in zip(powers, pieces(head, 1))
            )
            tops[head, at] = jnp.broadcast_to(row_max, (chunk, HD))
            sums[head, at] = jnp.broadcast_to(row_sum, (chunk, HD))

        scores = score(*units[0])
        for unit, following in zip(units, units[1:] + [None]):
            ahead = score(*following) if following else None
            finish(*unit, scores)
            scores = ahead

    def of_inner(kv, cols):
        return [crossed[kv, :, cols], listed[kv, pl.ds(BLOCK, BLOCK), cols]]

    pl.when(inner)(lambda: attend(of_inner))
    pl.when(jnp.logical_not(inner))(lambda: attend(lambda kv, cols: []))


def close_kernel(chunk, first, queries, closing, relayed, direct, mixed, tops, sums, *rest):
    out, ready, sems = rest[-3:]
    frame = lax.axis_index("tm")
    inner = (frame == 1) | (frame == 2)
    heads, rows, _ = ready.shape
    units = [(at, start) for at in range(heads) for start in range(0, rows, chunk)]

    def close(pieces_of):
        def pieces(at, kv):
            return pieces_of(kv, pl.ds(first + at * HD, HD), pl.ds(at * HD, HD))

        def score(at, start):
            rows_q = queries[pl.ds(start, chunk), pl.ds(first + at * HD, HD)]
            return [scores_of(rows_q, piece) for piece in pieces(at, 0)]

        def finish(at, start, scores):
            head, span = first // HD + at, pl.ds(start, chunk)
            old_top = tops[head, span]
            top = functools.reduce(
                jnp.maximum, [jnp.max(part, axis=1, keepdims=True) for part in scores], old_top
            )
            shrink = jnp.exp2((old_top - top) * RATE)
            powers = [jnp.exp2((part - top[:, :1]) * RATE) for part in scores]
            total = sums[head, span] * shrink + sum(
                jnp.sum(part, axis=1, keepdims=True) for part in powers
            )
            more = sum(
                jnp.dot(part.astype(jnp.bfloat16), piece, preferred_element_type=jnp.float32)
                for part, piece in zip(powers, pieces(at, 1))
            )
            whole = mixed[head, span] * shrink + more
            ready[at, span] = (whole / total).astype(jnp.bfloat16)

        copies = []
        scores = score(*units[0])
        for unit, following in zip(units, units[1:] + [None]):
            ahead = score(*following) if following else None
            finish(*unit, scores)
            scores = ahead
            at, start = unit
            if start + chunk == rows:
                here = pl.ds(first + at * HD, HD)
                copies.append(pltpu.make_async_copy(ready.at[at], out.at[:, here], sems.at[at]))
                copies[-1].start()
        for copy in copies:
            copy.wait()

    def of_inner(kv, here, there):
        return [closing[kv, :, there]]

    def of_edge(kv, here, there):
        return [relayed[kv, :, here], direct[kv, :, there]]

    pl.when(inner)(lambda: close(of_inner))
    pl.when(jnp.logical_not(inner))(lambda: close(of_edge))


def four_frames(queries, keys, values, band_blocks):
    rows, columns = queries.shape
    half = rows // 2
    heads = columns // HD
    anywhere = pl.BlockSpec(memory_space=pl.ANY)
    local = pl.BlockSpec(memory_space=pltpu.VMEM)
    scalars = pl.BlockSpec(memory_space=pltpu.SMEM)

    def send(array, pairs):
        return lax.ppermute(array, "tm", pairs)

    bands = jnp.transpose(band_blocks, (0, 2, 1))
    two = jax.ShapeDtypeStruct((2, 2 * BLOCK, columns), jnp.bfloat16)

    def stage(kernel, shapes, copies, operands, name, room):
        return pl.pallas_call(
            kernel,
            out_shape=shapes,
            in_specs=[scalars if operand is bands else anywhere for operand in operands],
            out_specs=[local] * len(shapes),
            scratch_shapes=[pltpu.SemaphoreType.DMA((copies,))],
            compiler_params=pltpu.CompilerParams(vmem_limit_bytes=room << 20),
            name=name,
        )(*operands)

    token = jax.ShapeDtypeStruct((8, HD), jnp.int32)
    listed, beside, after = stage(
        functools.partial(stage_near_kernel, half),
        [two, two, token],
        6,
        [bands, keys, values],
        "stage_near",
        51,
    )
    (crossed,) = stage(
        stage_crossed_kernel, [two], 4, [after, bands, keys, values], "stage_crossed", 32
    )
    beside = send(beside, [(0, 1), (1, 0), (2, 3), (3, 2)])
    listed = send(listed, [(1, 2), (2, 1)])
    crossed = send(crossed, [(0, 2), (3, 1)])
    relayed = send(listed, [(2, 3), (1, 0)])
    last = heads // 4
    cuts = [(0, heads - last), (heads - last, last)] if last else [(0, heads)]
    cuts = [(start * HD, size * HD) for start, size in cuts]
    last_parts = stage(
        functools.partial(stage_last_kernel, cuts),
        [
            jax.ShapeDtypeStruct((2, count * BLOCK, size), jnp.bfloat16)
            for count in (2, 1)
            for _, size in cuts
        ],
        4 * len(cuts),
        [beside, bands, keys, values],
        "stage_last",
        32,
    )
    direct, closing = last_parts[: len(cuts)], last_parts[len(cuts) :]
    direct = [send(part, [(0, 3), (3, 0)]) for part in direct]
    closing = [send(part, [(1, 2), (2, 1)]) for part in closing]

    state = jax.ShapeDtypeStruct((heads, rows, HD), jnp.float32)
    roomy = pltpu.CompilerParams(vmem_limit_bytes=32 << 20)
    mixed, tops, sums = pl.pallas_call(
        functools.partial(attend_kernel, rows // 2),
        out_shape=[state] * 3,
        in_specs=[local] * 6,
        out_specs=[local] * 3,
        compiler_params=roomy,
        name="attend",
    )(queries, keys, values, beside, listed, crossed)
    result = None
    for near, far, (start, size) in zip(closing, direct, cuts):
        operands = [queries, near, relayed, far, mixed, tops, sums]
        in_specs = [local] * len(operands)
        aliases = {}
        if result is not None:
            aliases = {len(operands): 0}
            in_specs.append(anywhere)
            operands.append(result)
        result = pl.pallas_call(
            functools.partial(close_kernel, rows // 2, start),
            out_shape=jax.ShapeDtypeStruct(queries.shape, queries.dtype),
            in_specs=in_specs,
            out_specs=anywhere,
            input_output_aliases=aliases,
            scratch_shapes=[
                pltpu.VMEM((size // HD, rows, HD), jnp.bfloat16),
                pltpu.SemaphoreType.DMA((size // HD,)),
            ],
            compiler_params=roomy,
            name="close",
        )(*operands)
    return result


def shards(queries, keys, values, band_blocks):
    if lax.axis_size("tm") == 4 and queries.shape[0] == 4 * BLOCK and band_blocks.shape[2] == 2:
        return four_frames(queries, keys, values, band_blocks)
    return any_frames(queries, keys, values, band_blocks)


def solution(mesh):
    placed = (
        P(("groups", "tm"), ("head", "sub")),
        P(("groups", "tm"), ("head", "sub")),
        P(("groups", "tm"), ("head", "sub")),
        P(),
    )
    return jax.shard_map(
        shards,
        mesh=mesh,
        in_specs=placed,
        out_specs=P(("groups", "tm"), ("head", "sub")),
        check_vma=False,
    )
```

```python
import functools

import jax
import jax.numpy as jnp
from jax import lax
from jax.experimental import pallas as pl
from jax.experimental.pallas import tpu as pltpu
from jax.sharding import PartitionSpec as P

HD = 128
BLOCK = 128
LOG2E = 1.4426950408889634

masked_fill = -1e30


def padded(block, sides, width):
    for axis, dim in sides:
        count = lax.axis_size(axis)
        forward = [(i, i + 1) for i in range(count - 1)]
        backward = [(target, source) for source, target in forward]
        low = lax.ppermute(
            lax.slice_in_dim(block, block.shape[dim] - width, None, axis=dim), axis, forward
        )
        high = lax.ppermute(lax.slice_in_dim(block, 0, width, axis=dim), axis, backward)
        block = jnp.concatenate([low, block, high], axis=dim)
    return block


def any_frames(queries, keys, values, band_blocks):
    frame_rows, columns = queries.shape
    frames = lax.axis_size("tm")
    current = lax.axis_index("tm")
    half_rows = frame_rows // 2
    frame_blocks = frame_rows // BLOCK
    capacity = band_blocks.shape[2]
    heads_dev = columns // HD
    paired = jnp.stack([keys, values], 0)
    near_kv = padded(paired, (("tm", 1),), half_rows)
    position = jnp.arange(2 * frame_rows)
    near_ok = ((position >= half_rows) | (current > 0)) & (
        (position < half_rows + frame_rows) | (current < frames - 1)
    )
    kv_blocks = jnp.concatenate(
        [
            paired.reshape(2, frame_blocks, BLOCK, columns),
            jnp.zeros((2, 1, BLOCK, columns), jnp.bfloat16),
        ],
        1,
    )
    outgoing = lax.dynamic_index_in_dim(band_blocks, current, 1, keepdims=False)
    incoming = lax.dynamic_index_in_dim(band_blocks, current, 0, keepdims=False)
    outbound = jnp.take(kv_blocks, outgoing, axis=1)
    arrived = lax.all_to_all(outbound, "tm", split_axis=1, concat_axis=1, tiled=True)
    far_kv = arrived.reshape(2, frames * capacity * BLOCK, columns)
    far_ok = jnp.repeat((incoming != frame_blocks).reshape(-1), BLOCK)
    all_kv = jnp.concatenate([near_kv, far_kv], 1)
    visible = jnp.concatenate([near_ok, far_ok], 0)
    inv_root = HD ** (-0.5)

    def per_head(head_at):
        start = head_at * HD
        query_head = lax.dynamic_slice_in_dim(queries, start, HD, 1)
        key_head = lax.dynamic_slice_in_dim(all_kv[0], start, HD, 1)
        value_head = lax.dynamic_slice_in_dim(all_kv[1], start, HD, 1)
        scores = (
            lax.dot_general(
                query_head, key_head, (((1,), (1,)), ((), ())), preferred_element_type=jnp.float32
            )
            * inv_root
        )
        scores = jnp.where(visible[None, :], scores, masked_fill)
        row_max = jnp.max(scores, axis=1, keepdims=True)
        powers = jnp.exp(scores - row_max)
        row_sum = jnp.sum(powers, axis=1, keepdims=True)
        mixed_sum = jnp.dot(
            powers.astype(jnp.bfloat16), value_head, preferred_element_type=jnp.float32
        )
        return (mixed_sum / row_sum).astype(jnp.bfloat16)

    result = lax.map(per_head, jnp.arange(heads_dev, dtype=jnp.int32))
    return jnp.transpose(result, (1, 0, 2)).reshape(frame_rows, columns)


def run_copies(pairs, sems):
    copies = [
        pltpu.make_async_copy(source, target, sems.at[at])
        for at, (source, target) in enumerate(pairs)
    ]
    for copy in copies:
        copy.start()
    for copy in copies:
        copy.wait()


def rows_of(block):
    return pl.ds(pl.multiple_of(block * BLOCK, BLOCK), BLOCK)


def stage_near_kernel(half, bands, keys, values, listed, beside, token, sems):
    frame = lax.axis_index("tm")
    rows = pl.ds(pl.multiple_of(lax.rem(frame + 1, 2) * half, half), half)
    near = [
        pltpu.make_async_copy(source.at[rows], beside.at[kv], sems.at[kv])
        for kv, source in enumerate((keys, values))
    ]

    @pl.when((frame == 1) | (frame == 2))
    def _():
        reader = jnp.where(frame == 1, 3, 0)
        pairs = []
        for place in range(2):
            slot = jnp.where(frame == 1, place, 1 - place)
            rows = rows_of(bands[reader, slot, frame])
            for kv, source in enumerate((keys, values)):
                pairs.append((source.at[rows], listed.at[kv, pl.ds(place * BLOCK, BLOCK)]))
        for copy in near:
            copy.start()
        run_copies(pairs, sems.at[pl.ds(2, 4)])

    @pl.when((frame == 0) | (frame == 3))
    def _():
        for copy in near:
            copy.start()

    token[...] = jnp.zeros_like(token)
    for copy in near:
        copy.wait()


def stage_crossed_kernel(after, bands, keys, values, crossed, sems):
    frame = lax.axis_index("tm")

    @pl.when((frame == 0) | (frame == 3))
    def _():
        reader = jnp.where(frame == 0, 2, 1)
        pairs = []
        for slot in range(2):
            rows = rows_of(bands[reader, slot, frame])
            for kv, source in enumerate((keys, values)):
                pairs.append((source.at[rows], crossed.at[kv, pl.ds(slot * BLOCK, BLOCK)]))
        run_copies(pairs, sems)


def stage_last_kernel(cuts, after, bands, keys, values, *rest):
    direct, closing, sems = rest[: len(cuts)], rest[len(cuts) : -1], rest[-1]
    frame = lax.axis_index("tm")
    inner = (frame == 1) | (frame == 2)

    @pl.when(inner)
    def _():
        rows = rows_of(jnp.where(frame == 1, 5 - bands[3, 1, 1], 1 - bands[0, 0, 2]))
        run_copies(
            [
                (source.at[rows, pl.ds(*cut)], part.at[kv])
                for part, cut in zip(closing, cuts)
                for kv, source in enumerate((keys, values))
            ],
            sems,
        )

    @pl.when(jnp.logical_not(inner))
    def _():
        pairs = []
        for slot in range(2):
            rows = rows_of(bands[3 - frame, slot, frame])
            to = pl.ds(slot * BLOCK, BLOCK)
            for part, cut in zip(direct, cuts):
                for kv, source in enumerate((keys, values)):
                    pairs.append((source.at[rows, pl.ds(*cut)], part.at[kv, to]))
        run_copies(pairs, sems)


RATE = LOG2E * HD ** (-0.5)


def scores_of(queries, keys):
    return lax.dot_general(
        queries, keys, (((1,), (1,)), ((), ())), preferred_element_type=jnp.float32
    )


def attend_kernel(
    chunk, queries, keys, values, beside, listed, crossed, mixed, tops, sums
):
    frame = lax.axis_index("tm")
    inner = (frame == 1) | (frame == 2)
    rows, columns = queries.shape
    units = [(head, start) for head in range(columns // HD) for start in range(0, rows, chunk)]

    def attend(pieces_of):
        def pieces(head, kv):
            cols = pl.ds(head * HD, HD)
            own = values if kv else keys
            return [own[:, cols], beside[kv, :, cols]] + pieces_of(kv, cols)

        def score(head, start):
            rows_q = queries[pl.ds(start, chunk), pl.ds(head * HD, HD)]
            return [scores_of(rows_q, piece) for piece in pieces(head, 0)]

        def finish(head, start, scores):
            at = pl.ds(start, chunk)
            row_max = functools.reduce(
                jnp.maximum, [jnp.max(part, axis=1, keepdims=True) for part in scores]
            )
            powers = [jnp.exp2((part - row_max) * RATE) for part in scores]
            row_sum = sum(jnp.sum(part, axis=1, keepdims=True) for part in powers)
            mixed[head, at] = sum(
                jnp.dot(part.astype(jnp.bfloat16), piece, preferred_element_type=jnp.float32)
                for part, piece in zip(powers, pieces(head, 1))
            )
            tops[head, at] = jnp.broadcast_to(row_max, (chunk, HD))
            sums[head, at] = jnp.broadcast_to(row_sum, (chunk, HD))

        scores = score(*units[0])
        for unit, following in zip(units, units[1:] + [None]):
            ahead = score(*following) if following else None
            finish(*unit, scores)
            scores = ahead

    def of_inner(kv, cols):
        return [crossed[kv, :, cols], listed[kv, pl.ds(BLOCK, BLOCK), cols]]

    pl.when(inner)(lambda: attend(of_inner))
    pl.when(jnp.logical_not(inner))(lambda: attend(lambda kv, cols: []))


def close_kernel(first, queries, closing, relayed, direct, mixed, tops, sums, *rest):
    out, ready, sems = rest[-3:]
    frame = lax.axis_index("tm")
    inner = (frame == 1) | (frame == 2)
    heads, rows, _ = ready.shape

    def close(pieces_of, chunk):
        units = [(at, start) for at in range(heads) for start in range(0, rows, chunk)]

        def pieces(at, kv):
            return pieces_of(kv, pl.ds(first + at * HD, HD), pl.ds(at * HD, HD))

        def score(at, start):
            rows_q = queries[pl.ds(start, chunk), pl.ds(first + at * HD, HD)]
            return [scores_of(rows_q, piece) for piece in pieces(at, 0)]

        def finish(at, start, scores):
            head, span = first // HD + at, pl.ds(start, chunk)
            old_top = tops[head, span]
            top = functools.reduce(
                jnp.maximum, [jnp.max(part, axis=1, keepdims=True) for part in scores], old_top
            )
            shrink = jnp.exp2((old_top - top) * RATE)
            powers = [jnp.exp2((part - top[:, :1]) * RATE) for part in scores]
            total = sums[head, span] * shrink + sum(
                jnp.sum(part, axis=1, keepdims=True) for part in powers
            )
            more = sum(
                jnp.dot(part.astype(jnp.bfloat16), piece, preferred_element_type=jnp.float32)
                for part, piece in zip(powers, pieces(at, 1))
            )
            whole = mixed[head, span] * shrink + more
            ready[at, span] = (whole / total).astype(jnp.bfloat16)

        copies = []
        scores = score(*units[0])
        for unit, following in zip(units, units[1:] + [None]):
            ahead = score(*following) if following else None
            finish(*unit, scores)
            scores = ahead
            at, start = unit
            if start + chunk == rows:
                here = pl.ds(first + at * HD, HD)
                copies.append(pltpu.make_async_copy(ready.at[at], out.at[:, here], sems.at[at]))
                copies[-1].start()
        for copy in copies:
            copy.wait()

    def of_inner(kv, here, there):
        return [closing[kv, :, there]]

    def of_edge(kv, here, there):
        return [relayed[kv, :, here], direct[kv, :, there]]

    pl.when(inner)(lambda: close(of_inner, rows))
    pl.when(jnp.logical_not(inner))(lambda: close(of_edge, rows // 2))


def four_frames(queries, keys, values, band_blocks):
    rows, columns = queries.shape
    half = rows // 2
    heads = columns // HD
    anywhere = pl.BlockSpec(memory_space=pl.ANY)
    local = pl.BlockSpec(memory_space=pltpu.VMEM)
    scalars = pl.BlockSpec(memory_space=pltpu.SMEM)

    def send(array, pairs):
        return lax.ppermute(array, "tm", pairs)

    bands = jnp.transpose(band_blocks, (0, 2, 1))
    two = jax.ShapeDtypeStruct((2, 2 * BLOCK, columns), jnp.bfloat16)

    def stage(kernel, shapes, copies, operands, name, room):
        return pl.pallas_call(
            kernel,
            out_shape=shapes,
            in_specs=[scalars if operand is bands else anywhere for operand in operands],
            out_specs=[local] * len(shapes),
            scratch_shapes=[pltpu.SemaphoreType.DMA((copies,))],
            compiler_params=pltpu.CompilerParams(vmem_limit_bytes=room << 20),
            name=name,
        )(*operands)

    token = jax.ShapeDtypeStruct((8, HD), jnp.int32)
    listed, beside, after = stage(
        functools.partial(stage_near_kernel, half),
        [two, two, token],
        6,
        [bands, keys, values],
        "stage_near",
        51,
    )
    (crossed,) = stage(
        stage_crossed_kernel, [two], 4, [after, bands, keys, values], "stage_crossed", 32
    )
    beside = send(beside, [(0, 1), (1, 0), (2, 3), (3, 2)])
    listed = send(listed, [(1, 2), (2, 1)])
    crossed = send(crossed, [(0, 2), (3, 1)])
    relayed = send(listed, [(2, 3), (1, 0)])
    last = heads // 4
    cuts = [(0, heads - last), (heads - last, last)] if last else [(0, heads)]
    cuts = [(start * HD, size * HD) for start, size in cuts]
    last_parts = stage(
        functools.partial(stage_last_kernel, cuts),
        [
            jax.ShapeDtypeStruct((2, count * BLOCK, size), jnp.bfloat16)
            for count in (2, 1)
            for _, size in cuts
        ],
        4 * len(cuts),
        [beside, bands, keys, values],
        "stage_last",
        32,
    )
    direct, closing = last_parts[: len(cuts)], last_parts[len(cuts) :]
    direct = [send(part, [(0, 3), (3, 0)]) for part in direct]
    closing = [send(part, [(1, 2), (2, 1)]) for part in closing]

    state = jax.ShapeDtypeStruct((heads, rows, HD), jnp.float32)
    roomy = pltpu.CompilerParams(vmem_limit_bytes=32 << 20)
    mixed, tops, sums = pl.pallas_call(
        functools.partial(attend_kernel, rows // 2),
        out_shape=[state] * 3,
        in_specs=[local] * 6,
        out_specs=[local] * 3,
        compiler_params=roomy,
        name="attend",
    )(queries, keys, values, beside, listed, crossed)
    result = None
    for near, far, (start, size) in zip(closing, direct, cuts):
        operands = [queries, near, relayed, far, mixed, tops, sums]
        in_specs = [local] * len(operands)
        aliases = {}
        if result is not None:
            aliases = {len(operands): 0}
            in_specs.append(anywhere)
            operands.append(result)
        result = pl.pallas_call(
            functools.partial(close_kernel, start),
            out_shape=jax.ShapeDtypeStruct(queries.shape, queries.dtype),
            in_specs=in_specs,
            out_specs=anywhere,
            input_output_aliases=aliases,
            scratch_shapes=[
                pltpu.VMEM((size // HD, rows, HD), jnp.bfloat16),
                pltpu.SemaphoreType.DMA((size // HD,)),
            ],
            compiler_params=roomy,
            name="close",
        )(*operands)
    return result


def shards(queries, keys, values, band_blocks):
    if lax.axis_size("tm") == 4 and queries.shape[0] == 4 * BLOCK and band_blocks.shape[2] == 2:
        return four_frames(queries, keys, values, band_blocks)
    return any_frames(queries, keys, values, band_blocks)


def solution(mesh):
    placed = (
        P(("groups", "tm"), ("head", "sub")),
        P(("groups", "tm"), ("head", "sub")),
        P(("groups", "tm"), ("head", "sub")),
        P(),
    )
    return jax.shard_map(
        shards,
        mesh=mesh,
        in_specs=placed,
        out_specs=P(("groups", "tm"), ("head", "sub")),
        check_vma=False,
    )
```

```python
import functools

import jax
import jax.numpy as jnp
from jax import lax
from jax.experimental import pallas as pl
from jax.experimental.pallas import tpu as pltpu
from jax.sharding import PartitionSpec as P

HD = 128
BLOCK = 128
LOG2E = 1.4426950408889634

masked_fill = -1e30


def padded(block, sides, width):
    for axis, dim in sides:
        count = lax.axis_size(axis)
        forward = [(i, i + 1) for i in range(count - 1)]
        backward = [(target, source) for source, target in forward]
        low = lax.ppermute(
            lax.slice_in_dim(block, block.shape[dim] - width, None, axis=dim), axis, forward
        )
        high = lax.ppermute(lax.slice_in_dim(block, 0, width, axis=dim), axis, backward)
        block = jnp.concatenate([low, block, high], axis=dim)
    return block


def any_frames(queries, keys, values, band_blocks):
    frame_rows, columns = queries.shape
    frames = lax.axis_size("tm")
    current = lax.axis_index("tm")
    half_rows = frame_rows // 2
    frame_blocks = frame_rows // BLOCK
    capacity = band_blocks.shape[2]
    heads_dev = columns // HD
    paired = jnp.stack([keys, values], 0)
    near_kv = padded(paired, (("tm", 1),), half_rows)
    position = jnp.arange(2 * frame_rows)
    near_ok = ((position >= half_rows) | (current > 0)) & (
        (position < half_rows + frame_rows) | (current < frames - 1)
    )
    kv_blocks = jnp.concatenate(
        [
            paired.reshape(2, frame_blocks, BLOCK, columns),
            jnp.zeros((2, 1, BLOCK, columns), jnp.bfloat16),
        ],
        1,
    )
    outgoing = lax.dynamic_index_in_dim(band_blocks, current, 1, keepdims=False)
    incoming = lax.dynamic_index_in_dim(band_blocks, current, 0, keepdims=False)
    outbound = jnp.take(kv_blocks, outgoing, axis=1)
    arrived = lax.all_to_all(outbound, "tm", split_axis=1, concat_axis=1, tiled=True)
    far_kv = arrived.reshape(2, frames * capacity * BLOCK, columns)
    far_ok = jnp.repeat((incoming != frame_blocks).reshape(-1), BLOCK)
    all_kv = jnp.concatenate([near_kv, far_kv], 1)
    visible = jnp.concatenate([near_ok, far_ok], 0)
    inv_root = HD ** (-0.5)

    def per_head(head_at):
        start = head_at * HD
        query_head = lax.dynamic_slice_in_dim(queries, start, HD, 1)
        key_head = lax.dynamic_slice_in_dim(all_kv[0], start, HD, 1)
        value_head = lax.dynamic_slice_in_dim(all_kv[1], start, HD, 1)
        scores = (
            lax.dot_general(
                query_head, key_head, (((1,), (1,)), ((), ())), preferred_element_type=jnp.float32
            )
            * inv_root
        )
        scores = jnp.where(visible[None, :], scores, masked_fill)
        row_max = jnp.max(scores, axis=1, keepdims=True)
        powers = jnp.exp(scores - row_max)
        row_sum = jnp.sum(powers, axis=1, keepdims=True)
        mixed_sum = jnp.dot(
            powers.astype(jnp.bfloat16), value_head, preferred_element_type=jnp.float32
        )
        return (mixed_sum / row_sum).astype(jnp.bfloat16)

    result = lax.map(per_head, jnp.arange(heads_dev, dtype=jnp.int32))
    return jnp.transpose(result, (1, 0, 2)).reshape(frame_rows, columns)


def run_copies(pairs, sems):
    copies = [
        pltpu.make_async_copy(source, target, sems.at[at])
        for at, (source, target) in enumerate(pairs)
    ]
    for copy in copies:
        copy.start()
    for copy in copies:
        copy.wait()


def rows_of(block):
    return pl.ds(pl.multiple_of(block * BLOCK, BLOCK), BLOCK)


def stage_near_kernel(half, bands, keys, values, listed, beside, token, sems):
    frame = lax.axis_index("tm")
    rows = pl.ds(pl.multiple_of(lax.rem(frame + 1, 2) * half, half), half)
    near = [
        pltpu.make_async_copy(source.at[rows], beside.at[kv], sems.at[kv])
        for kv, source in enumerate((keys, values))
    ]

    @pl.when((frame == 1) | (frame == 2))
    def _():
        reader = jnp.where(frame == 1, 3, 0)
        pairs = []
        for place in range(2):
            slot = jnp.where(frame == 1, place, 1 - place)
            rows = rows_of(bands[reader, slot, frame])
            for kv, source in enumerate((keys, values)):
                pairs.append((source.at[rows], listed.at[kv, pl.ds(place * BLOCK, BLOCK)]))
        for copy in near:
            copy.start()
        run_copies(pairs, sems.at[pl.ds(2, 4)])

    @pl.when((frame == 0) | (frame == 3))
    def _():
        for copy in near:
            copy.start()

    token[...] = jnp.zeros_like(token)
    for copy in near:
        copy.wait()


def stage_crossed_kernel(after, bands, keys, values, crossed, sems):
    frame = lax.axis_index("tm")

    @pl.when((frame == 0) | (frame == 3))
    def _():
        block = jnp.where(frame == 0, bands[2, 0, 0], bands[1, 1, 3])
        rows = rows_of(block)
        run_copies([(keys.at[rows], crossed.at[0]), (values.at[rows], crossed.at[1])], sems)


def relay_kernel(cuts, listed, *relayed):
    frame = lax.axis_index("tm")

    @pl.when((frame == 1) | (frame == 2))
    def _():
        for part, cut in zip(relayed, cuts):
            part[...] = listed[:, :, pl.ds(*cut)]


def stage_second_kernel(beside, bands, keys, values, traded, passed, sems):
    frame = lax.axis_index("tm")
    inner = (frame == 1) | (frame == 2)

    @pl.when(inner)
    def _():
        to_inner = rows_of(jnp.where(frame == 1, bands[2, 1, 0] - 2, bands[1, 0, 3]))
        to_edge = rows_of(jnp.where(frame == 1, bands[3, 1, 0] - 2, bands[0, 0, 3]))
        run_copies([(beside.at[:, to_inner], traded), (beside.at[:, to_edge], passed)], sems)

    @pl.when(jnp.logical_not(inner))
    def _():
        rows = rows_of(jnp.where(frame == 0, bands[3, 0, 0], bands[0, 1, 3]))
        run_copies([(keys.at[rows], traded.at[0]), (values.at[rows], traded.at[1])], sems)


def stage_closing_kernel(cuts, after, bands, keys, values, *rest):
    closing, sems = rest[:-1], rest[-1]
    frame = lax.axis_index("tm")

    @pl.when((frame == 1) | (frame == 2))
    def _():
        rows = rows_of(jnp.where(frame == 1, 5 - bands[3, 1, 1], 1 - bands[0, 0, 2]))
        run_copies(
            [
                (source.at[rows, pl.ds(*cut)], part.at[kv])
                for part, cut in zip(closing, cuts)
                for kv, source in enumerate((keys, values))
            ],
            sems,
        )


RATE = LOG2E * HD ** (-0.5)


def scores_of(queries, keys):
    return lax.dot_general(
        queries, keys, (((1,), (1,)), ((), ())), preferred_element_type=jnp.float32
    )


def attend_kernel(
    chunk, queries, keys, values, beside, listed, crossed, traded, mixed, tops, sums
):
    frame = lax.axis_index("tm")
    inner = (frame == 1) | (frame == 2)
    rows, columns = queries.shape
    units = [(head, start) for head in range(columns // HD) for start in range(0, rows, chunk)]

    def attend(pieces_of):
        def pieces(head, kv):
            cols = pl.ds(head * HD, HD)
            own = values if kv else keys
            return [own[:, cols], beside[kv, :, cols]] + pieces_of(kv, cols)

        def score(head, start):
            rows_q = queries[pl.ds(start, chunk), pl.ds(head * HD, HD)]
            return [scores_of(rows_q, piece) for piece in pieces(head, 0)]

        def finish(head, start, scores):
            at = pl.ds(start, chunk)
            row_max = functools.reduce(
                jnp.maximum, [jnp.max(part, axis=1, keepdims=True) for part in scores]
            )
            powers = [jnp.exp2((part - row_max) * RATE) for part in scores]
            row_sum = sum(jnp.sum(part, axis=1, keepdims=True) for part in powers)
            mixed[head, at] = sum(
                jnp.dot(part.astype(jnp.bfloat16), piece, preferred_element_type=jnp.float32)
                for part, piece in zip(powers, pieces(head, 1))
            )
            tops[head, at] = jnp.broadcast_to(row_max, (chunk, HD))
            sums[head, at] = jnp.broadcast_to(row_sum, (chunk, HD))

        scores = score(*units[0])
        for unit, following in zip(units, units[1:] + [None]):
            ahead = score(*following) if following else None
            finish(*unit, scores)
            scores = ahead

    def of_inner(kv, cols):
        listed_there = jnp.concatenate([crossed[kv, :, cols], traded[kv, :, cols]], 0)
        return [listed_there, listed[kv, pl.ds(BLOCK, BLOCK), cols]]

    def of_edge(kv, cols):
        return [traded[kv, :, cols]]

    pl.when(inner)(lambda: attend(of_inner))
    pl.when(jnp.logical_not(inner))(lambda: attend(of_edge))


def close_kernel(first, queries, closing, relayed, passed, mixed, tops, sums, *rest):
    out, ready, sems = rest[-3:]
    frame = lax.axis_index("tm")
    inner = (frame == 1) | (frame == 2)
    heads, rows, _ = ready.shape

    def close(pieces_of, chunk):
        units = [(at, start) for at in range(heads) for start in range(0, rows, chunk)]

        def pieces(at, kv):
            return pieces_of(kv, pl.ds(first + at * HD, HD), pl.ds(at * HD, HD))

        def score(at, start):
            rows_q = queries[pl.ds(start, chunk), pl.ds(first + at * HD, HD)]
            return [scores_of(rows_q, piece) for piece in pieces(at, 0)]

        def finish(at, start, scores):
            head, span = first // HD + at, pl.ds(start, chunk)
            old_top = tops[head, span]
            top = functools.reduce(
                jnp.maximum, [jnp.max(part, axis=1, keepdims=True) for part in scores], old_top
            )
            shrink = jnp.exp2((old_top - top) * RATE)
            powers = [jnp.exp2((part - top[:, :1]) * RATE) for part in scores]
            total = sums[head, span] * shrink + sum(
                jnp.sum(part, axis=1, keepdims=True) for part in powers
            )
            more = sum(
                jnp.dot(part.astype(jnp.bfloat16), piece, preferred_element_type=jnp.float32)
                for part, piece in zip(powers, pieces(at, 1))
            )
            whole = mixed[head, span] * shrink + more
            ready[at, span] = (whole / total).astype(jnp.bfloat16)

        copies = []
        scores = score(*units[0])
        for unit, following in zip(units, units[1:] + [None]):
            ahead = score(*following) if following else None
            finish(*unit, scores)
            scores = ahead
            at, start = unit
            if start + chunk == rows:
                here = pl.ds(first + at * HD, HD)
                copies.append(pltpu.make_async_copy(ready.at[at], out.at[:, here], sems.at[at]))
                copies[-1].start()
        for copy in copies:
            copy.wait()

    def of_inner(kv, here, there):
        return [closing[kv, :, there]]

    def of_edge(kv, here, there):
        return [relayed[kv, :, there], passed[kv, :, here]]

    pl.when(inner)(lambda: close(of_inner, rows))
    pl.when(jnp.logical_not(inner))(lambda: close(of_edge, rows // 2))


def four_frames(queries, keys, values, band_blocks):
    rows, columns = queries.shape
    half = rows // 2
    heads = columns // HD
    anywhere = pl.BlockSpec(memory_space=pl.ANY)
    local = pl.BlockSpec(memory_space=pltpu.VMEM)
    scalars = pl.BlockSpec(memory_space=pltpu.SMEM)

    def send(array, pairs):
        return lax.ppermute(array, "tm", pairs)

    bands = jnp.transpose(band_blocks, (0, 2, 1))
    one = jax.ShapeDtypeStruct((2, BLOCK, columns), jnp.bfloat16)
    two = jax.ShapeDtypeStruct((2, 2 * BLOCK, columns), jnp.bfloat16)

    def stage(kernel, shapes, copies, operands, name, room):
        return pl.pallas_call(
            kernel,
            out_shape=shapes,
            in_specs=[scalars if operand is bands else anywhere for operand in operands],
            out_specs=[local] * len(shapes),
            scratch_shapes=[pltpu.SemaphoreType.DMA((copies,))],
            compiler_params=pltpu.CompilerParams(vmem_limit_bytes=room << 20),
            name=name,
        )(*operands)

    token = jax.ShapeDtypeStruct((8, HD), jnp.int32)
    listed, beside, after = stage(
        functools.partial(stage_near_kernel, half),
        [two, two, token],
        6,
        [bands, keys, values],
        "stage_near",
        51,
    )
    (crossed,) = stage(
        stage_crossed_kernel, [one], 2, [after, bands, keys, values], "stage_crossed", 32
    )
    listed = send(listed, [(1, 2), (2, 1)])
    beside = send(beside, [(0, 1), (1, 0), (2, 3), (3, 2)])
    crossed = send(crossed, [(0, 2), (3, 1)])
    last = heads // 4
    cuts = [(0, heads - last), (heads - last, last)] if last else [(0, heads)]
    cuts = [(start * HD, size * HD) for start, size in cuts]

    def by_heads(blocks):
        return [jax.ShapeDtypeStruct((2, blocks * BLOCK, size), jnp.bfloat16) for _, size in cuts]

    relayed = pl.pallas_call(
        functools.partial(relay_kernel, cuts),
        out_shape=by_heads(2),
        in_specs=[local],
        out_specs=[local] * len(cuts),
        compiler_params=pltpu.CompilerParams(vmem_limit_bytes=32 << 20),
        name="relay",
    )(listed)
    relayed = [send(part, [(2, 3), (1, 0)]) for part in relayed]
    traded, passed = stage(
        stage_second_kernel, [one, one], 2, [beside, bands, keys, values], "stage_second", 32
    )
    traded = send(traded, [(0, 3), (3, 0), (1, 2), (2, 1)])
    passed = send(passed, [(1, 3), (2, 0)])
    closing = stage(
        functools.partial(stage_closing_kernel, cuts),
        by_heads(1),
        2 * len(cuts),
        [crossed, bands, keys, values],
        "stage_closing",
        32,
    )
    closing = [send(part, [(1, 2), (2, 1)]) for part in closing]

    state = jax.ShapeDtypeStruct((heads, rows, HD), jnp.float32)
    roomy = pltpu.CompilerParams(vmem_limit_bytes=32 << 20)
    mixed, tops, sums = pl.pallas_call(
        functools.partial(attend_kernel, rows // 2),
        out_shape=[state] * 3,
        in_specs=[local] * 7,
        out_specs=[local] * 3,
        compiler_params=roomy,
        name="attend",
    )(queries, keys, values, beside, listed, crossed, traded)
    result = None
    for near, far, (start, size) in zip(closing, relayed, cuts):
        operands = [queries, near, far, passed, mixed, tops, sums]
        in_specs = [local] * len(operands)
        aliases = {}
        if result is not None:
            aliases = {len(operands): 0}
            in_specs.append(anywhere)
            operands.append(result)
        result = pl.pallas_call(
            functools.partial(close_kernel, start),
            out_shape=jax.ShapeDtypeStruct(queries.shape, queries.dtype),
            in_specs=in_specs,
            out_specs=anywhere,
            input_output_aliases=aliases,
            scratch_shapes=[
                pltpu.VMEM((size // HD, rows, HD), jnp.bfloat16),
                pltpu.SemaphoreType.DMA((size // HD,)),
            ],
            compiler_params=roomy,
            name="close",
        )(*operands)
    return result


def shards(queries, keys, values, band_blocks):
    if lax.axis_size("tm") == 4 and queries.shape[0] == 4 * BLOCK and band_blocks.shape[2] == 2:
        return four_frames(queries, keys, values, band_blocks)
    return any_frames(queries, keys, values, band_blocks)


def solution(mesh):
    placed = (
        P(("groups", "tm"), ("head", "sub")),
        P(("groups", "tm"), ("head", "sub")),
        P(("groups", "tm"), ("head", "sub")),
        P(),
    )
    return jax.shard_map(
        shards,
        mesh=mesh,
        in_specs=placed,
        out_specs=P(("groups", "tm"), ("head", "sub")),
        check_vma=False,
    )
```

```python
import functools

import jax
import jax.numpy as jnp
from jax import lax
from jax.experimental import pallas as pl
from jax.experimental.pallas import tpu as pltpu
from jax.sharding import PartitionSpec as P

HD = 128
BLOCK = 128
LOG2E = 1.4426950408889634

masked_fill = -1e30


def padded(block, sides, width):
    for axis, dim in sides:
        count = lax.axis_size(axis)
        forward = [(i, i + 1) for i in range(count - 1)]
        backward = [(target, source) for source, target in forward]
        low = lax.ppermute(
            lax.slice_in_dim(block, block.shape[dim] - width, None, axis=dim), axis, forward
        )
        high = lax.ppermute(lax.slice_in_dim(block, 0, width, axis=dim), axis, backward)
        block = jnp.concatenate([low, block, high], axis=dim)
    return block


def any_frames(queries, keys, values, band_blocks):
    frame_rows, columns = queries.shape
    frames = lax.axis_size("tm")
    current = lax.axis_index("tm")
    half_rows = frame_rows // 2
    frame_blocks = frame_rows // BLOCK
    capacity = band_blocks.shape[2]
    heads_dev = columns // HD
    paired = jnp.stack([keys, values], 0)
    near_kv = padded(paired, (("tm", 1),), half_rows)
    position = jnp.arange(2 * frame_rows)
    near_ok = ((position >= half_rows) | (current > 0)) & (
        (position < half_rows + frame_rows) | (current < frames - 1)
    )
    kv_blocks = jnp.concatenate(
        [
            paired.reshape(2, frame_blocks, BLOCK, columns),
            jnp.zeros((2, 1, BLOCK, columns), jnp.bfloat16),
        ],
        1,
    )
    outgoing = lax.dynamic_index_in_dim(band_blocks, current, 1, keepdims=False)
    incoming = lax.dynamic_index_in_dim(band_blocks, current, 0, keepdims=False)
    outbound = jnp.take(kv_blocks, outgoing, axis=1)
    arrived = lax.all_to_all(outbound, "tm", split_axis=1, concat_axis=1, tiled=True)
    far_kv = arrived.reshape(2, frames * capacity * BLOCK, columns)
    far_ok = jnp.repeat((incoming != frame_blocks).reshape(-1), BLOCK)
    all_kv = jnp.concatenate([near_kv, far_kv], 1)
    visible = jnp.concatenate([near_ok, far_ok], 0)
    inv_root = HD ** (-0.5)

    def per_head(head_at):
        start = head_at * HD
        query_head = lax.dynamic_slice_in_dim(queries, start, HD, 1)
        key_head = lax.dynamic_slice_in_dim(all_kv[0], start, HD, 1)
        value_head = lax.dynamic_slice_in_dim(all_kv[1], start, HD, 1)
        scores = (
            lax.dot_general(
                query_head, key_head, (((1,), (1,)), ((), ())), preferred_element_type=jnp.float32
            )
            * inv_root
        )
        scores = jnp.where(visible[None, :], scores, masked_fill)
        row_max = jnp.max(scores, axis=1, keepdims=True)
        powers = jnp.exp(scores - row_max)
        row_sum = jnp.sum(powers, axis=1, keepdims=True)
        mixed_sum = jnp.dot(
            powers.astype(jnp.bfloat16), value_head, preferred_element_type=jnp.float32
        )
        return (mixed_sum / row_sum).astype(jnp.bfloat16)

    result = lax.map(per_head, jnp.arange(heads_dev, dtype=jnp.int32))
    return jnp.transpose(result, (1, 0, 2)).reshape(frame_rows, columns)


def run_copies(pairs, sems):
    copies = [
        pltpu.make_async_copy(source, target, sems.at[at])
        for at, (source, target) in enumerate(pairs)
    ]
    for copy in copies:
        copy.start()
    for copy in copies:
        copy.wait()


def rows_of(block):
    return pl.ds(pl.multiple_of(block * BLOCK, BLOCK), BLOCK)


def stage_near_kernel(half, bands, keys, values, listed, beside, token, sems):
    frame = lax.axis_index("tm")
    rows = pl.ds(pl.multiple_of(lax.rem(frame + 1, 2) * half, half), half)
    near = [
        pltpu.make_async_copy(source.at[rows], beside.at[kv], sems.at[kv])
        for kv, source in enumerate((keys, values))
    ]

    @pl.when((frame == 1) | (frame == 2))
    def _():
        reader = jnp.where(frame == 1, 3, 0)
        pairs = []
        for place in range(2):
            slot = jnp.where(frame == 1, place, 1 - place)
            rows = rows_of(bands[reader, slot, frame])
            for kv, source in enumerate((keys, values)):
                pairs.append((source.at[rows], listed.at[kv, pl.ds(place * BLOCK, BLOCK)]))
        for copy in near:
            copy.start()
        run_copies(pairs, sems.at[pl.ds(2, 4)])

    @pl.when((frame == 0) | (frame == 3))
    def _():
        for copy in near:
            copy.start()

    token[...] = jnp.zeros_like(token)
    for copy in near:
        copy.wait()


def other_rows(bands, frame):
    return rows_of(jnp.where(frame == 1, 5 - bands[3, 1, 1], 1 - bands[0, 0, 2]))


def stage_third_kernel(cut, after, bands, keys, values, crossed, closing, sems):
    frame = lax.axis_index("tm")
    inner = (frame == 1) | (frame == 2)

    @pl.when(inner)
    def _():
        rows = other_rows(bands, frame)
        run_copies(
            [
                (source.at[rows, pl.ds(*cut)], closing.at[kv])
                for kv, source in enumerate((keys, values))
            ],
            sems,
        )

    @pl.when(jnp.logical_not(inner))
    def _():
        rows = rows_of(jnp.where(frame == 0, bands[2, 0, 0], bands[1, 1, 3]))
        run_copies([(keys.at[rows], crossed.at[0]), (values.at[rows], crossed.at[1])], sems)


def relay_kernel(cuts, after, listed, *relayed):
    frame = lax.axis_index("tm")

    @pl.when((frame == 1) | (frame == 2))
    def _():
        for part, cut in zip(relayed, cuts):
            part[...] = listed[:, :, pl.ds(*cut)]


def stage_second_kernel(beside, bands, keys, values, traded, passed, sems):
    frame = lax.axis_index("tm")
    inner = (frame == 1) | (frame == 2)

    @pl.when(inner)
    def _():
        to_inner = rows_of(jnp.where(frame == 1, bands[2, 1, 0] - 2, bands[1, 0, 3]))
        to_edge = rows_of(jnp.where(frame == 1, bands[3, 1, 0] - 2, bands[0, 0, 3]))
        run_copies([(beside.at[:, to_inner], traded), (beside.at[:, to_edge], passed)], sems)

    @pl.when(jnp.logical_not(inner))
    def _():
        rows = rows_of(jnp.where(frame == 0, bands[3, 0, 0], bands[0, 1, 3]))
        run_copies([(keys.at[rows], traded.at[0]), (values.at[rows], traded.at[1])], sems)


def stage_closing_kernel(cuts, after, bands, keys, values, *rest):
    closing, sems = rest[:-1], rest[-1]
    frame = lax.axis_index("tm")

    @pl.when((frame == 1) | (frame == 2))
    def _():
        rows = other_rows(bands, frame)
        run_copies(
            [
                (source.at[rows, pl.ds(*cut)], part.at[kv])
                for part, cut in zip(closing, cuts)
                for kv, source in enumerate((keys, values))
            ],
            sems,
        )


RATE = LOG2E * HD ** (-0.5)


def scores_of(queries, keys):
    return lax.dot_general(
        queries, keys, (((1,), (1,)), ((), ())), preferred_element_type=jnp.float32
    )


def attend_kernel(
    chunk, queries, keys, values, beside, listed, crossed, traded, mixed, tops, sums
):
    frame = lax.axis_index("tm")
    inner = (frame == 1) | (frame == 2)
    rows, columns = queries.shape
    units = [(head, start) for head in range(columns // HD) for start in range(0, rows, chunk)]

    def attend(pieces_of):
        def pieces(head, kv):
            cols = pl.ds(head * HD, HD)
            own = values if kv else keys
            return [own[:, cols], beside[kv, :, cols]] + pieces_of(kv, cols)

        def score(head, start):
            rows_q = queries[pl.ds(start, chunk), pl.ds(head * HD, HD)]
            return [scores_of(rows_q, piece) for piece in pieces(head, 0)]

        def finish(head, start, scores):
            at = pl.ds(start, chunk)
            row_max = functools.reduce(
                jnp.maximum, [jnp.max(part, axis=1, keepdims=True) for part in scores]
            )
            powers = [jnp.exp2((part - row_max) * RATE) for part in scores]
            row_sum = sum(jnp.sum(part, axis=1, keepdims=True) for part in powers)
            mixed[head, at] = sum(
                jnp.dot(part.astype(jnp.bfloat16), piece, preferred_element_type=jnp.float32)
                for part, piece in zip(powers, pieces(head, 1))
            )
            tops[head, at] = jnp.broadcast_to(row_max, (chunk, HD))
            sums[head, at] = jnp.broadcast_to(row_sum, (chunk, HD))

        scores = score(*units[0])
        for unit, following in zip(units, units[1:] + [None]):
            ahead = score(*following) if following else None
            finish(*unit, scores)
            scores = ahead

    def of_inner(kv, cols):
        listed_there = jnp.concatenate([crossed[kv, :, cols], traded[kv, :, cols]], 0)
        return [listed_there, listed[kv, pl.ds(BLOCK, BLOCK), cols]]

    def of_edge(kv, cols):
        return [traded[kv, :, cols]]

    pl.when(inner)(lambda: attend(of_inner))
    pl.when(jnp.logical_not(inner))(lambda: attend(of_edge))


def close_kernel(
    first, early, queries, closing, early_relayed, late_relayed, passed, mixed, tops, sums, *rest
):
    out, ready, sems = rest[-3:]
    frame = lax.axis_index("tm")
    inner = (frame == 1) | (frame == 2)
    heads, rows, _ = ready.shape

    def close(pieces_of, chunk):
        units = [(at, start) for at in range(heads) for start in range(0, rows, chunk)]

        def pieces(at, kv):
            return pieces_of(kv, pl.ds(first + at * HD, HD), pl.ds(at * HD, HD))

        def score(at, start):
            rows_q = queries[pl.ds(start, chunk), pl.ds(first + at * HD, HD)]
            return [scores_of(rows_q, piece) for piece in pieces(at, 0)]

        def finish(at, start, scores):
            head, span = first // HD + at, pl.ds(start, chunk)
            old_top = tops[head, span]
            top = functools.reduce(
                jnp.maximum, [jnp.max(part, axis=1, keepdims=True) for part in scores], old_top
            )
            shrink = jnp.exp2((old_top - top) * RATE)
            powers = [jnp.exp2((part - top[:, :1]) * RATE) for part in scores]
            total = sums[head, span] * shrink + sum(
                jnp.sum(part, axis=1, keepdims=True) for part in powers
            )
            more = sum(
                jnp.dot(part.astype(jnp.bfloat16), piece, preferred_element_type=jnp.float32)
                for part, piece in zip(powers, pieces(at, 1))
            )
            whole = mixed[head, span] * shrink + more
            ready[at, span] = (whole / total).astype(jnp.bfloat16)

        copies = []
        scores = score(*units[0])
        for unit, following in zip(units, units[1:] + [None]):
            ahead = score(*following) if following else None
            finish(*unit, scores)
            scores = ahead
            at, start = unit
            if start + chunk == rows:
                here = pl.ds(first + at * HD, HD)
                copies.append(pltpu.make_async_copy(ready.at[at], out.at[:, here], sems.at[at]))
                copies[-1].start()
        for copy in copies:
            copy.wait()

    def of_inner(kv, here, there):
        return [closing[kv, :, there]]

    def of_edge(kv, here, there):
        if here.start < early:
            relayed = early_relayed[kv, :, here]
        else:
            relayed = late_relayed[kv, :, pl.ds(here.start - early, HD)]
        return [relayed, passed[kv, :, here]]

    pl.when(inner)(lambda: close(of_inner, rows))
    pl.when(jnp.logical_not(inner))(lambda: close(of_edge, rows // 2))


def four_frames(queries, keys, values, band_blocks):
    rows, columns = queries.shape
    half = rows // 2
    heads = columns // HD
    anywhere = pl.BlockSpec(memory_space=pl.ANY)
    local = pl.BlockSpec(memory_space=pltpu.VMEM)
    scalars = pl.BlockSpec(memory_space=pltpu.SMEM)

    def send(array, pairs):
        return lax.ppermute(array, "tm", pairs)

    bands = jnp.transpose(band_blocks, (0, 2, 1))
    one = jax.ShapeDtypeStruct((2, BLOCK, columns), jnp.bfloat16)
    two = jax.ShapeDtypeStruct((2, 2 * BLOCK, columns), jnp.bfloat16)

    def stage(kernel, shapes, copies, operands, name, room):
        return pl.pallas_call(
            kernel,
            out_shape=shapes,
            in_specs=[scalars if operand is bands else anywhere for operand in operands],
            out_specs=[local] * len(shapes),
            scratch_shapes=[pltpu.SemaphoreType.DMA((copies,))],
            compiler_params=pltpu.CompilerParams(vmem_limit_bytes=room << 20),
            name=name,
        )(*operands)

    token = jax.ShapeDtypeStruct((8, HD), jnp.int32)
    listed, beside, after = stage(
        functools.partial(stage_near_kernel, half),
        [two, two, token],
        6,
        [bands, keys, values],
        "stage_near",
        51,
    )
    last = heads // 4
    sizes = [1, heads - 2, 1]
    few = [(sum(sizes[:g]) * HD, size * HD) for g, size in enumerate(sizes)]
    cuts = [(0, (heads - last) * HD), ((heads - last) * HD, last * HD)]

    def by_heads(groups, blocks):
        return [
            jax.ShapeDtypeStruct((2, blocks * BLOCK, size), jnp.bfloat16) for _, size in groups
        ]

    crossed, first_closing = stage(
        functools.partial(stage_third_kernel, few[0]),
        [one] + by_heads(few[:1], 1),
        2,
        [after, bands, keys, values],
        "stage_third",
        32,
    )
    listed = send(listed, [(1, 2), (2, 1)])
    beside = send(beside, [(0, 1), (1, 0), (2, 3), (3, 2)])
    first_closing = send(first_closing, [(1, 2), (2, 1)])
    crossed = send(crossed, [(0, 2), (3, 1)])
    relayed = pl.pallas_call(
        functools.partial(relay_kernel, cuts),
        out_shape=by_heads(cuts, 2),
        in_specs=[anywhere, local],
        out_specs=[local] * len(cuts),
        compiler_params=pltpu.CompilerParams(vmem_limit_bytes=32 << 20),
        name="relay",
    )(first_closing, listed)
    relayed = [send(part, [(2, 3), (1, 0)]) for part in relayed]
    traded, passed = stage(
        stage_second_kernel, [one, one], 2, [beside, bands, keys, values], "stage_second", 32
    )
    traded = send(traded, [(0, 3), (3, 0), (1, 2), (2, 1)])
    passed = send(passed, [(1, 3), (2, 0)])
    closing = stage(
        functools.partial(stage_closing_kernel, few[1:]),
        by_heads(few[1:], 1),
        2 * len(few[1:]),
        [crossed, bands, keys, values],
        "stage_closing",
        32,
    )
    closing = [first_closing] + [send(part, [(1, 2), (2, 1)]) for part in closing]

    state = jax.ShapeDtypeStruct((heads, rows, HD), jnp.float32)
    roomy = pltpu.CompilerParams(vmem_limit_bytes=32 << 20)
    mixed, tops, sums = pl.pallas_call(
        functools.partial(attend_kernel, rows // 2),
        out_shape=[state] * 3,
        in_specs=[local] * 7,
        out_specs=[local] * 3,
        compiler_params=roomy,
        name="attend",
    )(queries, keys, values, beside, listed, crossed, traded)
    result = None
    for part, (start, size) in zip(closing, few):
        used = relayed if start + size > cuts[1][0] else relayed[:1] * 2
        operands = [queries, part, *used, passed, mixed, tops, sums]
        in_specs = [local] * len(operands)
        aliases = {}
        if result is not None:
            aliases = {len(operands): 0}
            in_specs.append(anywhere)
            operands.append(result)
        result = pl.pallas_call(
            functools.partial(close_kernel, start, cuts[1][0]),
            out_shape=jax.ShapeDtypeStruct(queries.shape, queries.dtype),
            in_specs=in_specs,
            out_specs=anywhere,
            input_output_aliases=aliases,
            scratch_shapes=[
                pltpu.VMEM((size // HD, rows, HD), jnp.bfloat16),
                pltpu.SemaphoreType.DMA((size // HD,)),
            ],
            compiler_params=roomy,
            name="close",
        )(*operands)
    return result


def shards(queries, keys, values, band_blocks):
    rows, columns = queries.shape
    shaped = rows == 4 * BLOCK and columns >= 4 * HD and band_blocks.shape[2] == 2
    if lax.axis_size("tm") == 4 and shaped:
        return four_frames(queries, keys, values, band_blocks)
    return any_frames(queries, keys, values, band_blocks)


def solution(mesh):
    placed = (
        P(("groups", "tm"), ("head", "sub")),
        P(("groups", "tm"), ("head", "sub")),
        P(("groups", "tm"), ("head", "sub")),
        P(),
    )
    return jax.shard_map(
        shards,
        mesh=mesh,
        in_specs=placed,
        out_specs=P(("groups", "tm"), ("head", "sub")),
        check_vma=False,
    )
```

```python
import functools

import jax
import jax.numpy as jnp
from jax import lax
from jax.experimental import pallas as pl
from jax.experimental.pallas import tpu as pltpu
from jax.sharding import PartitionSpec as P

HD = 128
BLOCK = 128
LOG2E = 1.4426950408889634

masked_fill = -1e30


def padded(block, sides, width):
    for axis, dim in sides:
        count = lax.axis_size(axis)
        forward = [(i, i + 1) for i in range(count - 1)]
        backward = [(target, source) for source, target in forward]
        low = lax.ppermute(
            lax.slice_in_dim(block, block.shape[dim] - width, None, axis=dim), axis, forward
        )
        high = lax.ppermute(lax.slice_in_dim(block, 0, width, axis=dim), axis, backward)
        block = jnp.concatenate([low, block, high], axis=dim)
    return block


def any_frames(queries, keys, values, band_blocks):
    frame_rows, columns = queries.shape
    frames = lax.axis_size("tm")
    current = lax.axis_index("tm")
    half_rows = frame_rows // 2
    frame_blocks = frame_rows // BLOCK
    capacity = band_blocks.shape[2]
    heads_dev = columns // HD
    paired = jnp.stack([keys, values], 0)
    near_kv = padded(paired, (("tm", 1),), half_rows)
    position = jnp.arange(2 * frame_rows)
    near_ok = ((position >= half_rows) | (current > 0)) & (
        (position < half_rows + frame_rows) | (current < frames - 1)
    )
    kv_blocks = jnp.concatenate(
        [
            paired.reshape(2, frame_blocks, BLOCK, columns),
            jnp.zeros((2, 1, BLOCK, columns), jnp.bfloat16),
        ],
        1,
    )
    outgoing = lax.dynamic_index_in_dim(band_blocks, current, 1, keepdims=False)
    incoming = lax.dynamic_index_in_dim(band_blocks, current, 0, keepdims=False)
    outbound = jnp.take(kv_blocks, outgoing, axis=1)
    arrived = lax.all_to_all(outbound, "tm", split_axis=1, concat_axis=1, tiled=True)
    far_kv = arrived.reshape(2, frames * capacity * BLOCK, columns)
    far_ok = jnp.repeat((incoming != frame_blocks).reshape(-1), BLOCK)
    all_kv = jnp.concatenate([near_kv, far_kv], 1)
    visible = jnp.concatenate([near_ok, far_ok], 0)
    inv_root = HD ** (-0.5)

    def per_head(head_at):
        start = head_at * HD
        query_head = lax.dynamic_slice_in_dim(queries, start, HD, 1)
        key_head = lax.dynamic_slice_in_dim(all_kv[0], start, HD, 1)
        value_head = lax.dynamic_slice_in_dim(all_kv[1], start, HD, 1)
        scores = (
            lax.dot_general(
                query_head, key_head, (((1,), (1,)), ((), ())), preferred_element_type=jnp.float32
            )
            * inv_root
        )
        scores = jnp.where(visible[None, :], scores, masked_fill)
        row_max = jnp.max(scores, axis=1, keepdims=True)
        powers = jnp.exp(scores - row_max)
        row_sum = jnp.sum(powers, axis=1, keepdims=True)
        mixed_sum = jnp.dot(
            powers.astype(jnp.bfloat16), value_head, preferred_element_type=jnp.float32
        )
        return (mixed_sum / row_sum).astype(jnp.bfloat16)

    result = lax.map(per_head, jnp.arange(heads_dev, dtype=jnp.int32))
    return jnp.transpose(result, (1, 0, 2)).reshape(frame_rows, columns)


def run_copies(pairs, sems):
    copies = [
        pltpu.make_async_copy(source, target, sems.at[at])
        for at, (source, target) in enumerate(pairs)
    ]
    for copy in copies:
        copy.start()
    for copy in copies:
        copy.wait()


def rows_of(block):
    return pl.ds(pl.multiple_of(block * BLOCK, BLOCK), BLOCK)


def stage_near_kernel(half, keys, values, facing, beside, token, sems):
    frame = lax.axis_index("tm")
    outer = pl.ds(pl.multiple_of(lax.rem(frame + 1, 2) * half, half), half)
    inner = pl.ds(pl.multiple_of(lax.rem(frame, 2) * half, half), half)
    token[...] = jnp.zeros_like(token)
    run_copies(
        [
            (source.at[rows], target.at[kv])
            for target, rows in ((facing, inner), (beside, outer))
            for kv, source in enumerate((keys, values))
        ],
        sems,
    )


def stage_missing_kernel(after, bands, keys, values, missing, sems):
    frame = lax.axis_index("tm")

    @pl.when((frame == 1) | (frame == 2))
    def _():
        rows = rows_of(jnp.where(frame == 1, bands[3, 0, 1], bands[0, 1, 2]))
        run_copies([(keys.at[rows], missing.at[0]), (values.at[rows], missing.at[1])], sems)


def stage_picked_kernel(facing, bands, picked, sems):
    frame = lax.axis_index("tm")

    @pl.when((frame == 1) | (frame == 2))
    def _():
        rows = rows_of(jnp.where(frame == 1, bands[0, 0, 2], bands[3, 1, 1] - 2))
        run_copies([(facing.at[:, rows], picked)], sems)


def stage_crossed_kernel(after, after_too, bands, keys, values, crossed, sems):
    frame = lax.axis_index("tm")

    @pl.when((frame == 0) | (frame == 3))
    def _():
        rows = rows_of(jnp.where(frame == 0, bands[2, 0, 0], bands[1, 1, 3]))
        run_copies([(keys.at[rows], crossed.at[0]), (values.at[rows], crossed.at[1])], sems)


def stage_passed_kernel(beside, bands, passed, sems):
    frame = lax.axis_index("tm")

    @pl.when((frame == 1) | (frame == 2))
    def _():
        rows = rows_of(jnp.where(frame == 1, bands[3, 1, 0] - 2, bands[0, 0, 3]))
        run_copies([(beside.at[:, rows], passed)], sems)


def stage_direct_kernel(after, bands, keys, values, direct, sems):
    frame = lax.axis_index("tm")

    @pl.when((frame == 0) | (frame == 3))
    def _():
        rows = rows_of(jnp.where(frame == 0, bands[3, 0, 0], bands[0, 1, 3]))
        run_copies([(keys.at[rows], direct.at[0]), (values.at[rows], direct.at[1])], sems)


def stage_traded_kernel(cut, after, beside, bands, traded, sems):
    frame = lax.axis_index("tm")

    @pl.when((frame == 1) | (frame == 2))
    def _():
        rows = rows_of(jnp.where(frame == 1, bands[2, 1, 0] - 2, bands[1, 0, 3]))
        run_copies([(beside.at[:, rows, pl.ds(*cut)], traded)], sems)


RATE = LOG2E * HD ** (-0.5)


def scores_of(queries, keys):
    return lax.dot_general(
        queries, keys, (((1,), (1,)), ((), ())), preferred_element_type=jnp.float32
    )


def attend_kernel(
    chunk, queries, keys, values, beside, facing, crossed, picked, lone, mixed, tops, sums
):
    frame = lax.axis_index("tm")
    inner = (frame == 1) | (frame == 2)
    rows, columns = queries.shape
    units = [(head, start) for head in range(columns // HD) for start in range(0, rows, chunk)]

    def attend(pieces_of):
        def pieces(head, kv):
            cols = pl.ds(head * HD, HD)
            own = values if kv else keys
            return [own[:, cols], beside[kv, :, cols]] + pieces_of(kv, cols)

        def score(head, start):
            rows_q = queries[pl.ds(start, chunk), pl.ds(head * HD, HD)]
            return [scores_of(rows_q, piece) for piece in pieces(head, 0)]

        def finish(head, start, scores):
            at = pl.ds(start, chunk)
            row_max = functools.reduce(
                jnp.maximum, [jnp.max(part, axis=1, keepdims=True) for part in scores]
            )
            powers = [jnp.exp2((part - row_max) * RATE) for part in scores]
            row_sum = sum(jnp.sum(part, axis=1, keepdims=True) for part in powers)
            mixed[head, at] = sum(
                jnp.dot(part.astype(jnp.bfloat16), piece, preferred_element_type=jnp.float32)
                for part, piece in zip(powers, pieces(head, 1))
            )
            tops[head, at] = jnp.broadcast_to(row_max, (chunk, HD))
            sums[head, at] = jnp.broadcast_to(row_sum, (chunk, HD))

        scores = score(*units[0])
        for unit, following in zip(units, units[1:] + [None]):
            ahead = score(*following) if following else None
            finish(*unit, scores)
            scores = ahead

    def of_inner(kv, cols):
        return [facing[kv, :, cols], crossed[kv, :, cols]]

    def of_edge(kv, cols):
        return [jnp.concatenate([picked[kv, :, cols], lone[kv, :, cols]], 0)]

    pl.when(inner)(lambda: attend(of_inner))
    pl.when(jnp.logical_not(inner))(lambda: attend(of_edge))


def close_kernel(first, queries, traded, passed, direct, mixed, tops, sums, *rest):
    out, ready, sems = rest[-3:]
    frame = lax.axis_index("tm")
    inner = (frame == 1) | (frame == 2)
    heads, rows, _ = ready.shape

    def close(pieces_of, chunk):
        units = [(at, start) for at in range(heads) for start in range(0, rows, chunk)]

        def pieces(at, kv):
            return pieces_of(kv, pl.ds(first + at * HD, HD), pl.ds(at * HD, HD))

        def score(at, start):
            rows_q = queries[pl.ds(start, chunk), pl.ds(first + at * HD, HD)]
            return [scores_of(rows_q, piece) for piece in pieces(at, 0)]

        def finish(at, start, scores):
            head, span = first // HD + at, pl.ds(start, chunk)
            old_top = tops[head, span]
            top = functools.reduce(
                jnp.maximum, [jnp.max(part, axis=1, keepdims=True) for part in scores], old_top
            )
            shrink = jnp.exp2((old_top - top) * RATE)
            powers = [jnp.exp2((part - top[:, :1]) * RATE) for part in scores]
            total = sums[head, span] * shrink + sum(
                jnp.sum(part, axis=1, keepdims=True) for part in powers
            )
            more = sum(
                jnp.dot(part.astype(jnp.bfloat16), piece, preferred_element_type=jnp.float32)
                for part, piece in zip(powers, pieces(at, 1))
            )
            whole = mixed[head, span] * shrink + more
            ready[at, span] = (whole / total).astype(jnp.bfloat16)

        copies = []
        scores = score(*units[0])
        for unit, following in zip(units, units[1:] + [None]):
            ahead = score(*following) if following else None
            finish(*unit, scores)
            scores = ahead
            at, start = unit
            if start + chunk == rows:
                here = pl.ds(first + at * HD, HD)
                copies.append(pltpu.make_async_copy(ready.at[at], out.at[:, here], sems.at[at]))
                copies[-1].start()
        for copy in copies:
            copy.wait()

    def of_inner(kv, here, there):
        return [traded[kv, :, there]]

    def of_edge(kv, here, there):
        return [jnp.concatenate([passed[kv, :, here], direct[kv, :, here]], 0)]

    pl.when(inner)(lambda: close(of_inner, rows))
    pl.when(jnp.logical_not(inner))(lambda: close(of_edge, rows // 2))


def four_frames(queries, keys, values, band_blocks):
    rows, columns = queries.shape
    half = rows // 2
    heads = columns // HD
    anywhere = pl.BlockSpec(memory_space=pl.ANY)
    local = pl.BlockSpec(memory_space=pltpu.VMEM)
    scalars = pl.BlockSpec(memory_space=pltpu.SMEM)

    def send(array, pairs):
        return lax.ppermute(array, "tm", pairs)

    bands = jnp.transpose(band_blocks, (0, 2, 1))
    one = jax.ShapeDtypeStruct((2, BLOCK, columns), jnp.bfloat16)
    two = jax.ShapeDtypeStruct((2, 2 * BLOCK, columns), jnp.bfloat16)

    def stage(kernel, shapes, copies, operands, name, room):
        return pl.pallas_call(
            kernel,
            out_shape=shapes,
            in_specs=[scalars if operand is bands else anywhere for operand in operands],
            out_specs=[local] * len(shapes),
            scratch_shapes=[pltpu.SemaphoreType.DMA((copies,))],
            compiler_params=pltpu.CompilerParams(vmem_limit_bytes=room << 20),
            name=name,
        )(*operands)

    token = jax.ShapeDtypeStruct((8, HD), jnp.int32)
    facing, beside, after = stage(
        functools.partial(stage_near_kernel, half),
        [two, two, token],
        4,
        [keys, values],
        "stage_near",
        51,
    )
    (missing,) = stage(
        stage_missing_kernel, [one], 2, [after, bands, keys, values], "stage_missing", 32
    )
    facing = send(facing, [(1, 2), (2, 1)])
    beside = send(beside, [(0, 1), (1, 0), (2, 3), (3, 2)])
    missing = send(missing, [(1, 2), (2, 1)])
    (picked,) = stage(stage_picked_kernel, [one], 1, [facing, bands], "stage_picked", 32)
    picked = send(picked, [(2, 3), (1, 0)])
    lone = send(missing, [(2, 3), (1, 0)])
    (passed,) = stage(stage_passed_kernel, [one], 1, [beside, bands], "stage_passed", 32)
    passed = send(passed, [(1, 3), (2, 0)])
    (crossed,) = stage(
        stage_crossed_kernel,
        [one],
        2,
        [missing, picked, bands, keys, values],
        "stage_crossed",
        32,
    )
    crossed = send(crossed, [(0, 2), (3, 1)])
    last = heads // 4
    cuts = [(0, heads - last), (heads - last, last)] if last else [(0, heads)]
    cuts = [(start * HD, size * HD) for start, size in cuts]
    (direct,) = stage(
        stage_direct_kernel, [one], 2, [missing, bands, keys, values], "stage_direct", 32
    )
    direct = send(direct, [(0, 3), (3, 0)])
    traded = []
    for cut, before in zip(cuts, (beside, passed)):
        (part,) = stage(
            functools.partial(stage_traded_kernel, cut),
            [jax.ShapeDtypeStruct((2, BLOCK, cut[1]), jnp.bfloat16)],
            1,
            [before, beside, bands],
            "stage_traded",
            32,
        )
        traded.append(send(part, [(1, 2), (2, 1)]))

    state = jax.ShapeDtypeStruct((heads, rows, HD), jnp.float32)
    roomy = pltpu.CompilerParams(vmem_limit_bytes=32 << 20)
    mixed, tops, sums = pl.pallas_call(
        functools.partial(attend_kernel, rows // 2),
        out_shape=[state] * 3,
        in_specs=[local] * 8,
        out_specs=[local] * 3,
        compiler_params=roomy,
        name="attend",
    )(queries, keys, values, beside, facing, crossed, picked, lone)
    result = None
    for part, (start, size) in zip(traded, cuts):
        operands = [queries, part, passed, direct, mixed, tops, sums]
        in_specs = [local] * len(operands)
        aliases = {}
        if result is not None:
            aliases = {len(operands): 0}
            in_specs.append(anywhere)
            operands.append(result)
        result = pl.pallas_call(
            functools.partial(close_kernel, start),
            out_shape=jax.ShapeDtypeStruct(queries.shape, queries.dtype),
            in_specs=in_specs,
            out_specs=anywhere,
            input_output_aliases=aliases,
            scratch_shapes=[
                pltpu.VMEM((size // HD, rows, HD), jnp.bfloat16),
                pltpu.SemaphoreType.DMA((size // HD,)),
            ],
            compiler_params=roomy,
            name="close",
        )(*operands)
    return result


def shards(queries, keys, values, band_blocks):
    if lax.axis_size("tm") == 4 and queries.shape[0] == 4 * BLOCK and band_blocks.shape[2] == 2:
        return four_frames(queries, keys, values, band_blocks)
    return any_frames(queries, keys, values, band_blocks)


def solution(mesh):
    placed = (
        P(("groups", "tm"), ("head", "sub")),
        P(("groups", "tm"), ("head", "sub")),
        P(("groups", "tm"), ("head", "sub")),
        P(),
    )
    return jax.shard_map(
        shards,
        mesh=mesh,
        in_specs=placed,
        out_specs=P(("groups", "tm"), ("head", "sub")),
        check_vma=False,
    )
```

```python
import functools

import jax
import jax.numpy as jnp
from jax import lax
from jax.experimental import pallas as pl
from jax.experimental.pallas import tpu as pltpu
from jax.sharding import PartitionSpec as P

HD = 128
BLOCK = 128
LOG2E = 1.4426950408889634

masked_fill = -1e30


def padded(block, sides, width):
    for axis, dim in sides:
        count = lax.axis_size(axis)
        forward = [(i, i + 1) for i in range(count - 1)]
        backward = [(target, source) for source, target in forward]
        low = lax.ppermute(
            lax.slice_in_dim(block, block.shape[dim] - width, None, axis=dim), axis, forward
        )
        high = lax.ppermute(lax.slice_in_dim(block, 0, width, axis=dim), axis, backward)
        block = jnp.concatenate([low, block, high], axis=dim)
    return block


def any_frames(queries, keys, values, band_blocks):
    frame_rows, columns = queries.shape
    frames = lax.axis_size("tm")
    current = lax.axis_index("tm")
    half_rows = frame_rows // 2
    frame_blocks = frame_rows // BLOCK
    capacity = band_blocks.shape[2]
    heads_dev = columns // HD
    paired = jnp.stack([keys, values], 0)
    near_kv = padded(paired, (("tm", 1),), half_rows)
    position = jnp.arange(2 * frame_rows)
    near_ok = ((position >= half_rows) | (current > 0)) & (
        (position < half_rows + frame_rows) | (current < frames - 1)
    )
    kv_blocks = jnp.concatenate(
        [
            paired.reshape(2, frame_blocks, BLOCK, columns),
            jnp.zeros((2, 1, BLOCK, columns), jnp.bfloat16),
        ],
        1,
    )
    outgoing = lax.dynamic_index_in_dim(band_blocks, current, 1, keepdims=False)
    incoming = lax.dynamic_index_in_dim(band_blocks, current, 0, keepdims=False)
    outbound = jnp.take(kv_blocks, outgoing, axis=1)
    arrived = lax.all_to_all(outbound, "tm", split_axis=1, concat_axis=1, tiled=True)
    far_kv = arrived.reshape(2, frames * capacity * BLOCK, columns)
    far_ok = jnp.repeat((incoming != frame_blocks).reshape(-1), BLOCK)
    all_kv = jnp.concatenate([near_kv, far_kv], 1)
    visible = jnp.concatenate([near_ok, far_ok], 0)
    inv_root = HD ** (-0.5)

    def per_head(head_at):
        start = head_at * HD
        query_head = lax.dynamic_slice_in_dim(queries, start, HD, 1)
        key_head = lax.dynamic_slice_in_dim(all_kv[0], start, HD, 1)
        value_head = lax.dynamic_slice_in_dim(all_kv[1], start, HD, 1)
        scores = (
            lax.dot_general(
                query_head, key_head, (((1,), (1,)), ((), ())), preferred_element_type=jnp.float32
            )
            * inv_root
        )
        scores = jnp.where(visible[None, :], scores, masked_fill)
        row_max = jnp.max(scores, axis=1, keepdims=True)
        powers = jnp.exp(scores - row_max)
        row_sum = jnp.sum(powers, axis=1, keepdims=True)
        mixed_sum = jnp.dot(
            powers.astype(jnp.bfloat16), value_head, preferred_element_type=jnp.float32
        )
        return (mixed_sum / row_sum).astype(jnp.bfloat16)

    result = lax.map(per_head, jnp.arange(heads_dev, dtype=jnp.int32))
    return jnp.transpose(result, (1, 0, 2)).reshape(frame_rows, columns)


def run_copies(pairs, sems):
    copies = [
        pltpu.make_async_copy(source, target, sems.at[at])
        for at, (source, target) in enumerate(pairs)
    ]
    for copy in copies:
        copy.start()
    for copy in copies:
        copy.wait()


def rows_of(block):
    return pl.ds(pl.multiple_of(block * BLOCK, BLOCK), BLOCK)


def stage_near_kernel(half, keys, values, facing, beside, token, sems):
    frame = lax.axis_index("tm")
    outer = pl.ds(pl.multiple_of(lax.rem(frame + 1, 2) * half, half), half)
    inner = pl.ds(pl.multiple_of(lax.rem(frame, 2) * half, half), half)
    token[...] = jnp.zeros_like(token)
    run_copies(
        [
            (source.at[rows], target.at[kv])
            for target, rows in ((facing, inner), (beside, outer))
            for kv, source in enumerate((keys, values))
        ],
        sems,
    )


def stage_missing_kernel(after, bands, keys, values, missing, sems):
    frame = lax.axis_index("tm")

    @pl.when((frame == 1) | (frame == 2))
    def _():
        rows = rows_of(jnp.where(frame == 1, bands[3, 0, 1], bands[0, 1, 2]))
        run_copies([(keys.at[rows], missing.at[0]), (values.at[rows], missing.at[1])], sems)


def stage_picked_kernel(facing, bands, picked, sems):
    frame = lax.axis_index("tm")

    @pl.when((frame == 1) | (frame == 2))
    def _():
        rows = rows_of(jnp.where(frame == 1, bands[0, 0, 2], bands[3, 1, 1] - 2))
        run_copies([(facing.at[:, rows], picked)], sems)


def stage_crossed_kernel(after, after_too, bands, keys, values, crossed, sems):
    frame = lax.axis_index("tm")

    @pl.when((frame == 0) | (frame == 3))
    def _():
        rows = rows_of(jnp.where(frame == 0, bands[2, 0, 0], bands[1, 1, 3]))
        run_copies([(keys.at[rows], crossed.at[0]), (values.at[rows], crossed.at[1])], sems)


def stage_passed_kernel(beside, bands, passed, sems):
    frame = lax.axis_index("tm")

    @pl.when((frame == 1) | (frame == 2))
    def _():
        rows = rows_of(jnp.where(frame == 1, bands[3, 1, 0] - 2, bands[0, 0, 3]))
        run_copies([(beside.at[:, rows], passed)], sems)


def stage_direct_kernel(after, bands, keys, values, direct, sems):
    frame = lax.axis_index("tm")

    @pl.when((frame == 0) | (frame == 3))
    def _():
        rows = rows_of(jnp.where(frame == 0, bands[3, 0, 0], bands[0, 1, 3]))
        run_copies([(keys.at[rows], direct.at[0]), (values.at[rows], direct.at[1])], sems)


def stage_traded_kernel(cut, after, after_too, beside, bands, traded, sems):
    frame = lax.axis_index("tm")

    @pl.when((frame == 1) | (frame == 2))
    def _():
        rows = rows_of(jnp.where(frame == 1, bands[2, 1, 0] - 2, bands[1, 0, 3]))
        run_copies([(beside.at[:, rows, pl.ds(*cut)], traded)], sems)


RATE = LOG2E * HD ** (-0.5)


def scores_of(queries, keys):
    return lax.dot_general(
        queries, keys, (((1,), (1,)), ((), ())), preferred_element_type=jnp.float32
    )


def attend_kernel(
    chunk, queries, keys, values, beside, facing, mixed, tops, sums
):
    frame = lax.axis_index("tm")
    inner = (frame == 1) | (frame == 2)
    rows, columns = queries.shape
    units = [(head, start) for head in range(columns // HD) for start in range(0, rows, chunk)]

    def attend(pieces_of):
        def pieces(head, kv):
            cols = pl.ds(head * HD, HD)
            own = values if kv else keys
            return [own[:, cols], beside[kv, :, cols]] + pieces_of(kv, cols)

        def score(head, start):
            rows_q = queries[pl.ds(start, chunk), pl.ds(head * HD, HD)]
            return [scores_of(rows_q, piece) for piece in pieces(head, 0)]

        def finish(head, start, scores):
            at = pl.ds(start, chunk)
            row_max = functools.reduce(
                jnp.maximum, [jnp.max(part, axis=1, keepdims=True) for part in scores]
            )
            powers = [jnp.exp2((part - row_max) * RATE) for part in scores]
            row_sum = sum(jnp.sum(part, axis=1, keepdims=True) for part in powers)
            mixed[head, at] = sum(
                jnp.dot(part.astype(jnp.bfloat16), piece, preferred_element_type=jnp.float32)
                for part, piece in zip(powers, pieces(head, 1))
            )
            tops[head, at] = jnp.broadcast_to(row_max, (chunk, HD))
            sums[head, at] = jnp.broadcast_to(row_sum, (chunk, HD))

        scores = score(*units[0])
        for unit, following in zip(units, units[1:] + [None]):
            ahead = score(*following) if following else None
            finish(*unit, scores)
            scores = ahead

    pl.when(inner)(lambda: attend(lambda kv, cols: [facing[kv, :, cols]]))
    pl.when(jnp.logical_not(inner))(lambda: attend(lambda kv, cols: []))


def close_kernel(
    first, queries, traded, crossed, picked, lone, passed, direct, mixed, tops, sums, *rest
):
    out, ready, sems = rest[-3:]
    frame = lax.axis_index("tm")
    inner = (frame == 1) | (frame == 2)
    heads, rows, _ = ready.shape

    def close(pieces_of, chunk):
        units = [(at, start) for at in range(heads) for start in range(0, rows, chunk)]

        def pieces(at, kv):
            return pieces_of(kv, pl.ds(first + at * HD, HD), pl.ds(at * HD, HD))

        def score(at, start):
            rows_q = queries[pl.ds(start, chunk), pl.ds(first + at * HD, HD)]
            return [scores_of(rows_q, piece) for piece in pieces(at, 0)]

        def finish(at, start, scores):
            head, span = first // HD + at, pl.ds(start, chunk)
            old_top = tops[head, span]
            top = functools.reduce(
                jnp.maximum, [jnp.max(part, axis=1, keepdims=True) for part in scores], old_top
            )
            shrink = jnp.exp2((old_top - top) * RATE)
            powers = [jnp.exp2((part - top[:, :1]) * RATE) for part in scores]
            total = sums[head, span] * shrink + sum(
                jnp.sum(part, axis=1, keepdims=True) for part in powers
            )
            more = sum(
                jnp.dot(part.astype(jnp.bfloat16), piece, preferred_element_type=jnp.float32)
                for part, piece in zip(powers, pieces(at, 1))
            )
            whole = mixed[head, span] * shrink + more
            ready[at, span] = (whole / total).astype(jnp.bfloat16)

        copies = []
        scores = score(*units[0])
        for unit, following in zip(units, units[1:] + [None]):
            ahead = score(*following) if following else None
            finish(*unit, scores)
            scores = ahead
            at, start = unit
            if start + chunk == rows:
                here = pl.ds(first + at * HD, HD)
                copies.append(pltpu.make_async_copy(ready.at[at], out.at[:, here], sems.at[at]))
                copies[-1].start()
        for copy in copies:
            copy.wait()

    def of_inner(kv, here, there):
        return [jnp.concatenate([crossed[kv, :, here], traded[kv, :, there]], 0)]

    def of_edge(kv, here, there):
        pairs = (picked, lone), (passed, direct)
        return [jnp.concatenate([part[kv, :, here] for part in pair], 0) for pair in pairs]

    pl.when(inner)(lambda: close(of_inner, rows // 2))
    pl.when(jnp.logical_not(inner))(lambda: close(of_edge, rows // 2))


def four_frames(queries, keys, values, band_blocks):
    rows, columns = queries.shape
    half = rows // 2
    heads = columns // HD
    anywhere = pl.BlockSpec(memory_space=pl.ANY)
    local = pl.BlockSpec(memory_space=pltpu.VMEM)
    scalars = pl.BlockSpec(memory_space=pltpu.SMEM)

    def send(array, pairs):
        return lax.ppermute(array, "tm", pairs)

    bands = jnp.transpose(band_blocks, (0, 2, 1))
    one = jax.ShapeDtypeStruct((2, BLOCK, columns), jnp.bfloat16)
    two = jax.ShapeDtypeStruct((2, 2 * BLOCK, columns), jnp.bfloat16)

    def stage(kernel, shapes, copies, operands, name, room):
        return pl.pallas_call(
            kernel,
            out_shape=shapes,
            in_specs=[scalars if operand is bands else anywhere for operand in operands],
            out_specs=[local] * len(shapes),
            scratch_shapes=[pltpu.SemaphoreType.DMA((copies,))],
            compiler_params=pltpu.CompilerParams(vmem_limit_bytes=room << 20),
            name=name,
        )(*operands)

    token = jax.ShapeDtypeStruct((8, HD), jnp.int32)
    facing, beside, after = stage(
        functools.partial(stage_near_kernel, half),
        [two, two, token],
        4,
        [keys, values],
        "stage_near",
        51,
    )
    (missing,) = stage(
        stage_missing_kernel, [one], 2, [after, bands, keys, values], "stage_missing", 32
    )
    facing = send(facing, [(1, 2), (2, 1)])
    beside = send(beside, [(0, 1), (1, 0), (2, 3), (3, 2)])
    missing = send(missing, [(1, 2), (2, 1)])
    (picked,) = stage(stage_picked_kernel, [one], 1, [facing, bands], "stage_picked", 32)
    picked = send(picked, [(2, 3), (1, 0)])
    lone = send(missing, [(2, 3), (1, 0)])
    (passed,) = stage(stage_passed_kernel, [one], 1, [beside, bands], "stage_passed", 32)
    passed = send(passed, [(1, 3), (2, 0)])
    (crossed,) = stage(
        stage_crossed_kernel,
        [one],
        2,
        [missing, picked, bands, keys, values],
        "stage_crossed",
        32,
    )
    crossed = send(crossed, [(0, 2), (3, 1)])
    last = heads // 4
    cuts = [(0, heads - last), (heads - last, last)] if last else [(0, heads)]
    cuts = [(start * HD, size * HD) for start, size in cuts]
    (direct,) = stage(
        stage_direct_kernel, [one], 2, [missing, bands, keys, values], "stage_direct", 32
    )
    direct = send(direct, [(0, 3), (3, 0)])
    state = jax.ShapeDtypeStruct((heads, rows, HD), jnp.float32)
    roomy = pltpu.CompilerParams(vmem_limit_bytes=32 << 20)
    mixed, tops, sums = pl.pallas_call(
        functools.partial(attend_kernel, rows // 2),
        out_shape=[state] * 3,
        in_specs=[local] * 5,
        out_specs=[local] * 3,
        compiler_params=roomy,
        name="attend",
    )(queries, keys, values, beside, facing)
    traded = []
    for cut, before in zip(cuts, ((beside, beside), (passed, sums))):
        (part,) = stage(
            functools.partial(stage_traded_kernel, cut),
            [jax.ShapeDtypeStruct((2, BLOCK, cut[1]), jnp.bfloat16)],
            1,
            [*before, beside, bands],
            "stage_traded",
            32,
        )
        traded.append(send(part, [(1, 2), (2, 1)]))

    result = None
    for part, (start, size) in zip(traded, cuts):
        operands = [queries, part, crossed, picked, lone, passed, direct, mixed, tops, sums]
        in_specs = [local] * len(operands)
        aliases = {}
        if result is not None:
            aliases = {len(operands): 0}
            in_specs.append(anywhere)
            operands.append(result)
        result = pl.pallas_call(
            functools.partial(close_kernel, start),
            out_shape=jax.ShapeDtypeStruct(queries.shape, queries.dtype),
            in_specs=in_specs,
            out_specs=anywhere,
            input_output_aliases=aliases,
            scratch_shapes=[
                pltpu.VMEM((size // HD, rows, HD), jnp.bfloat16),
                pltpu.SemaphoreType.DMA((size // HD,)),
            ],
            compiler_params=roomy,
            name="close",
        )(*operands)
    return result


def shards(queries, keys, values, band_blocks):
    if lax.axis_size("tm") == 4 and queries.shape[0] == 4 * BLOCK and band_blocks.shape[2] == 2:
        return four_frames(queries, keys, values, band_blocks)
    return any_frames(queries, keys, values, band_blocks)


def solution(mesh):
    placed = (
        P(("groups", "tm"), ("head", "sub")),
        P(("groups", "tm"), ("head", "sub")),
        P(("groups", "tm"), ("head", "sub")),
        P(),
    )
    return jax.shard_map(
        shards,
        mesh=mesh,
        in_specs=placed,
        out_specs=P(("groups", "tm"), ("head", "sub")),
        check_vma=False,
    )
```

```python
import functools

import jax
import jax.numpy as jnp
from jax import lax
from jax.experimental import pallas as pl
from jax.experimental.pallas import tpu as pltpu
from jax.sharding import PartitionSpec as P

HD = 128
BLOCK = 128
LOG2E = 1.4426950408889634

masked_fill = -1e30


def padded(block, sides, width):
    for axis, dim in sides:
        count = lax.axis_size(axis)
        forward = [(i, i + 1) for i in range(count - 1)]
        backward = [(target, source) for source, target in forward]
        low = lax.ppermute(
            lax.slice_in_dim(block, block.shape[dim] - width, None, axis=dim), axis, forward
        )
        high = lax.ppermute(lax.slice_in_dim(block, 0, width, axis=dim), axis, backward)
        block = jnp.concatenate([low, block, high], axis=dim)
    return block


def any_frames(queries, keys, values, band_blocks):
    frame_rows, columns = queries.shape
    frames = lax.axis_size("tm")
    current = lax.axis_index("tm")
    half_rows = frame_rows // 2
    frame_blocks = frame_rows // BLOCK
    capacity = band_blocks.shape[2]
    heads_dev = columns // HD
    paired = jnp.stack([keys, values], 0)
    near_kv = padded(paired, (("tm", 1),), half_rows)
    position = jnp.arange(2 * frame_rows)
    near_ok = ((position >= half_rows) | (current > 0)) & (
        (position < half_rows + frame_rows) | (current < frames - 1)
    )
    kv_blocks = jnp.concatenate(
        [
            paired.reshape(2, frame_blocks, BLOCK, columns),
            jnp.zeros((2, 1, BLOCK, columns), jnp.bfloat16),
        ],
        1,
    )
    outgoing = lax.dynamic_index_in_dim(band_blocks, current, 1, keepdims=False)
    incoming = lax.dynamic_index_in_dim(band_blocks, current, 0, keepdims=False)
    outbound = jnp.take(kv_blocks, outgoing, axis=1)
    arrived = lax.all_to_all(outbound, "tm", split_axis=1, concat_axis=1, tiled=True)
    far_kv = arrived.reshape(2, frames * capacity * BLOCK, columns)
    far_ok = jnp.repeat((incoming != frame_blocks).reshape(-1), BLOCK)
    all_kv = jnp.concatenate([near_kv, far_kv], 1)
    visible = jnp.concatenate([near_ok, far_ok], 0)
    inv_root = HD ** (-0.5)

    def per_head(head_at):
        start = head_at * HD
        query_head = lax.dynamic_slice_in_dim(queries, start, HD, 1)
        key_head = lax.dynamic_slice_in_dim(all_kv[0], start, HD, 1)
        value_head = lax.dynamic_slice_in_dim(all_kv[1], start, HD, 1)
        scores = (
            lax.dot_general(
                query_head, key_head, (((1,), (1,)), ((), ())), preferred_element_type=jnp.float32
            )
            * inv_root
        )
        scores = jnp.where(visible[None, :], scores, masked_fill)
        row_max = jnp.max(scores, axis=1, keepdims=True)
        powers = jnp.exp(scores - row_max)
        row_sum = jnp.sum(powers, axis=1, keepdims=True)
        mixed_sum = jnp.dot(
            powers.astype(jnp.bfloat16), value_head, preferred_element_type=jnp.float32
        )
        return (mixed_sum / row_sum).astype(jnp.bfloat16)

    result = lax.map(per_head, jnp.arange(heads_dev, dtype=jnp.int32))
    return jnp.transpose(result, (1, 0, 2)).reshape(frame_rows, columns)


def run_copies(pairs, sems):
    copies = [
        pltpu.make_async_copy(source, target, sems.at[at])
        for at, (source, target) in enumerate(pairs)
    ]
    for copy in copies:
        copy.start()
    for copy in copies:
        copy.wait()


def rows_of(block):
    return pl.ds(pl.multiple_of(block * BLOCK, BLOCK), BLOCK)


def stage_near_kernel(half, keys, values, facing, beside, token, sems):
    frame = lax.axis_index("tm")
    outer = pl.ds(pl.multiple_of(lax.rem(frame + 1, 2) * half, half), half)
    inner = pl.ds(pl.multiple_of(lax.rem(frame, 2) * half, half), half)
    token[...] = jnp.zeros_like(token)
    run_copies(
        [
            (source.at[rows], target.at[kv])
            for target, rows in ((facing, inner), (beside, outer))
            for kv, source in enumerate((keys, values))
        ],
        sems,
    )


def stage_missing_kernel(after, bands, keys, values, missing, sems):
    frame = lax.axis_index("tm")

    @pl.when((frame == 1) | (frame == 2))
    def _():
        rows = rows_of(jnp.where(frame == 1, bands[3, 0, 1], bands[0, 1, 2]))
        run_copies([(keys.at[rows], missing.at[0]), (values.at[rows], missing.at[1])], sems)


def stage_picked_kernel(facing, bands, picked, sems):
    frame = lax.axis_index("tm")

    @pl.when((frame == 1) | (frame == 2))
    def _():
        rows = rows_of(jnp.where(frame == 1, bands[0, 0, 2], bands[3, 1, 1] - 2))
        run_copies([(facing.at[:, rows], picked)], sems)


def stage_crossed_kernel(after, after_too, bands, keys, values, crossed, sems):
    frame = lax.axis_index("tm")

    @pl.when((frame == 0) | (frame == 3))
    def _():
        rows = rows_of(jnp.where(frame == 0, bands[2, 0, 0], bands[1, 1, 3]))
        run_copies([(keys.at[rows], crossed.at[0]), (values.at[rows], crossed.at[1])], sems)


def stage_passed_kernel(beside, bands, passed, sems):
    frame = lax.axis_index("tm")

    @pl.when((frame == 1) | (frame == 2))
    def _():
        rows = rows_of(jnp.where(frame == 1, bands[3, 1, 0] - 2, bands[0, 0, 3]))
        run_copies([(beside.at[:, rows], passed)], sems)


def stage_direct_kernel(after, bands, keys, values, direct, sems):
    frame = lax.axis_index("tm")

    @pl.when((frame == 0) | (frame == 3))
    def _():
        rows = rows_of(jnp.where(frame == 0, bands[3, 0, 0], bands[0, 1, 3]))
        run_copies([(keys.at[rows], direct.at[0]), (values.at[rows], direct.at[1])], sems)


def stage_traded_kernel(cut, after, after_too, beside, bands, traded, sems):
    frame = lax.axis_index("tm")

    @pl.when((frame == 1) | (frame == 2))
    def _():
        rows = rows_of(jnp.where(frame == 1, bands[2, 1, 0] - 2, bands[1, 0, 3]))
        run_copies([(beside.at[:, rows, pl.ds(*cut)], traded)], sems)


RATE = LOG2E * HD ** (-0.5)


def scores_of(queries, keys):
    return lax.dot_general(
        queries, keys, (((1,), (1,)), ((), ())), preferred_element_type=jnp.float32
    )


def attend_kernel(
    chunk, queries, keys, values, beside, facing, mixed, tops, sums
):
    frame = lax.axis_index("tm")
    inner = (frame == 1) | (frame == 2)
    rows, columns = queries.shape
    units = [(head, start) for head in range(columns // HD) for start in range(0, rows, chunk)]

    def attend(pieces_of):
        def pieces(head, kv):
            cols = pl.ds(head * HD, HD)
            own = values if kv else keys
            return [own[:, cols], beside[kv, :, cols]] + pieces_of(kv, cols)

        def score(head, start):
            rows_q = queries[pl.ds(start, chunk), pl.ds(head * HD, HD)]
            return [scores_of(rows_q, piece) for piece in pieces(head, 0)]

        def finish(head, start, scores):
            at = pl.ds(start, chunk)
            row_max = functools.reduce(
                jnp.maximum, [jnp.max(part, axis=1, keepdims=True) for part in scores]
            )
            powers = [jnp.exp2((part - row_max) * RATE) for part in scores]
            row_sum = sum(jnp.sum(part, axis=1, keepdims=True) for part in powers)
            mixed[head, at] = sum(
                jnp.dot(part.astype(jnp.bfloat16), piece, preferred_element_type=jnp.float32)
                for part, piece in zip(powers, pieces(head, 1))
            )
            tops[head, at] = jnp.broadcast_to(row_max, (chunk, HD))
            sums[head, at] = jnp.broadcast_to(row_sum, (chunk, HD))

        scores = score(*units[0])
        for unit, following in zip(units, units[1:] + [None]):
            ahead = score(*following) if following else None
            finish(*unit, scores)
            scores = ahead

    pl.when(inner)(lambda: attend(lambda kv, cols: [facing[kv, :, cols]]))
    pl.when(jnp.logical_not(inner))(lambda: attend(lambda kv, cols: []))


def merge_kernel(chunk, queries, crossed, picked, lone, mixed, tops, sums, *state):
    frame = lax.axis_index("tm")
    inner = (frame == 1) | (frame == 2)
    rows, columns = queries.shape
    new_mixed, new_tops, new_sums = state

    def merge(piece):
        for head in range(columns // HD):
            cols = pl.ds(head * HD, HD)
            for start in range(0, rows, chunk):
                at = pl.ds(start, chunk)
                scores = scores_of(queries[at, cols], piece(0, cols))
                old_top = tops[head, at]
                top = jnp.maximum(old_top, jnp.max(scores, axis=1, keepdims=True))
                shrink = jnp.exp2((old_top - top) * RATE)
                powers = jnp.exp2((scores - top[:, :1]) * RATE)
                row_sum = jnp.sum(powers, axis=1, keepdims=True)
                more = jnp.dot(
                    powers.astype(jnp.bfloat16),
                    piece(1, cols),
                    preferred_element_type=jnp.float32,
                )
                new_mixed[head, at] = mixed[head, at] * shrink + more
                new_tops[head, at] = top
                new_sums[head, at] = sums[head, at] * shrink + row_sum

    def of_edge(kv, cols):
        return jnp.concatenate([picked[kv, :, cols], lone[kv, :, cols]], 0)

    pl.when(inner)(lambda: merge(lambda kv, cols: crossed[kv, :, cols]))
    pl.when(jnp.logical_not(inner))(lambda: merge(of_edge))


def close_kernel(first, queries, traded, passed, direct, mixed, tops, sums, *rest):
    out, ready, sems = rest[-3:]
    frame = lax.axis_index("tm")
    inner = (frame == 1) | (frame == 2)
    heads, rows, _ = ready.shape

    def close(pieces_of, chunk):
        units = [(at, start) for at in range(heads) for start in range(0, rows, chunk)]

        def pieces(at, kv):
            return pieces_of(kv, pl.ds(first + at * HD, HD), pl.ds(at * HD, HD))

        def score(at, start):
            rows_q = queries[pl.ds(start, chunk), pl.ds(first + at * HD, HD)]
            return [scores_of(rows_q, piece) for piece in pieces(at, 0)]

        def finish(at, start, scores):
            head, span = first // HD + at, pl.ds(start, chunk)
            old_top = tops[head, span]
            top = functools.reduce(
                jnp.maximum, [jnp.max(part, axis=1, keepdims=True) for part in scores], old_top
            )
            shrink = jnp.exp2((old_top - top) * RATE)
            powers = [jnp.exp2((part - top[:, :1]) * RATE) for part in scores]
            total = sums[head, span] * shrink + sum(
                jnp.sum(part, axis=1, keepdims=True) for part in powers
            )
            more = sum(
                jnp.dot(part.astype(jnp.bfloat16), piece, preferred_element_type=jnp.float32)
                for part, piece in zip(powers, pieces(at, 1))
            )
            whole = mixed[head, span] * shrink + more
            ready[at, span] = (whole / total).astype(jnp.bfloat16)

        copies = []
        scores = score(*units[0])
        for unit, following in zip(units, units[1:] + [None]):
            ahead = score(*following) if following else None
            finish(*unit, scores)
            scores = ahead
            at, start = unit
            if start + chunk == rows:
                here = pl.ds(first + at * HD, HD)
                copies.append(pltpu.make_async_copy(ready.at[at], out.at[:, here], sems.at[at]))
                copies[-1].start()
        for copy in copies:
            copy.wait()

    def of_inner(kv, here, there):
        return [traded[kv, :, there]]

    def of_edge(kv, here, there):
        return [jnp.concatenate([passed[kv, :, here], direct[kv, :, here]], 0)]

    pl.when(inner)(lambda: close(of_inner, rows))
    pl.when(jnp.logical_not(inner))(lambda: close(of_edge, rows // 2))


def four_frames(queries, keys, values, band_blocks):
    rows, columns = queries.shape
    half = rows // 2
    heads = columns // HD
    anywhere = pl.BlockSpec(memory_space=pl.ANY)
    local = pl.BlockSpec(memory_space=pltpu.VMEM)
    scalars = pl.BlockSpec(memory_space=pltpu.SMEM)

    def send(array, pairs):
        return lax.ppermute(array, "tm", pairs)

    bands = jnp.transpose(band_blocks, (0, 2, 1))
    one = jax.ShapeDtypeStruct((2, BLOCK, columns), jnp.bfloat16)
    two = jax.ShapeDtypeStruct((2, 2 * BLOCK, columns), jnp.bfloat16)

    def stage(kernel, shapes, copies, operands, name, room):
        return pl.pallas_call(
            kernel,
            out_shape=shapes,
            in_specs=[scalars if operand is bands else anywhere for operand in operands],
            out_specs=[local] * len(shapes),
            scratch_shapes=[pltpu.SemaphoreType.DMA((copies,))],
            compiler_params=pltpu.CompilerParams(vmem_limit_bytes=room << 20),
            name=name,
        )(*operands)

    token = jax.ShapeDtypeStruct((8, HD), jnp.int32)
    facing, beside, after = stage(
        functools.partial(stage_near_kernel, half),
        [two, two, token],
        4,
        [keys, values],
        "stage_near",
        51,
    )
    (missing,) = stage(
        stage_missing_kernel, [one], 2, [after, bands, keys, values], "stage_missing", 32
    )
    facing = send(facing, [(1, 2), (2, 1)])
    beside = send(beside, [(0, 1), (1, 0), (2, 3), (3, 2)])
    missing = send(missing, [(1, 2), (2, 1)])
    (picked,) = stage(stage_picked_kernel, [one], 1, [facing, bands], "stage_picked", 32)
    picked = send(picked, [(2, 3), (1, 0)])
    lone = send(missing, [(2, 3), (1, 0)])
    (passed,) = stage(stage_passed_kernel, [one], 1, [beside, bands], "stage_passed", 32)
    passed = send(passed, [(1, 3), (2, 0)])
    (crossed,) = stage(
        stage_crossed_kernel,
        [one],
        2,
        [missing, picked, bands, keys, values],
        "stage_crossed",
        32,
    )
    crossed = send(crossed, [(0, 2), (3, 1)])
    last = heads // 4
    cuts = [(0, heads - last), (heads - last, last)] if last else [(0, heads)]
    cuts = [(start * HD, size * HD) for start, size in cuts]
    (direct,) = stage(
        stage_direct_kernel, [one], 2, [picked, bands, keys, values], "stage_direct", 32
    )
    direct = send(direct, [(0, 3), (3, 0)])
    state = jax.ShapeDtypeStruct((heads, rows, HD), jnp.float32)
    roomy = pltpu.CompilerParams(vmem_limit_bytes=32 << 20)
    mixed, tops, sums = pl.pallas_call(
        functools.partial(attend_kernel, rows // 2),
        out_shape=[state] * 3,
        in_specs=[local] * 5,
        out_specs=[local] * 3,
        compiler_params=roomy,
        name="attend",
    )(queries, keys, values, beside, facing)
    traded = []
    for cut, before in zip(cuts, ((beside, beside), (passed, sums))):
        (part,) = stage(
            functools.partial(stage_traded_kernel, cut),
            [jax.ShapeDtypeStruct((2, BLOCK, cut[1]), jnp.bfloat16)],
            1,
            [*before, beside, bands],
            "stage_traded",
            32,
        )
        traded.append(send(part, [(1, 2), (2, 1)]))

    mixed, tops, sums = pl.pallas_call(
        functools.partial(merge_kernel, rows // 2),
        out_shape=[state] * 3,
        in_specs=[local] * 7,
        out_specs=[local] * 3,
        compiler_params=roomy,
        name="merge",
    )(queries, crossed, picked, lone, mixed, tops, sums)
    result = None
    for part, (start, size) in zip(traded, cuts):
        operands = [queries, part, passed, direct, mixed, tops, sums]
        in_specs = [local] * len(operands)
        aliases = {}
        if result is not None:
            aliases = {len(operands): 0}
            in_specs.append(anywhere)
            operands.append(result)
        result = pl.pallas_call(
            functools.partial(close_kernel, start),
            out_shape=jax.ShapeDtypeStruct(queries.shape, queries.dtype),
            in_specs=in_specs,
            out_specs=anywhere,
            input_output_aliases=aliases,
            scratch_shapes=[
                pltpu.VMEM((size // HD, rows, HD), jnp.bfloat16),
                pltpu.SemaphoreType.DMA((size // HD,)),
            ],
            compiler_params=roomy,
            name="close",
        )(*operands)
    return result


def shards(queries, keys, values, band_blocks):
    if lax.axis_size("tm") == 4 and queries.shape[0] == 4 * BLOCK and band_blocks.shape[2] == 2:
        return four_frames(queries, keys, values, band_blocks)
    return any_frames(queries, keys, values, band_blocks)


def solution(mesh):
    placed = (
        P(("groups", "tm"), ("head", "sub")),
        P(("groups", "tm"), ("head", "sub")),
        P(("groups", "tm"), ("head", "sub")),
        P(),
    )
    return jax.shard_map(
        shards,
        mesh=mesh,
        in_specs=placed,
        out_specs=P(("groups", "tm"), ("head", "sub")),
        check_vma=False,
    )
```

```python
import functools

import jax
import jax.numpy as jnp
from jax import lax
from jax.experimental import pallas as pl
from jax.experimental.pallas import tpu as pltpu
from jax.sharding import PartitionSpec as P

HD = 128
BLOCK = 128
LOG2E = 1.4426950408889634

masked_fill = -1e30


def padded(block, sides, width):
    for axis, dim in sides:
        count = lax.axis_size(axis)
        forward = [(i, i + 1) for i in range(count - 1)]
        backward = [(target, source) for source, target in forward]
        low = lax.ppermute(
            lax.slice_in_dim(block, block.shape[dim] - width, None, axis=dim), axis, forward
        )
        high = lax.ppermute(lax.slice_in_dim(block, 0, width, axis=dim), axis, backward)
        block = jnp.concatenate([low, block, high], axis=dim)
    return block


def any_frames(queries, keys, values, band_blocks):
    frame_rows, columns = queries.shape
    frames = lax.axis_size("tm")
    current = lax.axis_index("tm")
    half_rows = frame_rows // 2
    frame_blocks = frame_rows // BLOCK
    capacity = band_blocks.shape[2]
    heads_dev = columns // HD
    paired = jnp.stack([keys, values], 0)
    near_kv = padded(paired, (("tm", 1),), half_rows)
    position = jnp.arange(2 * frame_rows)
    near_ok = ((position >= half_rows) | (current > 0)) & (
        (position < half_rows + frame_rows) | (current < frames - 1)
    )
    kv_blocks = jnp.concatenate(
        [
            paired.reshape(2, frame_blocks, BLOCK, columns),
            jnp.zeros((2, 1, BLOCK, columns), jnp.bfloat16),
        ],
        1,
    )
    outgoing = lax.dynamic_index_in_dim(band_blocks, current, 1, keepdims=False)
    incoming = lax.dynamic_index_in_dim(band_blocks, current, 0, keepdims=False)
    outbound = jnp.take(kv_blocks, outgoing, axis=1)
    arrived = lax.all_to_all(outbound, "tm", split_axis=1, concat_axis=1, tiled=True)
    far_kv = arrived.reshape(2, frames * capacity * BLOCK, columns)
    far_ok = jnp.repeat((incoming != frame_blocks).reshape(-1), BLOCK)
    all_kv = jnp.concatenate([near_kv, far_kv], 1)
    visible = jnp.concatenate([near_ok, far_ok], 0)
    inv_root = HD ** (-0.5)

    def per_head(head_at):
        start = head_at * HD
        query_head = lax.dynamic_slice_in_dim(queries, start, HD, 1)
        key_head = lax.dynamic_slice_in_dim(all_kv[0], start, HD, 1)
        value_head = lax.dynamic_slice_in_dim(all_kv[1], start, HD, 1)
        scores = (
            lax.dot_general(
                query_head, key_head, (((1,), (1,)), ((), ())), preferred_element_type=jnp.float32
            )
            * inv_root
        )
        scores = jnp.where(visible[None, :], scores, masked_fill)
        row_max = jnp.max(scores, axis=1, keepdims=True)
        powers = jnp.exp(scores - row_max)
        row_sum = jnp.sum(powers, axis=1, keepdims=True)
        mixed_sum = jnp.dot(
            powers.astype(jnp.bfloat16), value_head, preferred_element_type=jnp.float32
        )
        return (mixed_sum / row_sum).astype(jnp.bfloat16)

    result = lax.map(per_head, jnp.arange(heads_dev, dtype=jnp.int32))
    return jnp.transpose(result, (1, 0, 2)).reshape(frame_rows, columns)


def run_copies(pairs, sems):
    copies = [
        pltpu.make_async_copy(source, target, sems.at[at])
        for at, (source, target) in enumerate(pairs)
    ]
    for copy in copies:
        copy.start()
    for copy in copies:
        copy.wait()


def rows_of(block):
    return pl.ds(pl.multiple_of(block * BLOCK, BLOCK), BLOCK)


def stage_near_kernel(half, keys, values, facing, beside, token, sems):
    frame = lax.axis_index("tm")
    outer = pl.ds(pl.multiple_of(lax.rem(frame + 1, 2) * half, half), half)
    inner = pl.ds(pl.multiple_of(lax.rem(frame, 2) * half, half), half)
    token[...] = jnp.zeros_like(token)
    run_copies(
        [
            (source.at[rows], target.at[kv])
            for target, rows in ((facing, inner), (beside, outer))
            for kv, source in enumerate((keys, values))
        ],
        sems,
    )


def stage_missing_kernel(after, bands, keys, values, missing, sems):
    frame = lax.axis_index("tm")

    @pl.when((frame == 1) | (frame == 2))
    def _():
        rows = rows_of(jnp.where(frame == 1, bands[3, 0, 1], bands[0, 1, 2]))
        run_copies([(keys.at[rows], missing.at[0]), (values.at[rows], missing.at[1])], sems)


def stage_picked_kernel(facing, bands, picked, sems):
    frame = lax.axis_index("tm")

    @pl.when((frame == 1) | (frame == 2))
    def _():
        rows = rows_of(jnp.where(frame == 1, bands[0, 0, 2], bands[3, 1, 1] - 2))
        run_copies([(facing.at[:, rows], picked)], sems)


def stage_crossed_kernel(after, after_too, bands, keys, values, crossed, sems):
    frame = lax.axis_index("tm")

    @pl.when((frame == 0) | (frame == 3))
    def _():
        rows = rows_of(jnp.where(frame == 0, bands[2, 0, 0], bands[1, 1, 3]))
        run_copies([(keys.at[rows], crossed.at[0]), (values.at[rows], crossed.at[1])], sems)


def stage_passed_kernel(beside, bands, passed, sems):
    frame = lax.axis_index("tm")

    @pl.when((frame == 1) | (frame == 2))
    def _():
        rows = rows_of(jnp.where(frame == 1, bands[3, 1, 0] - 2, bands[0, 0, 3]))
        run_copies([(beside.at[:, rows], passed)], sems)


def stage_direct_kernel(after, bands, keys, values, direct, sems):
    frame = lax.axis_index("tm")

    @pl.when((frame == 0) | (frame == 3))
    def _():
        rows = rows_of(jnp.where(frame == 0, bands[3, 0, 0], bands[0, 1, 3]))
        run_copies([(keys.at[rows], direct.at[0]), (values.at[rows], direct.at[1])], sems)


def stage_traded_kernel(cut, after, after_too, beside, bands, traded, sems):
    frame = lax.axis_index("tm")

    @pl.when((frame == 1) | (frame == 2))
    def _():
        rows = rows_of(jnp.where(frame == 1, bands[2, 1, 0] - 2, bands[1, 0, 3]))
        run_copies([(beside.at[:, rows, pl.ds(*cut)], traded)], sems)


RATE = LOG2E * HD ** (-0.5)


def scores_of(queries, keys):
    return lax.dot_general(
        queries, keys, (((1,), (1,)), ((), ())), preferred_element_type=jnp.float32
    )


def attend_kernel(
    chunk, queries, keys, values, beside, facing, picked, mixed, tops, sums, token
):
    frame = lax.axis_index("tm")
    inner = (frame == 1) | (frame == 2)
    rows, columns = queries.shape
    token[...] = jnp.zeros_like(token)
    units = [(head, start) for head in range(columns // HD) for start in range(0, rows, chunk)]

    def attend(pieces_of):
        def pieces(head, kv):
            cols = pl.ds(head * HD, HD)
            own = values if kv else keys
            return [own[:, cols], beside[kv, :, cols]] + pieces_of(kv, cols)

        def score(head, start):
            rows_q = queries[pl.ds(start, chunk), pl.ds(head * HD, HD)]
            return [scores_of(rows_q, piece) for piece in pieces(head, 0)]

        def finish(head, start, scores):
            at = pl.ds(start, chunk)
            row_max = functools.reduce(
                jnp.maximum, [jnp.max(part, axis=1, keepdims=True) for part in scores]
            )
            powers = [jnp.exp2((part - row_max) * RATE) for part in scores]
            row_sum = sum(jnp.sum(part, axis=1, keepdims=True) for part in powers)
            mixed[head, at] = sum(
                jnp.dot(part.astype(jnp.bfloat16), piece, preferred_element_type=jnp.float32)
                for part, piece in zip(powers, pieces(head, 1))
            )
            tops[head, at] = jnp.broadcast_to(row_max, (chunk, HD))
            sums[head, at] = jnp.broadcast_to(row_sum, (chunk, HD))

        scores = score(*units[0])
        for unit, following in zip(units, units[1:] + [None]):
            ahead = score(*following) if following else None
            finish(*unit, scores)
            scores = ahead

    pl.when(inner)(lambda: attend(lambda kv, cols: [facing[kv, :, cols]]))
    pl.when(jnp.logical_not(inner))(lambda: attend(lambda kv, cols: [picked[kv, :, cols]]))


def merge_kernel(chunk, after, queries, crossed, mixed, tops, sums, *state):
    frame = lax.axis_index("tm")
    rows, columns = queries.shape
    new_mixed, new_tops, new_sums = state

    @pl.when((frame == 1) | (frame == 2))
    def _():
        for head in range(columns // HD):
            cols = pl.ds(head * HD, HD)
            for start in range(0, rows, chunk):
                at = pl.ds(start, chunk)
                scores = scores_of(queries[at, cols], crossed[0, :, cols])
                old_top = tops[head, at]
                top = jnp.maximum(old_top, jnp.max(scores, axis=1, keepdims=True))
                shrink = jnp.exp2((old_top - top) * RATE)
                powers = jnp.exp2((scores - top[:, :1]) * RATE)
                row_sum = jnp.sum(powers, axis=1, keepdims=True)
                more = jnp.dot(
                    powers.astype(jnp.bfloat16),
                    crossed[1, :, cols],
                    preferred_element_type=jnp.float32,
                )
                new_mixed[head, at] = mixed[head, at] * shrink + more
                new_sums[head, at] = sums[head, at] * shrink + row_sum
                new_tops[head, at] = top


def close_kernel(first, queries, traded, lone, passed, direct, mixed, tops, sums, *rest):
    out, ready, sems = rest[-3:]
    frame = lax.axis_index("tm")
    inner = (frame == 1) | (frame == 2)
    heads, rows, _ = ready.shape

    def close(pieces_of, chunk):
        units = [(at, start) for at in range(heads) for start in range(0, rows, chunk)]

        def pieces(at, kv):
            return pieces_of(kv, pl.ds(first + at * HD, HD), pl.ds(at * HD, HD))

        def score(at, start):
            rows_q = queries[pl.ds(start, chunk), pl.ds(first + at * HD, HD)]
            return [scores_of(rows_q, piece) for piece in pieces(at, 0)]

        def finish(at, start, scores):
            head, span = first // HD + at, pl.ds(start, chunk)
            old_top = tops[head, span]
            top = functools.reduce(
                jnp.maximum, [jnp.max(part, axis=1, keepdims=True) for part in scores], old_top
            )
            shrink = jnp.exp2((old_top - top) * RATE)
            powers = [jnp.exp2((part - top[:, :1]) * RATE) for part in scores]
            total = sums[head, span] * shrink + sum(
                jnp.sum(part, axis=1, keepdims=True) for part in powers
            )
            more = sum(
                jnp.dot(part.astype(jnp.bfloat16), piece, preferred_element_type=jnp.float32)
                for part, piece in zip(powers, pieces(at, 1))
            )
            whole = mixed[head, span] * shrink + more
            ready[at, span] = (whole / total).astype(jnp.bfloat16)

        copies = []
        scores = score(*units[0])
        for unit, following in zip(units, units[1:] + [None]):
            ahead = score(*following) if following else None
            finish(*unit, scores)
            scores = ahead
            at, start = unit
            if start + chunk == rows:
                here = pl.ds(first + at * HD, HD)
                copies.append(pltpu.make_async_copy(ready.at[at], out.at[:, here], sems.at[at]))
                copies[-1].start()
        for copy in copies:
            copy.wait()

    def of_inner(kv, here, there):
        return [traded[kv, :, there]]

    def of_edge(kv, here, there):
        pair = jnp.concatenate([passed[kv, :, here], direct[kv, :, here]], 0)
        return [pair, lone[kv, :, here]]

    pl.when(inner)(lambda: close(of_inner, rows))
    pl.when(jnp.logical_not(inner))(lambda: close(of_edge, rows // 2))


def four_frames(queries, keys, values, band_blocks):
    rows, columns = queries.shape
    half = rows // 2
    heads = columns // HD
    anywhere = pl.BlockSpec(memory_space=pl.ANY)
    local = pl.BlockSpec(memory_space=pltpu.VMEM)
    scalars = pl.BlockSpec(memory_space=pltpu.SMEM)

    def send(array, pairs):
        return lax.ppermute(array, "tm", pairs)

    bands = jnp.transpose(band_blocks, (0, 2, 1))
    one = jax.ShapeDtypeStruct((2, BLOCK, columns), jnp.bfloat16)
    two = jax.ShapeDtypeStruct((2, 2 * BLOCK, columns), jnp.bfloat16)

    def stage(kernel, shapes, copies, operands, name, room):
        return pl.pallas_call(
            kernel,
            out_shape=shapes,
            in_specs=[scalars if operand is bands else anywhere for operand in operands],
            out_specs=[local] * len(shapes),
            scratch_shapes=[pltpu.SemaphoreType.DMA((copies,))],
            compiler_params=pltpu.CompilerParams(vmem_limit_bytes=room << 20),
            name=name,
        )(*operands)

    token = jax.ShapeDtypeStruct((8, HD), jnp.int32)
    facing, beside, after = stage(
        functools.partial(stage_near_kernel, half),
        [two, two, token],
        4,
        [keys, values],
        "stage_near",
        51,
    )
    (missing,) = stage(
        stage_missing_kernel, [one], 2, [after, bands, keys, values], "stage_missing", 32
    )
    facing = send(facing, [(1, 2), (2, 1)])
    beside = send(beside, [(0, 1), (1, 0), (2, 3), (3, 2)])
    missing = send(missing, [(1, 2), (2, 1)])
    (picked,) = stage(stage_picked_kernel, [one], 1, [facing, bands], "stage_picked", 32)
    picked = send(picked, [(2, 3), (1, 0)])
    lone = send(missing, [(2, 3), (1, 0)])
    (passed,) = stage(stage_passed_kernel, [one], 1, [beside, bands], "stage_passed", 32)
    passed = send(passed, [(1, 3), (2, 0)])
    (crossed,) = stage(
        stage_crossed_kernel,
        [one],
        2,
        [missing, picked, bands, keys, values],
        "stage_crossed",
        32,
    )
    crossed = send(crossed, [(0, 2), (3, 1)])
    last = heads // 4
    cuts = [(0, heads - last), (heads - last, last)] if last else [(0, heads)]
    cuts = [(start * HD, size * HD) for start, size in cuts]
    (direct,) = stage(
        stage_direct_kernel, [one], 2, [picked, bands, keys, values], "stage_direct", 32
    )
    direct = send(direct, [(0, 3), (3, 0)])
    state = jax.ShapeDtypeStruct((heads, rows, HD), jnp.float32)
    roomy = pltpu.CompilerParams(vmem_limit_bytes=32 << 20)
    mixed, tops, sums, after = pl.pallas_call(
        functools.partial(attend_kernel, rows // 2),
        out_shape=[state] * 3 + [token],
        in_specs=[local] * 6,
        out_specs=[local] * 4,
        compiler_params=roomy,
        name="attend",
    )(queries, keys, values, beside, facing, picked)
    traded = []
    for cut, before in zip(cuts, ((beside, beside), (passed, after))):
        (part,) = stage(
            functools.partial(stage_traded_kernel, cut),
            [jax.ShapeDtypeStruct((2, BLOCK, cut[1]), jnp.bfloat16)],
            1,
            [*before, beside, bands],
            "stage_traded",
            32,
        )
        traded.append(send(part, [(1, 2), (2, 1)]))

    mixed, tops, sums = pl.pallas_call(
        functools.partial(merge_kernel, rows // 2),
        out_shape=[state] * 3,
        in_specs=[anywhere] + [local] * 5,
        out_specs=[local] * 3,
        input_output_aliases={3: 0, 4: 1, 5: 2},
        compiler_params=roomy,
        name="merge",
    )(lone, queries, crossed, mixed, tops, sums)
    result = None
    for part, (start, size) in zip(traded, cuts):
        operands = [queries, part, lone, passed, direct, mixed, tops, sums]
        in_specs = [local] * len(operands)
        aliases = {}
        if result is not None:
            aliases = {len(operands): 0}
            in_specs.append(anywhere)
            operands.append(result)
        result = pl.pallas_call(
            functools.partial(close_kernel, start),
            out_shape=jax.ShapeDtypeStruct(queries.shape, queries.dtype),
            in_specs=in_specs,
            out_specs=anywhere,
            input_output_aliases=aliases,
            scratch_shapes=[
                pltpu.VMEM((size // HD, rows, HD), jnp.bfloat16),
                pltpu.SemaphoreType.DMA((size // HD,)),
            ],
            compiler_params=roomy,
            name="close",
        )(*operands)
    return result


def shards(queries, keys, values, band_blocks):
    if lax.axis_size("tm") == 4 and queries.shape[0] == 4 * BLOCK and band_blocks.shape[2] == 2:
        return four_frames(queries, keys, values, band_blocks)
    return any_frames(queries, keys, values, band_blocks)


def solution(mesh):
    placed = (
        P(("groups", "tm"), ("head", "sub")),
        P(("groups", "tm"), ("head", "sub")),
        P(("groups", "tm"), ("head", "sub")),
        P(),
    )
    return jax.shard_map(
        shards,
        mesh=mesh,
        in_specs=placed,
        out_specs=P(("groups", "tm"), ("head", "sub")),
        check_vma=False,
    )
```

```python
import functools

import jax
import jax.numpy as jnp
from jax import lax
from jax.experimental import pallas as pl
from jax.experimental.pallas import tpu as pltpu
from jax.sharding import PartitionSpec as P

HD = 128
BLOCK = 128
LOG2E = 1.4426950408889634

masked_fill = -1e30


def padded(block, sides, width):
    for axis, dim in sides:
        count = lax.axis_size(axis)
        forward = [(i, i + 1) for i in range(count - 1)]
        backward = [(target, source) for source, target in forward]
        low = lax.ppermute(
            lax.slice_in_dim(block, block.shape[dim] - width, None, axis=dim), axis, forward
        )
        high = lax.ppermute(lax.slice_in_dim(block, 0, width, axis=dim), axis, backward)
        block = jnp.concatenate([low, block, high], axis=dim)
    return block


def any_frames(queries, keys, values, band_blocks):
    frame_rows, columns = queries.shape
    frames = lax.axis_size("tm")
    current = lax.axis_index("tm")
    half_rows = frame_rows // 2
    frame_blocks = frame_rows // BLOCK
    capacity = band_blocks.shape[2]
    heads_dev = columns // HD
    paired = jnp.stack([keys, values], 0)
    near_kv = padded(paired, (("tm", 1),), half_rows)
    position = jnp.arange(2 * frame_rows)
    near_ok = ((position >= half_rows) | (current > 0)) & (
        (position < half_rows + frame_rows) | (current < frames - 1)
    )
    kv_blocks = jnp.concatenate(
        [
            paired.reshape(2, frame_blocks, BLOCK, columns),
            jnp.zeros((2, 1, BLOCK, columns), jnp.bfloat16),
        ],
        1,
    )
    outgoing = lax.dynamic_index_in_dim(band_blocks, current, 1, keepdims=False)
    incoming = lax.dynamic_index_in_dim(band_blocks, current, 0, keepdims=False)
    outbound = jnp.take(kv_blocks, outgoing, axis=1)
    arrived = lax.all_to_all(outbound, "tm", split_axis=1, concat_axis=1, tiled=True)
    far_kv = arrived.reshape(2, frames * capacity * BLOCK, columns)
    far_ok = jnp.repeat((incoming != frame_blocks).reshape(-1), BLOCK)
    all_kv = jnp.concatenate([near_kv, far_kv], 1)
    visible = jnp.concatenate([near_ok, far_ok], 0)
    inv_root = HD ** (-0.5)

    def per_head(head_at):
        start = head_at * HD
        query_head = lax.dynamic_slice_in_dim(queries, start, HD, 1)
        key_head = lax.dynamic_slice_in_dim(all_kv[0], start, HD, 1)
        value_head = lax.dynamic_slice_in_dim(all_kv[1], start, HD, 1)
        scores = (
            lax.dot_general(
                query_head, key_head, (((1,), (1,)), ((), ())), preferred_element_type=jnp.float32
            )
            * inv_root
        )
        scores = jnp.where(visible[None, :], scores, masked_fill)
        row_max = jnp.max(scores, axis=1, keepdims=True)
        powers = jnp.exp(scores - row_max)
        row_sum = jnp.sum(powers, axis=1, keepdims=True)
        mixed_sum = jnp.dot(
            powers.astype(jnp.bfloat16), value_head, preferred_element_type=jnp.float32
        )
        return (mixed_sum / row_sum).astype(jnp.bfloat16)

    result = lax.map(per_head, jnp.arange(heads_dev, dtype=jnp.int32))
    return jnp.transpose(result, (1, 0, 2)).reshape(frame_rows, columns)


def run_copies(pairs, sems):
    copies = [
        pltpu.make_async_copy(source, target, sems.at[at])
        for at, (source, target) in enumerate(pairs)
    ]
    for copy in copies:
        copy.start()
    for copy in copies:
        copy.wait()


def rows_of(block):
    return pl.ds(pl.multiple_of(block * BLOCK, BLOCK), BLOCK)


def stage_facing_kernel(half, keys, values, facing, token, sems):
    frame = lax.axis_index("tm")
    rows = pl.ds(pl.multiple_of(lax.rem(frame, 2) * half, half), half)
    token[...] = jnp.zeros_like(token)
    run_copies([(keys.at[rows], facing.at[0]), (values.at[rows], facing.at[1])], sems)


def stage_beside_kernel(half, after, keys, values, beside, token, sems):
    frame = lax.axis_index("tm")
    rows = pl.ds(pl.multiple_of(lax.rem(frame + 1, 2) * half, half), half)
    token[...] = jnp.zeros_like(token)
    run_copies([(keys.at[rows], beside.at[0]), (values.at[rows], beside.at[1])], sems)


def stage_missing_kernel(after, bands, keys, values, missing, sems):
    frame = lax.axis_index("tm")

    @pl.when((frame == 1) | (frame == 2))
    def _():
        rows = rows_of(jnp.where(frame == 1, bands[3, 0, 1], bands[0, 1, 2]))
        run_copies([(keys.at[rows], missing.at[0]), (values.at[rows], missing.at[1])], sems)


def stage_picked_kernel(facing, bands, picked, sems):
    frame = lax.axis_index("tm")

    @pl.when((frame == 1) | (frame == 2))
    def _():
        rows = rows_of(jnp.where(frame == 1, bands[0, 0, 2], bands[3, 1, 1] - 2))
        run_copies([(facing.at[:, rows], picked)], sems)


def stage_crossed_kernel(after, after_too, bands, keys, values, crossed, sems):
    frame = lax.axis_index("tm")

    @pl.when((frame == 0) | (frame == 3))
    def _():
        rows = rows_of(jnp.where(frame == 0, bands[2, 0, 0], bands[1, 1, 3]))
        run_copies([(keys.at[rows], crossed.at[0]), (values.at[rows], crossed.at[1])], sems)


def stage_passed_kernel(beside, bands, passed, sems):
    frame = lax.axis_index("tm")

    @pl.when((frame == 1) | (frame == 2))
    def _():
        rows = rows_of(jnp.where(frame == 1, bands[3, 1, 0] - 2, bands[0, 0, 3]))
        run_copies([(beside.at[:, rows], passed)], sems)


def stage_direct_kernel(after, bands, keys, values, direct, sems):
    frame = lax.axis_index("tm")

    @pl.when((frame == 0) | (frame == 3))
    def _():
        rows = rows_of(jnp.where(frame == 0, bands[3, 0, 0], bands[0, 1, 3]))
        run_copies([(keys.at[rows], direct.at[0]), (values.at[rows], direct.at[1])], sems)


def stage_traded_kernel(cut, after, after_too, beside, bands, traded, sems):
    frame = lax.axis_index("tm")

    @pl.when((frame == 1) | (frame == 2))
    def _():
        rows = rows_of(jnp.where(frame == 1, bands[2, 1, 0] - 2, bands[1, 0, 3]))
        run_copies([(beside.at[:, rows, pl.ds(*cut)], traded)], sems)


RATE = LOG2E * HD ** (-0.5)


def scores_of(queries, keys):
    return lax.dot_general(
        queries, keys, (((1,), (1,)), ((), ())), preferred_element_type=jnp.float32
    )


def attend_kernel(
    chunk, queries, keys, values, beside, facing, picked, mixed, tops, sums, token
):
    frame = lax.axis_index("tm")
    inner = (frame == 1) | (frame == 2)
    rows, columns = queries.shape
    token[...] = jnp.zeros_like(token)
    units = [(head, start) for head in range(columns // HD) for start in range(0, rows, chunk)]

    def attend(pieces_of):
        def pieces(head, kv):
            cols = pl.ds(head * HD, HD)
            own = values if kv else keys
            return [own[:, cols], beside[kv, :, cols]] + pieces_of(kv, cols)

        def score(head, start):
            rows_q = queries[pl.ds(start, chunk), pl.ds(head * HD, HD)]
            return [scores_of(rows_q, piece) for piece in pieces(head, 0)]

        def finish(head, start, scores):
            at = pl.ds(start, chunk)
            row_max = functools.reduce(
                jnp.maximum, [jnp.max(part, axis=1, keepdims=True) for part in scores]
            )
            powers = [jnp.exp2((part - row_max) * RATE) for part in scores]
            row_sum = sum(jnp.sum(part, axis=1, keepdims=True) for part in powers)
            mixed[head, at] = sum(
                jnp.dot(part.astype(jnp.bfloat16), piece, preferred_element_type=jnp.float32)
                for part, piece in zip(powers, pieces(head, 1))
            )
            tops[head, at] = jnp.broadcast_to(row_max, (chunk, HD))
            sums[head, at] = jnp.broadcast_to(row_sum, (chunk, HD))

        scores = score(*units[0])
        for unit, following in zip(units, units[1:] + [None]):
            ahead = score(*following) if following else None
            finish(*unit, scores)
            scores = ahead

    pl.when(inner)(lambda: attend(lambda kv, cols: [facing[kv, :, cols]]))
    pl.when(jnp.logical_not(inner))(lambda: attend(lambda kv, cols: [picked[kv, :, cols]]))


def merge_kernel(chunk, after, queries, crossed, mixed, tops, sums, *state):
    frame = lax.axis_index("tm")
    rows, columns = queries.shape
    new_mixed, new_tops, new_sums = state

    @pl.when((frame == 1) | (frame == 2))
    def _():
        for head in range(columns // HD):
            cols = pl.ds(head * HD, HD)
            for start in range(0, rows, chunk):
                at = pl.ds(start, chunk)
                scores = scores_of(queries[at, cols], crossed[0, :, cols])
                old_top = tops[head, at]
                top = jnp.maximum(old_top, jnp.max(scores, axis=1, keepdims=True))
                shrink = jnp.exp2((old_top - top) * RATE)
                powers = jnp.exp2((scores - top[:, :1]) * RATE)
                row_sum = jnp.sum(powers, axis=1, keepdims=True)
                more = jnp.dot(
                    powers.astype(jnp.bfloat16),
                    crossed[1, :, cols],
                    preferred_element_type=jnp.float32,
                )
                new_mixed[head, at] = mixed[head, at] * shrink + more
                new_sums[head, at] = sums[head, at] * shrink + row_sum
                new_tops[head, at] = top


def close_kernel(first, queries, traded, lone, passed, direct, mixed, tops, sums, *rest):
    out, ready, sems = rest[-3:]
    frame = lax.axis_index("tm")
    inner = (frame == 1) | (frame == 2)
    heads, rows, _ = ready.shape

    def close(pieces_of, chunk):
        units = [(at, start) for at in range(heads) for start in range(0, rows, chunk)]

        def pieces(at, kv):
            return pieces_of(kv, pl.ds(first + at * HD, HD), pl.ds(at * HD, HD))

        def score(at, start):
            rows_q = queries[pl.ds(start, chunk), pl.ds(first + at * HD, HD)]
            return [scores_of(rows_q, piece) for piece in pieces(at, 0)]

        def finish(at, start, scores):
            head, span = first // HD + at, pl.ds(start, chunk)
            old_top = tops[head, span]
            top = functools.reduce(
                jnp.maximum, [jnp.max(part, axis=1, keepdims=True) for part in scores], old_top
            )
            shrink = jnp.exp2((old_top - top) * RATE)
            powers = [jnp.exp2((part - top[:, :1]) * RATE) for part in scores]
            total = sums[head, span] * shrink + sum(
                jnp.sum(part, axis=1, keepdims=True) for part in powers
            )
            more = sum(
                jnp.dot(part.astype(jnp.bfloat16), piece, preferred_element_type=jnp.float32)
                for part, piece in zip(powers, pieces(at, 1))
            )
            whole = mixed[head, span] * shrink + more
            ready[at, span] = (whole / total).astype(jnp.bfloat16)

        copies = []
        scores = score(*units[0])
        for unit, following in zip(units, units[1:] + [None]):
            ahead = score(*following) if following else None
            finish(*unit, scores)
            scores = ahead
            at, start = unit
            if start + chunk == rows:
                here = pl.ds(first + at * HD, HD)
                copies.append(pltpu.make_async_copy(ready.at[at], out.at[:, here], sems.at[at]))
                copies[-1].start()
        for copy in copies:
            copy.wait()

    def of_inner(kv, here, there):
        return [traded[kv, :, there]]

    def of_edge(kv, here, there):
        pair = jnp.concatenate([passed[kv, :, here], direct[kv, :, here]], 0)
        return [pair, lone[kv, :, here]]

    pl.when(inner)(lambda: close(of_inner, rows))
    pl.when(jnp.logical_not(inner))(lambda: close(of_edge, rows // 2))


def four_frames(queries, keys, values, band_blocks):
    rows, columns = queries.shape
    half = rows // 2
    heads = columns // HD
    anywhere = pl.BlockSpec(memory_space=pl.ANY)
    local = pl.BlockSpec(memory_space=pltpu.VMEM)
    scalars = pl.BlockSpec(memory_space=pltpu.SMEM)

    def send(array, pairs):
        return lax.ppermute(array, "tm", pairs)

    bands = jnp.transpose(band_blocks, (0, 2, 1))
    one = jax.ShapeDtypeStruct((2, BLOCK, columns), jnp.bfloat16)
    two = jax.ShapeDtypeStruct((2, 2 * BLOCK, columns), jnp.bfloat16)

    def stage(kernel, shapes, copies, operands, name, room):
        return pl.pallas_call(
            kernel,
            out_shape=shapes,
            in_specs=[scalars if operand is bands else anywhere for operand in operands],
            out_specs=[local] * len(shapes),
            scratch_shapes=[pltpu.SemaphoreType.DMA((copies,))],
            compiler_params=pltpu.CompilerParams(vmem_limit_bytes=room << 20),
            name=name,
        )(*operands)

    token = jax.ShapeDtypeStruct((8, HD), jnp.int32)
    facing, after = stage(
        functools.partial(stage_facing_kernel, half),
        [two, token],
        2,
        [keys, values],
        "stage_facing",
        52,
    )
    beside, after = stage(
        functools.partial(stage_beside_kernel, half),
        [two, token],
        2,
        [after, keys, values],
        "stage_beside",
        52,
    )
    (missing,) = stage(
        stage_missing_kernel, [one], 2, [after, bands, keys, values], "stage_missing", 32
    )
    facing = send(facing, [(1, 2), (2, 1)])
    beside = send(beside, [(0, 1), (1, 0), (2, 3), (3, 2)])
    missing = send(missing, [(1, 2), (2, 1)])
    (picked,) = stage(stage_picked_kernel, [one], 1, [facing, bands], "stage_picked", 32)
    picked = send(picked, [(2, 3), (1, 0)])
    lone = send(missing, [(2, 3), (1, 0)])
    (passed,) = stage(stage_passed_kernel, [one], 1, [beside, bands], "stage_passed", 32)
    passed = send(passed, [(1, 3), (2, 0)])
    (crossed,) = stage(
        stage_crossed_kernel,
        [one],
        2,
        [missing, picked, bands, keys, values],
        "stage_crossed",
        32,
    )
    crossed = send(crossed, [(0, 2), (3, 1)])
    last = heads // 4
    cuts = [(0, heads - last), (heads - last, last)] if last else [(0, heads)]
    cuts = [(start * HD, size * HD) for start, size in cuts]
    (direct,) = stage(
        stage_direct_kernel, [one], 2, [picked, bands, keys, values], "stage_direct", 32
    )
    direct = send(direct, [(0, 3), (3, 0)])
    state = jax.ShapeDtypeStruct((heads, rows, HD), jnp.float32)
    roomy = pltpu.CompilerParams(vmem_limit_bytes=32 << 20)
    mixed, tops, sums, after = pl.pallas_call(
        functools.partial(attend_kernel, rows // 2),
        out_shape=[state] * 3 + [token],
        in_specs=[local] * 6,
        out_specs=[local] * 4,
        compiler_params=roomy,
        name="attend",
    )(queries, keys, values, beside, facing, picked)
    traded = []
    for cut, before in zip(cuts, ((beside, beside), (passed, after))):
        (part,) = stage(
            functools.partial(stage_traded_kernel, cut),
            [jax.ShapeDtypeStruct((2, BLOCK, cut[1]), jnp.bfloat16)],
            1,
            [*before, beside, bands],
            "stage_traded",
            32,
        )
        traded.append(send(part, [(1, 2), (2, 1)]))

    mixed, tops, sums = pl.pallas_call(
        functools.partial(merge_kernel, rows),
        out_shape=[state] * 3,
        in_specs=[anywhere] + [local] * 5,
        out_specs=[local] * 3,
        input_output_aliases={3: 0, 4: 1, 5: 2},
        compiler_params=roomy,
        name="merge",
    )(lone, queries, crossed, mixed, tops, sums)
    result = None
    for part, (start, size) in zip(traded, cuts):
        operands = [queries, part, lone, passed, direct, mixed, tops, sums]
        in_specs = [local] * len(operands)
        aliases = {}
        if result is not None:
            aliases = {len(operands): 0}
            in_specs.append(anywhere)
            operands.append(result)
        result = pl.pallas_call(
            functools.partial(close_kernel, start),
            out_shape=jax.ShapeDtypeStruct(queries.shape, queries.dtype),
            in_specs=in_specs,
            out_specs=anywhere,
            input_output_aliases=aliases,
            scratch_shapes=[
                pltpu.VMEM((size // HD, rows, HD), jnp.bfloat16),
                pltpu.SemaphoreType.DMA((size // HD,)),
            ],
            compiler_params=roomy,
            name="close",
        )(*operands)
    return result


def shards(queries, keys, values, band_blocks):
    if lax.axis_size("tm") == 4 and queries.shape[0] == 4 * BLOCK and band_blocks.shape[2] == 2:
        return four_frames(queries, keys, values, band_blocks)
    return any_frames(queries, keys, values, band_blocks)


def solution(mesh):
    placed = (
        P(("groups", "tm"), ("head", "sub")),
        P(("groups", "tm"), ("head", "sub")),
        P(("groups", "tm"), ("head", "sub")),
        P(),
    )
    return jax.shard_map(
        shards,
        mesh=mesh,
        in_specs=placed,
        out_specs=P(("groups", "tm"), ("head", "sub")),
        check_vma=False,
    )
```

```python
import functools

import jax
import jax.numpy as jnp
from jax import lax
from jax.experimental import pallas as pl
from jax.experimental.pallas import tpu as pltpu
from jax.sharding import PartitionSpec as P

HD = 128
BLOCK = 128
LOG2E = 1.4426950408889634

masked_fill = -1e30


def padded(block, sides, width):
    for axis, dim in sides:
        count = lax.axis_size(axis)
        forward = [(i, i + 1) for i in range(count - 1)]
        backward = [(target, source) for source, target in forward]
        low = lax.ppermute(
            lax.slice_in_dim(block, block.shape[dim] - width, None, axis=dim), axis, forward
        )
        high = lax.ppermute(lax.slice_in_dim(block, 0, width, axis=dim), axis, backward)
        block = jnp.concatenate([low, block, high], axis=dim)
    return block


def any_frames(queries, keys, values, band_blocks):
    frame_rows, columns = queries.shape
    frames = lax.axis_size("tm")
    current = lax.axis_index("tm")
    half_rows = frame_rows // 2
    frame_blocks = frame_rows // BLOCK
    capacity = band_blocks.shape[2]
    heads_dev = columns // HD
    paired = jnp.stack([keys, values], 0)
    near_kv = padded(paired, (("tm", 1),), half_rows)
    position = jnp.arange(2 * frame_rows)
    near_ok = ((position >= half_rows) | (current > 0)) & (
        (position < half_rows + frame_rows) | (current < frames - 1)
    )
    kv_blocks = jnp.concatenate(
        [
            paired.reshape(2, frame_blocks, BLOCK, columns),
            jnp.zeros((2, 1, BLOCK, columns), jnp.bfloat16),
        ],
        1,
    )
    outgoing = lax.dynamic_index_in_dim(band_blocks, current, 1, keepdims=False)
    incoming = lax.dynamic_index_in_dim(band_blocks, current, 0, keepdims=False)
    outbound = jnp.take(kv_blocks, outgoing, axis=1)
    arrived = lax.all_to_all(outbound, "tm", split_axis=1, concat_axis=1, tiled=True)
    far_kv = arrived.reshape(2, frames * capacity * BLOCK, columns)
    far_ok = jnp.repeat((incoming != frame_blocks).reshape(-1), BLOCK)
    all_kv = jnp.concatenate([near_kv, far_kv], 1)
    visible = jnp.concatenate([near_ok, far_ok], 0)
    inv_root = HD ** (-0.5)

    def per_head(head_at):
        start = head_at * HD
        query_head = lax.dynamic_slice_in_dim(queries, start, HD, 1)
        key_head = lax.dynamic_slice_in_dim(all_kv[0], start, HD, 1)
        value_head = lax.dynamic_slice_in_dim(all_kv[1], start, HD, 1)
        scores = (
            lax.dot_general(
                query_head, key_head, (((1,), (1,)), ((), ())), preferred_element_type=jnp.float32
            )
            * inv_root
        )
        scores = jnp.where(visible[None, :], scores, masked_fill)
        row_max = jnp.max(scores, axis=1, keepdims=True)
        powers = jnp.exp(scores - row_max)
        row_sum = jnp.sum(powers, axis=1, keepdims=True)
        mixed_sum = jnp.dot(
            powers.astype(jnp.bfloat16), value_head, preferred_element_type=jnp.float32
        )
        return (mixed_sum / row_sum).astype(jnp.bfloat16)

    result = lax.map(per_head, jnp.arange(heads_dev, dtype=jnp.int32))
    return jnp.transpose(result, (1, 0, 2)).reshape(frame_rows, columns)


def run_copies(pairs, sems):
    copies = [
        pltpu.make_async_copy(source, target, sems.at[at])
        for at, (source, target) in enumerate(pairs)
    ]
    for copy in copies:
        copy.start()
    for copy in copies:
        copy.wait()


def rows_of(block):
    return pl.ds(pl.multiple_of(block * BLOCK, BLOCK), BLOCK)


def stage_facing_kernel(half, keys, values, facing, token, sems):
    frame = lax.axis_index("tm")
    rows = pl.ds(pl.multiple_of(lax.rem(frame, 2) * half, half), half)
    token[...] = jnp.zeros_like(token)
    run_copies([(keys.at[rows], facing.at[0]), (values.at[rows], facing.at[1])], sems)


def stage_beside_kernel(half, after, keys, values, beside, token, sems):
    frame = lax.axis_index("tm")
    rows = pl.ds(pl.multiple_of(lax.rem(frame + 1, 2) * half, half), half)
    token[...] = jnp.zeros_like(token)
    run_copies([(keys.at[rows], beside.at[0]), (values.at[rows], beside.at[1])], sems)


def stage_missing_kernel(after, bands, keys, values, missing, sems):
    frame = lax.axis_index("tm")

    @pl.when((frame == 1) | (frame == 2))
    def _():
        rows = rows_of(jnp.where(frame == 1, bands[3, 0, 1], bands[0, 1, 2]))
        run_copies([(keys.at[rows], missing.at[0]), (values.at[rows], missing.at[1])], sems)


def stage_picked_kernel(facing, bands, picked, sems):
    frame = lax.axis_index("tm")

    @pl.when((frame == 1) | (frame == 2))
    def _():
        rows = rows_of(jnp.where(frame == 1, bands[0, 0, 2], bands[3, 1, 1] - 2))
        run_copies([(facing.at[:, rows], picked)], sems)


def stage_crossed_kernel(after, after_too, bands, keys, values, crossed, sems):
    frame = lax.axis_index("tm")

    @pl.when((frame == 0) | (frame == 3))
    def _():
        rows = rows_of(jnp.where(frame == 0, bands[2, 0, 0], bands[1, 1, 3]))
        run_copies([(keys.at[rows], crossed.at[0]), (values.at[rows], crossed.at[1])], sems)


def stage_passed_kernel(beside, bands, passed, sems):
    frame = lax.axis_index("tm")

    @pl.when((frame == 1) | (frame == 2))
    def _():
        rows = rows_of(jnp.where(frame == 1, bands[3, 1, 0] - 2, bands[0, 0, 3]))
        run_copies([(beside.at[:, rows], passed)], sems)


def stage_direct_kernel(after, bands, keys, values, direct, sems):
    frame = lax.axis_index("tm")

    @pl.when((frame == 0) | (frame == 3))
    def _():
        rows = rows_of(jnp.where(frame == 0, bands[3, 0, 0], bands[0, 1, 3]))
        run_copies([(keys.at[rows], direct.at[0]), (values.at[rows], direct.at[1])], sems)


def stage_traded_kernel(cut, after, after_too, beside, bands, traded, sems):
    frame = lax.axis_index("tm")

    @pl.when((frame == 1) | (frame == 2))
    def _():
        rows = rows_of(jnp.where(frame == 1, bands[2, 1, 0] - 2, bands[1, 0, 3]))
        run_copies([(beside.at[:, rows, pl.ds(*cut)], traded)], sems)


RATE = LOG2E * HD ** (-0.5)


def scores_of(queries, keys):
    return lax.dot_general(
        queries, keys, (((1,), (1,)), ((), ())), preferred_element_type=jnp.float32
    )


def attend_kernel(
    chunk, queries, keys, values, beside, facing, picked, mixed, tops, sums, token
):
    frame = lax.axis_index("tm")
    inner = (frame == 1) | (frame == 2)
    rows, columns = queries.shape
    token[...] = jnp.zeros_like(token)
    units = [(head, start) for head in range(columns // HD) for start in range(0, rows, chunk)]

    def attend(pieces_of):
        def pieces(head, kv):
            cols = pl.ds(head * HD, HD)
            own = values if kv else keys
            return [own[:, cols], beside[kv, :, cols]] + pieces_of(kv, cols)

        def score(head, start):
            rows_q = queries[pl.ds(start, chunk), pl.ds(head * HD, HD)]
            return [scores_of(rows_q, piece) for piece in pieces(head, 0)]

        def finish(head, start, scores):
            at = pl.ds(start, chunk)
            row_max = functools.reduce(
                jnp.maximum, [jnp.max(part, axis=1, keepdims=True) for part in scores]
            )
            powers = [jnp.exp2((part - row_max) * RATE) for part in scores]
            row_sum = sum(jnp.sum(part, axis=1, keepdims=True) for part in powers)
            mixed[head, at] = sum(
                jnp.dot(part.astype(jnp.bfloat16), piece, preferred_element_type=jnp.float32)
                for part, piece in zip(powers, pieces(head, 1))
            )
            tops[head, at] = jnp.broadcast_to(row_max, (chunk, HD))
            sums[head, at] = jnp.broadcast_to(row_sum, (chunk, HD))

        scores = score(*units[0])
        for unit, following in zip(units, units[1:] + [None]):
            ahead = score(*following) if following else None
            finish(*unit, scores)
            scores = ahead

    pl.when(inner)(lambda: attend(lambda kv, cols: [facing[kv, :, cols]]))
    pl.when(jnp.logical_not(inner))(lambda: attend(lambda kv, cols: [picked[kv, :, cols]]))


def merge_kernel(chunk, after, queries, crossed, mixed, tops, sums, *state):
    frame = lax.axis_index("tm")
    rows, columns = queries.shape
    new_mixed, new_tops, new_sums = state

    @pl.when((frame == 1) | (frame == 2))
    def _():
        for head in range(columns // HD):
            cols = pl.ds(head * HD, HD)
            for start in range(0, rows, chunk):
                at = pl.ds(start, chunk)
                scores = scores_of(queries[at, cols], crossed[0, :, cols])
                old_top = tops[head, at]
                top = jnp.maximum(old_top, jnp.max(scores, axis=1, keepdims=True))
                shrink = jnp.exp2((old_top - top) * RATE)
                powers = jnp.exp2((scores - top[:, :1]) * RATE)
                row_sum = jnp.sum(powers, axis=1, keepdims=True)
                more = jnp.dot(
                    powers.astype(jnp.bfloat16),
                    crossed[1, :, cols],
                    preferred_element_type=jnp.float32,
                )
                new_mixed[head, at] = mixed[head, at] * shrink + more
                new_sums[head, at] = sums[head, at] * shrink + row_sum
                new_tops[head, at] = top


def close_kernel(first, queries, traded, lone, passed, direct, mixed, tops, sums, *rest):
    out, ready, sems = rest[-3:]
    frame = lax.axis_index("tm")
    inner = (frame == 1) | (frame == 2)
    heads, rows, _ = ready.shape

    def close(pieces_of, chunk):
        units = [(at, start) for at in range(heads) for start in range(0, rows, chunk)]

        def pieces(at, kv):
            return pieces_of(kv, pl.ds(first + at * HD, HD), pl.ds(at * HD, HD))

        def score(at, start):
            rows_q = queries[pl.ds(start, chunk), pl.ds(first + at * HD, HD)]
            return [scores_of(rows_q, piece) for piece in pieces(at, 0)]

        def finish(at, start, scores):
            head, span = first // HD + at, pl.ds(start, chunk)
            old_top = tops[head, span]
            top = functools.reduce(
                jnp.maximum, [jnp.max(part, axis=1, keepdims=True) for part in scores], old_top
            )
            shrink = jnp.exp2((old_top - top) * RATE)
            powers = [jnp.exp2((part - top[:, :1]) * RATE) for part in scores]
            total = sums[head, span] * shrink + sum(
                jnp.sum(part, axis=1, keepdims=True) for part in powers
            )
            more = sum(
                jnp.dot(part.astype(jnp.bfloat16), piece, preferred_element_type=jnp.float32)
                for part, piece in zip(powers, pieces(at, 1))
            )
            whole = mixed[head, span] * shrink + more
            ready[at, span] = (whole / total).astype(jnp.bfloat16)

        copies = []
        scores = score(*units[0])
        for unit, following in zip(units, units[1:] + [None]):
            ahead = score(*following) if following else None
            finish(*unit, scores)
            scores = ahead
            at, start = unit
            if start + chunk == rows:
                here = pl.ds(first + at * HD, HD)
                copies.append(pltpu.make_async_copy(ready.at[at], out.at[:, here], sems.at[at]))
                copies[-1].start()
        for copy in copies:
            copy.wait()

    def of_inner(kv, here, there):
        return [traded[kv, :, there]]

    def of_edge(kv, here, there):
        pair = jnp.concatenate([passed[kv, :, here], direct[kv, :, here]], 0)
        return [pair, lone[kv, :, here]]

    pl.when(inner)(lambda: close(of_inner, rows))
    pl.when(jnp.logical_not(inner))(lambda: close(of_edge, rows // 2))


def four_frames(queries, keys, values, band_blocks):
    rows, columns = queries.shape
    half = rows // 2
    heads = columns // HD
    anywhere = pl.BlockSpec(memory_space=pl.ANY)
    local = pl.BlockSpec(memory_space=pltpu.VMEM)
    scalars = pl.BlockSpec(memory_space=pltpu.SMEM)

    def send(array, pairs):
        return lax.ppermute(array, "tm", pairs)

    bands = jnp.transpose(band_blocks, (0, 2, 1))
    one = jax.ShapeDtypeStruct((2, BLOCK, columns), jnp.bfloat16)
    two = jax.ShapeDtypeStruct((2, 2 * BLOCK, columns), jnp.bfloat16)

    def stage(kernel, shapes, copies, operands, name, room):
        return pl.pallas_call(
            kernel,
            out_shape=shapes,
            in_specs=[scalars if operand is bands else anywhere for operand in operands],
            out_specs=[local] * len(shapes),
            scratch_shapes=[pltpu.SemaphoreType.DMA((copies,))],
            compiler_params=pltpu.CompilerParams(vmem_limit_bytes=room << 20),
            name=name,
        )(*operands)

    token = jax.ShapeDtypeStruct((8, HD), jnp.int32)
    facing, after = stage(
        functools.partial(stage_facing_kernel, half),
        [two, token],
        2,
        [keys, values],
        "stage_facing",
        52,
    )
    beside, after = stage(
        functools.partial(stage_beside_kernel, half),
        [two, token],
        2,
        [after, keys, values],
        "stage_beside",
        52,
    )
    (missing,) = stage(
        stage_missing_kernel, [one], 2, [after, bands, keys, values], "stage_missing", 32
    )
    facing = send(facing, [(1, 2), (2, 1)])
    beside = send(beside, [(0, 1), (1, 0), (2, 3), (3, 2)])
    missing = send(missing, [(1, 2), (2, 1)])
    (picked,) = stage(stage_picked_kernel, [one], 1, [facing, bands], "stage_picked", 32)
    picked = send(picked, [(2, 3), (1, 0)])
    lone = send(missing, [(2, 3), (1, 0)])
    (passed,) = stage(stage_passed_kernel, [one], 1, [beside, bands], "stage_passed", 32)
    passed = send(passed, [(1, 3), (2, 0)])
    (crossed,) = stage(
        stage_crossed_kernel,
        [one],
        2,
        [missing, picked, bands, keys, values],
        "stage_crossed",
        32,
    )
    crossed = send(crossed, [(0, 2), (3, 1)])
    last = 3 * heads // 8
    cuts = [(0, heads - last), (heads - last, last)] if last else [(0, heads)]
    cuts = [(start * HD, size * HD) for start, size in cuts]
    (direct,) = stage(
        stage_direct_kernel, [one], 2, [picked, bands, keys, values], "stage_direct", 32
    )
    direct = send(direct, [(0, 3), (3, 0)])
    state = jax.ShapeDtypeStruct((heads, rows, HD), jnp.float32)
    roomy = pltpu.CompilerParams(vmem_limit_bytes=32 << 20)
    mixed, tops, sums, after = pl.pallas_call(
        functools.partial(attend_kernel, rows // 2),
        out_shape=[state] * 3 + [token],
        in_specs=[local] * 6,
        out_specs=[local] * 4,
        compiler_params=roomy,
        name="attend",
    )(queries, keys, values, beside, facing, picked)
    traded = []
    for cut, before in zip(cuts, ((beside, beside), (passed, after))):
        (part,) = stage(
            functools.partial(stage_traded_kernel, cut),
            [jax.ShapeDtypeStruct((2, BLOCK, cut[1]), jnp.bfloat16)],
            1,
            [*before, beside, bands],
            "stage_traded",
            32,
        )
        traded.append(send(part, [(1, 2), (2, 1)]))

    mixed, tops, sums = pl.pallas_call(
        functools.partial(merge_kernel, rows),
        out_shape=[state] * 3,
        in_specs=[anywhere] + [local] * 5,
        out_specs=[local] * 3,
        input_output_aliases={3: 0, 4: 1, 5: 2},
        compiler_params=roomy,
        name="merge",
    )(lone, queries, crossed, mixed, tops, sums)
    result = None
    for part, (start, size) in zip(traded, cuts):
        operands = [queries, part, lone, passed, direct, mixed, tops, sums]
        in_specs = [local] * len(operands)
        aliases = {}
        if result is not None:
            aliases = {len(operands): 0}
            in_specs.append(anywhere)
            operands.append(result)
        result = pl.pallas_call(
            functools.partial(close_kernel, start),
            out_shape=jax.ShapeDtypeStruct(queries.shape, queries.dtype),
            in_specs=in_specs,
            out_specs=anywhere,
            input_output_aliases=aliases,
            scratch_shapes=[
                pltpu.VMEM((size // HD, rows, HD), jnp.bfloat16),
                pltpu.SemaphoreType.DMA((size // HD,)),
            ],
            compiler_params=roomy,
            name="close",
        )(*operands)
    return result


def shards(queries, keys, values, band_blocks):
    if lax.axis_size("tm") == 4 and queries.shape[0] == 4 * BLOCK and band_blocks.shape[2] == 2:
        return four_frames(queries, keys, values, band_blocks)
    return any_frames(queries, keys, values, band_blocks)


def solution(mesh):
    placed = (
        P(("groups", "tm"), ("head", "sub")),
        P(("groups", "tm"), ("head", "sub")),
        P(("groups", "tm"), ("head", "sub")),
        P(),
    )
    return jax.shard_map(
        shards,
        mesh=mesh,
        in_specs=placed,
        out_specs=P(("groups", "tm"), ("head", "sub")),
        check_vma=False,
    )
```
